128 devices in a mesh: fsdp: 8 (over z_hi, x), ctx: 16 (over z_lo, y, core).
Axes of the slice: x: 4, y: 4, z: 4 (z_hi: 2, z_lo: 2; z = z_hi * 2 + z_lo), core: 2. Of those that a mesh axis runs over, the one named last changes fastest.
Arguments:
- tokens: bfloat16 [8, 4096, 576], P('fsdp', 'ctx'), may hold values from -6 to 6
- positions: int32 [8, 4096], P('fsdp', 'ctx'), may hold values from 0 to 4095, as said below
- norm1_gain: bfloat16 [576], P('fsdp'), may hold values from 0.5 to 1.5
- w_query: bfloat16 [576, 576], P('fsdp'), may hold values from -0.25 to 0.25
- keyvalue_projection: bfloat16 [576, 384], P('fsdp'), may hold values from -0.25 to 0.25
- w_out: bfloat16 [576, 576], P(None, 'fsdp'), may hold values from -6 to 6
- norm2_gain: bfloat16 [576], P('fsdp'), may hold values from 0.5 to 1.5
- w_gate: bfloat16 [576, 1536], P('fsdp'), may hold values from -0.25 to 0.25
- w_up: bfloat16 [576, 1536], P('fsdp'), may hold values from -0.25 to 0.25
- w_down: bfloat16 [1536, 576], P(None, 'fsdp'), may hold values from -0.15625 to 0.15625
- cotangent: bfloat16 [8, 4096, 576], P('fsdp', 'ctx'), may hold values from -6 to 6
Outputs:
- block_out: bfloat16 [8, 4096, 576], P('fsdp', 'ctx')
- input_grad: float32 [8, 4096, 576], P('fsdp', 'ctx')
- grad_norm1: float32 [576], P('fsdp')
- grad_query: float32 [576, 576], P('fsdp')
- grad_keyvalue: float32 [576, 384], P('fsdp')
- grad_out: float32 [576, 576], P(None, 'fsdp')
- grad_norm2: float32 [576], P('fsdp')
- grad_gate: float32 [576, 1536], P('fsdp')
- grad_up: float32 [576, 1536], P('fsdp')
- grad_down: float32 [1536, 576], P(None, 'fsdp')
The draws below stay inside these ranges and needn't reach their ends.
Inputs may be any that keep to these rules, and one draw needn't show every extreme that they name: Each sequence's positions are a permutation of 0 to 4095 made of aligned runs of 128 stored tokens holding consecutive positions in increasing order.
All inputs are finite; a program needn't handle non-finite values.
Results may differ from the reference program's by a relative error of at most 0.025.
Values may be sent and summed in bfloat16 or wider, within the bound.
A program may use at most 128 MiB of HBM per device.

```python
import math
import jax
import jax.numpy as jnp
from jax import lax

MODEL_WIDTH = 576
HQ = 9
KEY_VALUE_HEADS = 3
HEAD_SIZE = 64
FF = 1536
LEN = 4096
SEQS = 8
HALF = 128


def draw_positions(key, part):
    key = jax.random.fold_in(key, 7)
    seq_keys = jax.random.split(key, SEQS)
    orders = jax.vmap(lambda one_key: jax.random.permutation(one_key, LEN // HALF))(seq_keys)
    starts = orders.astype(jnp.int32)[:, :, None] * HALF
    return (starts + jnp.arange(HALF, dtype=jnp.int32)[None, None, :]).reshape(SEQS, LEN).astype(jnp.int32)


def shard_levels(key, dims, cuts, low, largest):
    level = 1.0
    for axis_at, blocks in cuts:
        draws = jax.random.uniform(jax.random.fold_in(jax.random.fold_in(key, 6), axis_at), (blocks,), jnp.float32, low / len(cuts), largest / len(cuts))
        level = level * jnp.repeat(jnp.exp(draws), dims[axis_at] // blocks).reshape((-1,) + (1,) * (len(dims) - 1 - axis_at))
    return level


def gaussian(rng, extent, scale, reach, pieces=(), kind=jnp.bfloat16):
    loudness = shard_levels(rng, extent, pieces, -0.22, 0.18) if pieces else 1.0
    entries = jax.random.normal(rng, extent, jnp.float32) * scale * loudness
    return jnp.minimum(jnp.maximum(entries, -reach), reach).astype(kind)


def setup_inputs(seed: int = 0) -> dict:
    streams_of = jax.random.split(jax.random.key(seed), 12)
    return {
        "tokens": gaussian(streams_of[0], (SEQS, LEN, MODEL_WIDTH), 1.0, 6.0, ((0, 8), (1, 16))),
        "positions": draw_positions(jax.random.fold_in(streams_of[11], 71), 0),
        "norm1_gain": jnp.clip(1.0 + 0.1 * jax.random.normal(streams_of[2], (MODEL_WIDTH,), jnp.float32), 0.5, 1.5).astype(jnp.bfloat16),
        "w_query": gaussian(streams_of[3], (MODEL_WIDTH, HQ * HEAD_SIZE), MODEL_WIDTH ** -0.5, 0.25, ((0, 8),)),
        "keyvalue_projection": gaussian(streams_of[4], (MODEL_WIDTH, 2 * KEY_VALUE_HEADS * HEAD_SIZE), MODEL_WIDTH ** -0.5, 0.25, ((0, 8),)),
        "w_out": gaussian(streams_of[5], (HQ * HEAD_SIZE, MODEL_WIDTH), (max(1, 2 * HQ * HEAD_SIZE // LEN)) ** -0.5, 6.0, ((1, 8),)),
        "norm2_gain": jnp.clip(1.0 + 0.1 * jax.random.normal(streams_of[6], (MODEL_WIDTH,), jnp.float32), 0.5, 1.5).astype(jnp.bfloat16),
        "w_gate": gaussian(streams_of[7], (MODEL_WIDTH, FF), MODEL_WIDTH ** -0.5, 0.25, ((0, 8),)),
        "w_up": gaussian(streams_of[8], (MODEL_WIDTH, FF), MODEL_WIDTH ** -0.5, 0.25, ((0, 8),)),
        "w_down": gaussian(streams_of[9], (FF, MODEL_WIDTH), FF ** -0.5, 0.15625, ((1, 8),)),
        "cotangent": gaussian(streams_of[10], (SEQS, LEN, MODEL_WIDTH), 1.0, 6.0, ((0, 8), (1, 16))),
    }


@jax.custom_vjp
def lowered_input(v):
    return lax.optimization_barrier(v.astype(jnp.bfloat16)).astype(jnp.float32)

@jax.custom_vjp
def lowered_gradient(v):
    return v

def low_keep(v):
    return (lowered_input(v), None)

def low_pass(kept, grad):
    return (grad,)

def back_keep(v):
    return (v, None)

def back_low(kept, grad):
    return (lowered_input(grad),)
lowered_input.defvjp(low_keep, low_pass)
lowered_gradient.defvjp(back_keep, back_low)

def angles(pos, width):
    half = width // 2
    freqs = jnp.power(jnp.float32(100000.0), -(jnp.arange(half).astype(jnp.float32) * (2.0 / width)))
    angle = pos.astype(jnp.float32)[:, None] * freqs[None, :]
    return (jnp.cos(angle)[:, None, :], jnp.sin(angle)[:, None, :])

def rotate_pairs(value_rows, cosine_table, sine_table):
    half = value_rows.shape[-1] // 2
    first = value_rows[..., :half]
    second = value_rows[..., half:]
    return jnp.concatenate([first * cosine_table - second * sine_table, second * cosine_table + first * sine_table], axis=-1)

def highest_precision(left, right):
    return jnp.dot(left, right, precision=lax.Precision.HIGHEST)

def normalize(value_rows, gain):
    return value_rows * lax.rsqrt(lax.optimization_barrier(jnp.mean(value_rows * value_rows, axis=-1, keepdims=True)) + 1e-05) * gain

def attention(queries, key_rows, value_rows, pos):
    sequence_length = queries.shape[0]
    block = math.gcd(sequence_length, 512)
    groups = key_rows.shape[1]
    share = queries.shape[1] // groups
    scale = 1.0 / math.sqrt(queries.shape[-1])
    query_blocks = queries.reshape(sequence_length // block, block, groups, share, queries.shape[-1])
    pos_blocks = pos.reshape(sequence_length // block, block)

    def one_block(item):
        query_block, pos_block = item
        scores = jnp.einsum('qgrd,kgd->grqk', query_block, key_rows, precision=lax.Precision.HIGHEST) * scale
        scores = lowered_gradient(scores)
        allowed = pos[None, None, None, :] <= pos_block[None, None, :, None]
        scores = jnp.where(allowed, scores, -1e+30)
        probs = lowered_input(jax.nn.softmax(scores, axis=-1))
        return jnp.einsum('grqk,kgd->qgrd', probs, value_rows, precision=lax.Precision.HIGHEST)
    result = lax.map(jax.checkpoint(one_block), (query_blocks, pos_blocks))
    return result.reshape(sequence_length, -1)

def layer(inputs, pos, gain_one, query_weight, keyvalue_matrix, out_weight, gain_two, gate_weight, up_weight, down_weight):
    sequence_length = inputs.shape[0]
    first_activation = lowered_input(normalize(inputs, gain_one))
    query_pre = lowered_gradient(highest_precision(first_activation, query_weight)).reshape(sequence_length, HQ, HEAD_SIZE)
    keyvalue_before_rotation = lowered_gradient(highest_precision(first_activation, keyvalue_matrix)).reshape(sequence_length, 2 * KEY_VALUE_HEADS, HEAD_SIZE)
    cosine_table, sine_table = angles(pos, HEAD_SIZE)
    queries = lowered_input(rotate_pairs(query_pre, cosine_table, sine_table))
    key_rows = lowered_input(rotate_pairs(keyvalue_before_rotation[:, :KEY_VALUE_HEADS], cosine_table, sine_table))
    value_rows = lowered_input(keyvalue_before_rotation[:, KEY_VALUE_HEADS:])
    attended = lowered_input(lowered_gradient(attention(queries, key_rows, value_rows, pos)))
    mid = inputs + lowered_gradient(highest_precision(attended, out_weight))
    act_two = lowered_input(normalize(mid, gain_two))
    gate = lowered_gradient(highest_precision(act_two, gate_weight))
    up_part = lowered_gradient(highest_precision(act_two, up_weight))
    hidden = lowered_input(jax.nn.silu(gate) * up_part)
    return mid + lowered_gradient(highest_precision(hidden, down_weight))

def reference(tokens, positions, norm1_gain, w_query, keyvalue_projection, w_out, norm2_gain, w_gate, w_up, w_down, cotangent):
    params = tuple((weight.astype(jnp.float32) for weight in (norm1_gain, w_query, keyvalue_projection, w_out, norm2_gain, w_gate, w_up, w_down)))

    def step(totals, item):
        seq_in, seq_pos, seq_cot = item

        def apply(inputs, *weights):
            return layer(inputs, seq_pos, *weights)
        result, pull = jax.vjp(apply, seq_in.astype(jnp.float32), *params)
        grads = pull(seq_cot.astype(jnp.float32))
        totals = tuple((total + grad for total, grad in zip(totals, grads[1:])))
        return (totals, (result.astype(jnp.bfloat16), grads[0]))
    zeros = tuple((jnp.zeros_like(weight) for weight in params))
    totals, (results, input_grads) = lax.scan(step, zeros, (tokens, positions, cotangent))
    return (results, input_grads, totals[0], totals[1], totals[2], totals[3], totals[4], totals[5], totals[6], totals[7])
```

```python
import numpy as np

import jax
import jax.numpy as jnp
from jax import lax
from jax.experimental import pallas as pl
from jax.experimental.pallas import tpu as pltpu
from jax.sharding import PartitionSpec as P

MESH = pl.DeviceIdType.MESH
BF = jnp.bfloat16
F32 = jnp.float32
D = 576
DP = 640
ROWS = 256
WA = 512
WB = 2816
FC = 256
NEG = -1e30
STEPS = (0, 1, 3, 2)
BACK = (2, 1, 3, 0)


def mm(a, b):
    return jnp.dot(a, b, preferred_element_type=F32)


def mm_nt(a, b):
    return lax.dot_general(a, b, (((1,), (1,)), ((), ())), preferred_element_type=F32)


def mm_tn(a, b):
    return lax.dot_general(a, b, (((0,), (0,)), ((), ())), preferred_element_type=F32)


def lane_iota(shape):
    return lax.broadcasted_iota(jnp.int32, shape, len(shape) - 1)


def partner_lanes(u):
    lane = lane_iota(u.shape)
    return jnp.where(lane % 64 < 32, pltpu.roll(u, 96, 1), pltpu.roll(u, 32, 1))


def kernel(
    xc, wa_in, wb_in, cos_in, sin_in,
    bo_out, ig_out, ga_out, gb_out,
    xc_r, wa, wb, cos_s, sin_s, kv, bias, perm,
    qt, qx, dot_, dox, st_m, st_l, acc, ot, dqt,
    xs, dy, mid, act1, act1t, attb, dmid,
    dkv_p, d1_r, d2_s, d2_r,
    ga, gac, gbc, gax, gbx, ga2, gb2, gaz, gbz, ga3, gb3, gal, gbl, ga4, gb4, gay, gby,
    gaf, gbf, bo_s, bo_r, ig_s, ig_r,
    ss, rs, ls,
):
    f = lax.axis_index("fsdp")
    c = lax.axis_index("ctx")
    zh, xx = f // 4, f % 4
    zl, yy, k = c // 8, (c // 2) % 4, c % 2
    fz = (1 - zh) * 4 + xx

    def ctx_at(z, y, core):
        return z * 8 + y * 2 + core

    def slot_at(z, y, core):
        return y * 4 + z * 2 + core

    other = ctx_at(zl, yy, 1 - k)
    sends = []
    used = [0]

    def take(n):
        used[0] += n
        return used[0] - n

    def remote(src, dst, sem, fs, cs):
        return pltpu.make_async_remote_copy(
            src_ref=src, dst_ref=dst, send_sem=ss.at[sem], recv_sem=rs.at[sem],
            device_id={"fsdp": fs, "ctx": cs}, device_id_type=MESH,
        )

    def send(src, dst, sem, fs, cs):
        copy = remote(src, dst, sem, fs, cs)
        copy.start()
        sends.append(copy)
        return copy

    def arrived(dst, sem):
        remote(dst, dst, sem, f, other).wait_recv()

    barrier = pltpu.get_barrier_semaphore()
    for step in range(1, 16):
        pl.semaphore_signal(
            barrier, inc=1, device_id={"fsdp": f, "ctx": (c + step) % 16}, device_id_type=MESH
        )
    pl.semaphore_signal(barrier, inc=1, device_id={"fsdp": fz, "ctx": c}, device_id_type=MESH)
    for step in range(1, 4):
        pl.semaphore_signal(
            barrier, inc=1, device_id={"fsdp": zh * 4 + (xx + step) % 4, "ctx": c},
            device_id_type=MESH,
        )
    pl.semaphore_wait(barrier, 19)

    sem_x = take(16)
    for step in range(1, 16):
        send(xc.at[(c + step) % 16], xc_r.at[c], sem_x + step, f, (c + step) % 16)
    local = [
        pltpu.make_async_copy(xc.at[c], xc_r.at[c], ls.at[0]),
        pltpu.make_async_copy(wa_in.at[k], wa.at[k, f], ls.at[1]),
        pltpu.make_async_copy(wb_in.at[k], wb.at[k, f], ls.at[2]),
        pltpu.make_async_copy(cos_in.at[:, c], cos_s, ls.at[3]),
        pltpu.make_async_copy(sin_in.at[:, c], sin_s, ls.at[4]),
    ]
    for copy in local:
        copy.start()

    def gather_first(w_in, w, sem):
        send(w_in.at[k], w.at[k, f], sem, fz, c)
        for step in range(1, 4):
            send(w_in.at[k], w.at[k, f], sem + step, zh * 4 + (xx + step) % 4, c)

    def gather_second(w, sem):
        arrived(w.at[k, fz], sem)
        return [
            send(w.at[k, fz], w.at[k, fz], sem + 3 + step, zh * 4 + (xx + step) % 4, c)
            for step in range(1, 4)
        ]

    def gather_third(w, sem):
        for step in range(1, 4):
            from_x = (xx + 4 - step) % 4
            arrived(w.at[k, zh * 4 + from_x], sem + step)
            arrived(w.at[k, (1 - zh) * 4 + from_x], sem + 3 + step)
        return [send(w.at[k], w.at[k], sem + 7, f, other)]

    def gather_last(w, sem):
        arrived(w.at[1 - k], sem + 7)

    sem_a = take(8)
    sem_b = take(8)
    gather_first(wa_in, wa, sem_a)
    gather_first(wb_in, wb, sem_b)

    def make_bias(slot, carry):
        e = ctx_at((slot // 2) % 2, slot // 4, slot % 2)
        j = lax.broadcasted_iota(jnp.int32, (128, 128), 0)
        i = lax.broadcasted_iota(jnp.int32, (128, 128), 1)
        ok = (j // 8 < i // 8) | ((j // 8 == i // 8) & (8 * e + j % 8 <= 8 * c + i % 8))
        bias[pl.ds(pl.multiple_of(slot * 128, 128), 128), :] = jnp.where(ok, 0.0, NEG)
        return carry

    lax.fori_loop(0, 16, make_bias, 0)
    gather_second(wa, sem_a)
    for copy in local:
        copy.wait()
    for step in range(1, 16):
        arrived(xc_r.at[(c + 16 - step) % 16], sem_x + step)

    x_raw = xc_r[:, 0:16, :].reshape(ROWS, DP)
    lane = lane_iota((ROWS, DP))
    tag = jnp.sum(jnp.where(lane == 72, x_raw.astype(F32), 0.0), axis=1, keepdims=True)
    place = lane_iota((ROWS, ROWS)).astype(F32)
    perm[...] = jnp.where(tag == place, 1.0, 0.0).astype(BF)
    perm_t = jnp.where(tag == place, 1.0, 0.0).T.astype(BF)
    x = mm(perm_t, x_raw)
    x = jnp.where(lane % 80 < 72, x, 0.0)
    xs[...] = x
    dy[...] = mm(perm_t, xc_r[:, 16:32, :].reshape(ROWS, DP)).astype(BF)

    gather_third(wa, sem_a)
    r1 = lax.rsqrt(jnp.sum(x * x, axis=-1, keepdims=True) * (1.0 / D) + 1e-5)
    gather_last(wa, sem_a)

    def gain_row(which):
        hot = jnp.where(lane_iota((16, 128)) == 64 + which, 1.0, 0.0).astype(BF)
        block = wa[1, :, :, 0:128].reshape(DP, 128)
        return mm_nt(hot, block)[0:1, :]

    gain1, gain2 = gain_row(0), gain_row(1)
    a1 = x * r1 * gain1
    a1b = a1.astype(BF)
    act1[...] = a1b
    act1t[...] = a1.T.astype(BF)

    cos = cos_s[...].reshape(ROWS, 128)
    sin = sin_s[...].reshape(ROWS, 128)
    low = lane_iota((ROWS, 128)) < 64
    cos_kv = jnp.where(low, cos, 1.0)
    sin_kv = jnp.where(low, sin, 0.0)

    mine = slot_at(zl, yy, k)
    kv_pre = mm(a1b, wa[1, :, :, 128:512].reshape(DP, 384))
    for g in range(3):
        u = kv_pre[:, 128 * g : 128 * g + 128]
        kv[mine, g] = (u * cos_kv + partner_lanes(u) * sin_kv).astype(BF)
    sem_k = take(16)

    send(kv.at[mine], kv.at[mine], sem_k, f, other)
    for off in STEPS:
        for a in (0, 1):
            if (a, off) != (0, 0):
                to = ctx_at(zl if a == 0 else 1 - zl, (yy + off) % 4, k)
                send(kv.at[mine], kv.at[mine], sem_k + a * 4 + off, f, to)

    def kv_direct(off):
        for a in (0, 1):
            if (a, off) != (0, 0):
                at = slot_at(zl if a == 0 else 1 - zl, (yy + 4 - off) % 4, k)
                arrived(kv.at[at], sem_k + a * 4 + off)
                send(kv.at[at], kv.at[at], sem_k + 8 + a * 4 + off, f, other)

    def kv_across(off):
        for a in (0, 1):
            at = slot_at(zl if a == 0 else 1 - zl, (yy + 4 - off) % 4, 1 - k)
            arrived(kv.at[at], sem_k if (a, off) == (0, 0) else sem_k + 8 + a * 4 + off)

    for t in range(5):
        w = wa[0, :, :, 128 * t : 128 * t + 128] if t < 4 else wa[1, :, :, 0:128]
        u = mm(a1b, w.reshape(DP, 128))
        u = (u * cos + partner_lanes(u) * sin).astype(BF).astype(F32) * 0.125
        for half in range(2):
            h = 2 * t + half
            if h < 9:
                g, r = h // 3, h % 3
                v = jnp.where(low, u if half == 0 else pltpu.roll(u, 64, 1), 0.0)
                vt = v.T
                for ih in range(2):
                    at = 384 * ih + 128 * r
                    qx[g, at : at + 128, :] = v[128 * ih : 128 * ih + 128].astype(BF)
                    qt[g, :, at : at + 128] = vt[:, 128 * ih : 128 * ih + 128].astype(BF)

    from_wb = gather_second(wb, sem_b)

    st_m[...] = jnp.full(st_m.shape, NEG, F32)
    st_l[...] = jnp.zeros(st_l.shape, F32)
    acc[...] = jnp.zeros(acc.shape, F32)

    def three(b):
        return jnp.concatenate([b, b, b], axis=1)

    def fold_forward(off):
        group = (yy + 4 - off) % 4

        def per_head(g, carry):
            b3 = three(bias[pl.ds(pl.multiple_of(group * 512, 512), 512), :])
            for key_half, lane_half in ((0, 0), (0, 1), (1, 1)):
                at = 384 * lane_half
                rows = kv[pl.ds(group * 4, 4), g, 128 * key_half : 128 * key_half + 128, :]
                rows = rows.reshape(512, 128)
                s = mm(rows, qt[g, :, at : at + 384])
                if key_half == lane_half:
                    s = s + b3
                old = st_m[g, :, at : at + 384]
                new = jnp.maximum(old, jnp.max(s, axis=0, keepdims=True))
                p = jnp.exp(s - new)
                scale = jnp.exp(old - new)
                st_m[g, :, at : at + 384] = new
                st_l[g, :, at : at + 384] = (
                    st_l[g, :, at : at + 384] * scale + jnp.sum(p, axis=0, keepdims=True)
                )
                acc[g, :, at : at + 384] = acc[g, :, at : at + 384] * scale + mm_tn(
                    rows, p.astype(BF)
                )
            return carry

        lax.fori_loop(0, 3, per_head, 0)

    kv_direct(0)
    kv_direct(STEPS[1])
    kv_across(0)
    fold_forward(0)
    kv_direct(STEPS[2])
    kv_across(STEPS[1])
    fold_forward(STEPS[1])
    kv_direct(STEPS[3])
    kv_across(STEPS[2])
    fold_forward(STEPS[2])
    from_wb += gather_third(wb, sem_b)
    kv_across(STEPS[3])
    fold_forward(STEPS[3])

    def head_rows(ref, g, r):
        return jnp.concatenate(
            [ref[g, :, 384 * ih + 128 * r : 384 * ih + 128 * r + 128].T for ih in range(2)], axis=0
        )

    for g in range(3):
        ot[g] = acc[g] / st_l[g]
        st_l[g] = st_m[g] + jnp.log(st_l[g])
    for t in range(5):
        a = pltpu.roll(head_rows(ot, 2 * t // 3, 2 * t % 3), 64, 1)
        b = head_rows(ot, (2 * t + 1) // 3, (2 * t + 1) % 3) if t < 4 else jnp.zeros((ROWS, 128), F32)
        attb[:, 128 * t : 128 * t + 128] = jnp.where(low, a, b).astype(BF)

    gather_last(wb, sem_b)

    def out_t(half):
        if half == 0:
            return wb[0, :, :, 2304:2816].reshape(DP, 512)
        return wb[1, :, :, 2304:2432].reshape(DP, 128)

    m0 = xs[...] + mm_nt(attb[:, 0:512], out_t(0)) + mm_nt(attb[:, 512:640], out_t(1))
    r2 = lax.rsqrt(jnp.sum(m0 * m0, axis=-1, keepdims=True) * (1.0 / D) + 1e-5)
    mid[...] = m0
    a2 = m0 * r2 * gain2
    a2b = a2.astype(BF)
    a2t = a2.T.astype(BF)
    dyb = dy[...]
    dyt = dyb.astype(F32).T.astype(BF)

    for copy in from_wb:
        copy.wait_send()
    sends[:] = [copy for copy in sends if all(copy is not done for done in from_wb)]
    gb = wb

    def ff(j, carry):
        total, dact = carry
        cols = pl.ds(pl.multiple_of(j * FC, FC), FC)
        dcol = pl.ds(pl.multiple_of(1536 + (j % 3) * FC, FC), FC)
        wg = wb[0, :, :, cols].reshape(DP, FC)
        wu = wb[1, :, :, cols].reshape(DP, FC)
        wd = wb[j // 3, :, :, dcol].reshape(DP, FC)
        gate, up = mm(a2b, wg), mm(a2b, wu)
        sig = jax.nn.sigmoid(gate)
        swish = gate * sig
        hid = (swish * up).astype(BF)
        total = total + mm_nt(hid, wd)
        dh = mm(dyb, wd)
        dg = (dh * up * sig * (1.0 + gate * (1.0 - sig))).astype(BF)
        du = (dh * swish).astype(BF)
        gb[j // 3, :, :, dcol] = mm(dyt, hid).astype(BF).reshape(8, 80, FC)
        gb[0, :, :, cols] = mm(a2t, dg).astype(BF).reshape(8, 80, FC)
        gb[1, :, :, cols] = mm(a2t, du).astype(BF).reshape(8, 80, FC)
        dact = dact + mm_nt(dg, wg) + mm_nt(du, wu)
        return total, dact

    zero = jnp.zeros((ROWS, DP), F32)
    total, dact = lax.fori_loop(0, 6, ff, (zero, zero))

    def give_back(value, src, dst, sem):
        src[...] = mm(perm[...], value.astype(BF)).astype(BF).reshape(16, 16, DP)
        for step in range(1, 16):
            send(src.at[(c + step) % 16], dst.at[c], sem + step, f, (c + step) % 16)
        dst[c] = src[c]

    sem_o = take(16)
    sem_i = take(16)
    m0 = mid[...]
    give_back(m0 + total, bo_s, bo_r, sem_o)

    dyf = dyb.astype(F32)
    gain_grad2 = jnp.sum(dact * m0 * r2, axis=0, keepdims=True)
    wgt = dact * gain2
    inner = jnp.sum(wgt * m0, axis=-1, keepdims=True) * (1.0 / D)
    dm = dyf + r2 * wgt - m0 * (r2 * r2 * r2) * inner
    dmid[...] = dm
    dmb = dm.astype(BF)
    dmt = dm.T.astype(BF)

    def reducer(width, parts, core_r, x_r, sum2, z_r, sum3, l_r, sum4, y_r, final):
        sem = take(9)
        half = width // 2
        mine_cols = pl.ds(pl.multiple_of(zl * half, 128), half)
        their_cols = pl.ds(pl.multiple_of((1 - zl) * half, 128), half)

        def one():
            send(parts.at[1 - k], core_r, sem, f, other)

        def two():
            arrived(core_r, sem)
            parts[k] = (parts[k].astype(F32) + core_r[...].astype(F32)).astype(BF)
            for step in range(1, 4):
                to = (xx + step) % 4
                for q in range(2):
                    pair = x_r.at[step - 1, q]
                    send(parts.at[k, q * 4 + to], pair, sem_x2 + 2 * (step - 1) + q, q_f(to), c)

        def three_():
            for step in range(3):
                for q in range(2):
                    arrived(x_r.at[step, q], sem_x2 + 2 * step + q)
            for q in range(2):
                v = parts[k, q * 4 + xx].astype(F32)
                for step in range(3):
                    v = v + x_r[step, q].astype(F32)
                sum2[q] = v.astype(BF)
            send(sum2.at[1 - zh], z_r, sem + 1, fz, c)

        def four():
            arrived(z_r, sem + 1)
            sum3[...] = (sum2[zh].astype(F32) + z_r[...].astype(F32)).astype(BF)
            send(sum3.at[:, their_cols], l_r, sem + 2, f, ctx_at(1 - zl, yy, k))

        def five():
            arrived(l_r, sem + 2)
            sum4[...] = (sum3[:, mine_cols].astype(F32) + l_r[...].astype(F32)).astype(BF)
            for step in range(1, 4):
                send(sum4, y_r.at[step - 1], sem + 2 + step, f, ctx_at(zl, (yy + step) % 4, k))

        def six():
            for step in range(1, 4):
                arrived(y_r.at[step - 1], sem + 2 + step)
            v = sum4[...].astype(F32)
            for step in range(3):
                v = v + y_r[step].astype(F32)
            final[k, :, mine_cols] = v.astype(BF)
            piece = final.at[k, :, mine_cols]
            send(piece, piece, sem + 6, f, ctx_at(1 - zl, yy, k))

        def seven():
            arrived(final.at[k, :, their_cols], sem + 6)
            send(final.at[k], final.at[k], sem + 7, f, other)

        def eight():
            arrived(final.at[1 - k], sem + 7)

        sem_x2 = take(6)

        def q_f(to):
            return zh * 4 + to

        return one, two, three_, four, five, six, seven, eight

    for t in range(5):
        w = wb[0, :, :, 2304 + 128 * t : 2432 + 128 * t] if t < 4 else wb[1, :, :, 2304:2432]
        u = mm(dmb, w.reshape(DP, 128)).astype(BF).astype(F32)
        for half in range(2):
            h = 2 * t + half
            if h < 9:
                g, r = h // 3, h % 3
                v = jnp.where(low, 0.0, u if half == 1 else pltpu.roll(u, 64, 1))
                vt = v.T
                for ih in range(2):
                    at = 384 * ih + 128 * r
                    dox[g, at : at + 128, :] = v[128 * ih : 128 * ih + 128].astype(BF)
                    dot_[g, :, at : at + 128] = vt[:, 128 * ih : 128 * ih + 128].astype(BF)
    gb[0, :, :, 2304:2816] = mm(dmt, attb[:, 0:512]).astype(BF).reshape(8, 80, 512)
    gb[1, :, :, 2304:2432] = mm(dmt, attb[:, 512:640]).astype(BF).reshape(8, 80, 128)
    red_b = reducer(WB, gb, gbc, gbx, gb2, gbz, gb3, gbl, gb4, gby, gbf)
    red_b[0]()
    for g in range(3):
        st_m[g] = jnp.sum(dot_[g].astype(F32) * ot[g], axis=0, keepdims=True)
    dqt[...] = jnp.zeros(dqt.shape, F32)

    def fold_backward(at_step, off):
        group = (yy + 4 - off) % 4

        def per_head(g, carry):
            b3 = three(bias[pl.ds(pl.multiple_of(group * 512, 512), 512), :])
            for key_half in range(2):
                rows = kv[pl.ds(group * 4, 4), g, 128 * key_half : 128 * key_half + 128, :]
                rows = rows.reshape(512, 128)
                grad = None
                for lane_half in range(key_half, 2):
                    at = 384 * lane_half
                    s = mm(rows, qt[g, :, at : at + 384])
                    if key_half == lane_half:
                        s = s + b3
                    p = jnp.exp(s - st_l[g, :, at : at + 384])
                    dp = mm(rows, dot_[g, :, at : at + 384])
                    ds = (p * (dp - st_m[g, :, at : at + 384])).astype(BF)
                    part = mm(ds, qx[g, at : at + 384, :]) + mm(
                        p.astype(BF), dox[g, at : at + 384, :]
                    )
                    grad = part if grad is None else grad + part
                    dqt[g, :, at : at + 384] += mm_tn(rows, ds)
                dkv_p[at_step, :, g, 128 * key_half : 128 * key_half + 128, :] = grad.astype(
                    BF
                ).reshape(4, 128, 128)
            return carry

        lax.fori_loop(0, 3, per_head, 0)

    sem_d = take(12)

    def dkv_first(at_step):
        for z in range(2):
            send(
                dkv_p.at[at_step, 2 * z + 1 - k], d1_r.at[at_step, z], sem_d1 + 2 * at_step + z,
                f, other,
            )

    sem_d1 = take(8)

    def dkv_second(at_step, off):
        for z in range(2):
            arrived(d1_r.at[at_step, z], sem_d1 + 2 * at_step + z)
        for z in range(2):
            d2_s[at_step, z] = (
                dkv_p[at_step, 2 * z + k].astype(F32) + d1_r[at_step, z].astype(F32)
            ).astype(BF)
        for a in (0, 1):
            if (a, off) != (0, 0):
                z = zl if a == 0 else 1 - zl
                send(
                    d2_s.at[at_step, z], d2_r.at[a * 4 + off], sem_d + a * 4 + off,
                    f, ctx_at(z, (yy + 4 - off) % 4, k),
                )

    fold_backward(0, BACK[0])
    dkv_first(0)
    red_b[1]()
    fold_backward(1, BACK[1])
    dkv_first(1)
    dkv_second(0, BACK[0])
    fold_backward(2, BACK[2])
    dkv_first(2)
    dkv_second(1, BACK[1])
    red_b[2]()
    fold_backward(3, BACK[3])
    dkv_first(3)
    dkv_second(2, BACK[2])
    red_b[3]()

    dq_tiles = []
    for t in range(5):
        a = head_rows(dqt, 2 * t // 3, 2 * t % 3)
        if t < 4:
            b = pltpu.roll(head_rows(dqt, (2 * t + 1) // 3, (2 * t + 1) % 3), 64, 1)
        else:
            b = jnp.zeros((ROWS, 128), F32)
        u = jnp.where(low, a, b) * 0.125
        dq_tiles.append((u * cos - partner_lanes(u) * sin).astype(BF))
    dq = jnp.concatenate(dq_tiles, axis=1)
    a1t = act1t[...]
    ga[0] = mm(a1t, dq[:, 0:512]).astype(BF).reshape(8, 80, 512)
    dact1 = mm_nt(dq[:, 0:512], wa[0].reshape(DP, 512)) + mm_nt(
        dq[:, 512:640], wa[1, :, :, 0:128].reshape(DP, 128)
    )
    red_b[4]()
    dkv_second(3, BACK[3])

    for a in (0, 1):
        for off in range(4):
            if (a, off) != (0, 0):
                arrived(d2_r.at[a * 4 + off], sem_d + a * 4 + off)
    for g in range(3):
        u = d2_s[3, zl, g].astype(F32)
        for n in range(1, 8):
            u = u + d2_r[n, g].astype(F32)
        u = (u * cos_kv - partner_lanes(u) * sin_kv).astype(BF)
        at = 128 + 128 * g
        ga[1, :, :, at : at + 128] = mm(a1t, u).astype(BF).reshape(8, 80, 128)
        dact1 = dact1 + mm_nt(u, wa[1, :, :, at : at + 128].reshape(DP, 128))

    x = xs[...]
    gain_grad1 = jnp.sum(dact1 * x * r1, axis=0, keepdims=True)
    gains = jnp.concatenate([gain_grad1, gain_grad2, jnp.zeros((6, DP), F32)], axis=0)
    hot = jnp.where(
        lane_iota((8, 128)) == 64 + lax.broadcasted_iota(jnp.int32, (8, 128), 0), 1.0, 0.0
    )
    hot = jnp.where(lax.broadcasted_iota(jnp.int32, (8, 128), 0) < 2, hot, 0.0)
    gain_cols = mm(gains.T.astype(BF), hot.astype(BF))
    ga[1, :, :, 0:128] = (mm(a1t, dq[:, 512:640]) + gain_cols).astype(BF).reshape(8, 80, 128)
    red_a = reducer(WA, ga, gac, gax, ga2, gaz, ga3, gal, ga4, gay, gaf)
    red_a[0]()

    wgt = dact1 * gain1
    inner = jnp.sum(wgt * x, axis=-1, keepdims=True) * (1.0 / D)
    give_back(
        dmid[...] + r1 * wgt - x * (r1 * r1 * r1) * inner, ig_s, ig_r, sem_i
    )
    red_a[1]()
    red_b[5]()
    red_a[2]()
    red_b[6]()
    red_a[3]()
    red_a[4]()
    red_b[7]()
    gb_out[...] = gbf[...]
    red_a[5]()
    for step in range(1, 16):
        arrived(bo_r.at[(c + 16 - step) % 16], sem_o + step)
    bo_out[...] = bo_r[...]
    red_a[6]()
    for step in range(1, 16):
        arrived(ig_r.at[(c + 16 - step) % 16], sem_i + step)
    ig_out[...] = ig_r[...]
    red_a[7]()
    ga_out[...] = gaf[...]
    for copy in sends:
        copy.wait_send()


def tables():
    freq = np.power(np.float32(100000.0), -(np.arange(32, dtype=np.float32) * np.float32(2.0 / 64)))
    angle = np.arange(4096, dtype=np.float32)[:, None] * freq[None, :].astype(np.float32)
    cos, sin = np.cos(angle), np.sin(angle)
    cos = np.concatenate([cos, cos, cos, cos], axis=1)
    sin = np.concatenate([-sin, sin, -sin, sin], axis=1)
    shape = (32, 16, 8, 128)
    return cos.reshape(shape).astype(np.float32), sin.reshape(shape).astype(np.float32)


def pad_model(rows):
    return jnp.pad(rows.reshape(ROWS, 8, 72), ((0, 0), (0, 0), (0, 8))).reshape(ROWS, DP)


def by_target(rows):
    return rows.reshape(2, 16, 8, DP).transpose(1, 0, 2, 3).reshape(16, 16, DP)


def by_token(rows):
    rows = rows.reshape(16, 2, 8, 8, 80)[..., :72]
    return rows.transpose(1, 0, 2, 3, 4).reshape(1, ROWS, D)


def local(tokens, positions, gain1, wq, wkv, wo, gain2, wg, wu, wd, cotangent):
    place = (positions[0] // 128) * 8 + positions[0] % 8
    x = pad_model(tokens[0])
    x = jnp.where(lane_iota((ROWS, DP)) == 72, place[:, None].astype(BF), x)
    xc = jnp.concatenate([by_target(x), by_target(pad_model(cotangent[0]))], axis=1)
    w_kv = wkv.reshape(72, 2, 3, 64).transpose(0, 2, 1, 3).reshape(72, 384)
    gains = jnp.stack([gain1, gain2], axis=1)
    wa = jnp.concatenate([wq, gains, jnp.zeros((72, 62), BF), w_kv], axis=1)
    wa = jnp.pad(jnp.stack([wa[:, :WA], wa[:, WA:]]), ((0, 0), (0, 8), (0, 0)))
    wot, wdt = wo.T, wd.T
    wb = jnp.stack(
        [
            jnp.concatenate([wg, wdt[:, :768], wot[:, :512]], axis=1),
            jnp.concatenate([wu, wdt[:, 768:], wot[:, 512:], jnp.zeros((72, 448), BF)], axis=1),
        ]
    )
    wb = jnp.pad(wb, ((0, 0), (0, 8), (0, 0)))
    cos, sin = tables()

    def v(shape, dtype=BF):
        return pltpu.VMEM(shape, dtype)

    any_space = pl.BlockSpec(memory_space=pl.ANY)
    vmem = pl.BlockSpec(memory_space=pltpu.VMEM)
    scratch = [
        v((16, 32, DP)), v((2, 8, 80, WA)), v((2, 8, 80, WB)),
        v((32, 8, 128), F32), v((32, 8, 128), F32),
        v((16, 3, 256, 128)), v((2048, 128), F32), v((ROWS, ROWS)),
        v((3, 128, 768)), v((3, 768, 128)), v((3, 128, 768)), v((3, 768, 128)),
        v((3, 1, 768), F32), v((3, 1, 768), F32), v((3, 128, 768), F32), v((3, 128, 768), F32),
        v((3, 128, 768), F32),
        v((ROWS, DP), F32), v((ROWS, DP)), v((ROWS, DP), F32), v((ROWS, DP)), v((DP, ROWS)),
        v((ROWS, DP)), v((ROWS, DP), F32),
        v((4, 4, 3, 256, 128)), v((4, 2, 3, 256, 128)), v((4, 2, 3, 256, 128)),
        v((8, 3, 256, 128)),
        v((2, 8, 80, WA)), v((8, 80, WA)), v((8, 80, WB)),
        v((3, 2, 80, WA)), v((3, 2, 80, WB)), v((2, 80, WA)), v((2, 80, WB)),
        v((80, WA)), v((80, WB)), v((80, WA)), v((80, WB)),
        v((80, WA // 2)), v((80, WB // 2)), v((80, WA // 2)), v((80, WB // 2)),
        v((3, 80, WA // 2)), v((3, 80, WB // 2)), v((2, 80, WA)), v((2, 80, WB)),
        v((16, 16, DP)), v((16, 16, DP)), v((16, 16, DP)), v((16, 16, DP)),
        pltpu.SemaphoreType.DMA((140,)), pltpu.SemaphoreType.DMA((140,)),
        pltpu.SemaphoreType.DMA((5,)),
    ]
    bo, ig, ga, gb = pl.pallas_call(
        kernel,
        out_shape=(
            jax.ShapeDtypeStruct((16, 16, DP), BF),
            jax.ShapeDtypeStruct((16, 16, DP), BF),
            jax.ShapeDtypeStruct((2, 80, WA), BF),
            jax.ShapeDtypeStruct((2, 80, WB), BF),
        ),
        in_specs=[any_space] * 5,
        out_specs=(vmem,) * 4,
        scratch_shapes=scratch,
        compiler_params=pltpu.CompilerParams(
            collective_id=0, has_side_effects=True, vmem_limit_bytes=62 * 1024 * 1024
        ),
        name="layer",
    )(xc, wa, wb, jnp.asarray(cos), jnp.asarray(sin))

    ga = ga[:, :72].astype(F32)
    gb = gb[:, :72].astype(F32)
    g_q = jnp.concatenate([ga[0], ga[1, :, :64]], axis=1)
    g_kv = ga[1, :, 128:512].reshape(72, 3, 2, 64).transpose(0, 2, 1, 3).reshape(72, 384)
    g_out = jnp.concatenate([gb[0, :, 2304:2816], gb[1, :, 2304:2368]], axis=1).T
    g_down = jnp.concatenate([gb[0, :, 1536:2304], gb[1, :, 1536:2304]], axis=1).T
    return (
        by_token(bo),
        by_token(ig).astype(F32),
        ga[1, :, 64],
        g_q,
        g_kv,
        g_out,
        ga[1, :, 65],
        gb[0, :, :1536],
        gb[1, :, :1536],
        g_down,
    )


def solution(mesh):
    rows, model, last = P("fsdp", "ctx", None), P("fsdp", None), P(None, "fsdp")
    gain = P("fsdp")
    return jax.shard_map(
        local,
        mesh=mesh,
        in_specs=(rows, P("fsdp", "ctx"), gain, model, model, last, gain, model, model, last, rows),
        out_specs=(rows, rows, gain, model, model, last, gain, model, model, last),
        check_vma=False,
    )
```

```python
import numpy as np

import jax
import jax.numpy as jnp
from jax import lax
from jax.experimental import pallas as pl
from jax.experimental.pallas import tpu as pltpu
from jax.sharding import PartitionSpec as P

MESH = pl.DeviceIdType.MESH
BF = jnp.bfloat16
F32 = jnp.float32
D = 576
DP = 640
ROWS = 256
WA = 512
TB = 24
FC = 256
NEG = -1e30
STEPS = (0, 1, 3, 2)
BACK = (2, 1, 3, 0)
LAST = (1, 2)
CHIPS = ((0, 1), (0, 3), (1, 0), (1, 1), (1, 3), (0, 2), (1, 2))


def mm(a, b):
    return jnp.dot(a, b, preferred_element_type=F32)


def mm_nt(a, b):
    return lax.dot_general(a, b, (((1,), (1,)), ((), ())), preferred_element_type=F32)


def mm_tn(a, b):
    return lax.dot_general(a, b, (((0,), (0,)), ((), ())), preferred_element_type=F32)


def up_tile(half, t):
    return t if t < 10 else t + (6 if half == 0 else 4)


def down_tile(t):
    return t // 6, 10 + t % 6 if t < 10 else 6 + t


def lane_iota(shape):
    return lax.broadcasted_iota(jnp.int32, shape, len(shape) - 1)


def partner_lanes(u):
    lane = lane_iota(u.shape)
    return jnp.where(lane % 64 < 32, pltpu.roll(u, 96, 1), pltpu.roll(u, 32, 1))


def kernel(
    pos, g1_in, g2_in, tok_h, cot_h, wq_h, wkv_h, wo_h, wg_h, wu_h, wd_h, cols_h, rows_h, cos_in, sin_in,
    bo_out, ig_out, ga_out, gb_out,
    tok, cot, wq_in, wkv_in, wo_in, wg_in, wu_in, wd_in, spread_cols, spread_rows,
    xc, wa_in, wb_in, xc_r, wa, wb, cos_s, sin_s, kv, bias, perm,
    qt, qx, dot_, dox, st_m, st_l, acc, ot, dqt,
    xs, dy, mid, act1, act1t, attb, dmid,
    dkv_p, d1_r, d2_s, d2_r, dz_s, dz_r,
    ga, gac, gax, gay_s, gay, gaf,
    gbc, q1, t1, q2, t2, q3, gbf,
    bo_s, bo_r, ig_s, ig_r,
    ss, rs, ls,
):
    f = lax.axis_index("fsdp")
    c = lax.axis_index("ctx")
    zh, xx = f // 4, f % 4
    zl, yy, k = c // 8, (c // 2) % 4, c % 2
    fz = (1 - zh) * 4 + xx

    def ctx_at(z, y, core):
        return z * 8 + y * 2 + core

    def slot_at(z, y, core):
        return y * 4 + z * 2 + core

    other = ctx_at(zl, yy, 1 - k)
    sends = []
    used = [0]

    def take(n):
        used[0] += n
        return used[0] - n

    def remote(src, dst, sem, fs, cs):
        return pltpu.make_async_remote_copy(
            src_ref=src, dst_ref=dst, send_sem=ss.at[sem], recv_sem=rs.at[sem],
            device_id={"fsdp": fs, "ctx": cs}, device_id_type=MESH,
        )

    def send(src, dst, sem, fs, cs):
        copy = remote(src, dst, sem, fs, cs)
        copy.start()
        sends.append(copy)
        return copy

    def arrived(dst, sem):
        remote(dst, dst, sem, f, other).wait_recv()

    loads = [
        pltpu.make_async_copy(src, dst, ls.at[7 + n])
        for n, (src, dst) in enumerate(
            (
                (wq_h, wq_in), (wkv_h, wkv_in), (tok_h, tok), (cols_h, spread_cols),
                (rows_h, spread_rows), (cot_h, cot), (wg_h, wg_in), (wu_h, wu_in), (wd_h, wd_in),
                (wo_h, wo_in),
            )
        )
    ]
    for copy in loads:
        copy.start()

    barrier = pltpu.get_barrier_semaphore()
    for step in range(1, 16):
        pl.semaphore_signal(
            barrier, inc=1, device_id={"fsdp": f, "ctx": (c + step) % 16}, device_id_type=MESH
        )
    for step in range(1, 8):
        pl.semaphore_signal(
            barrier, inc=1, device_id={"fsdp": (f + step) % 8, "ctx": c}, device_id_type=MESH
        )
    pl.semaphore_signal(
        barrier, inc=1, device_id={"fsdp": fz, "ctx": ctx_at(1 - zl, yy, k)}, device_id_type=MESH
    )

    rows_of = lax.broadcasted_iota(jnp.int32, (ROWS, 1), 0)
    run = jnp.where((rows_of // 8) % 2 == 0, pos[0, 0], pos[0, 128]).astype(F32)
    tag = run * (1.0 / 16.0) + (rows_of % 8).astype(F32)

    def pack_rows(ref):
        return mm(spread_rows[...], mm_tn(ref[...], spread_cols[...]).astype(BF))

    for copy in loads:
        copy.wait()
    xc[:, 0:16, :] = (
        jnp.where(lane_iota((ROWS, DP)) == 72, tag, pack_rows(tok)).astype(BF).reshape(16, 16, DP)
    )
    xc[:, 16:32, :] = pack_rows(cot).astype(BF).reshape(16, 16, DP)

    def pad_rows(value):
        return jnp.concatenate([value.astype(F32), jnp.zeros((8, value.shape[1]), F32)], axis=0)

    wq_all = pad_rows(wq_in[...])
    wkv_all = pad_rows(wkv_in[...])
    low80 = lane_iota((80, 128)) < 64
    wa_in[0] = wq_all[:, 0:512].astype(BF)
    row16 = lax.broadcasted_iota(jnp.int32, (16, 72), 0)
    gains_in = jnp.where(row16 == 0, g1_in[...].astype(F32), g2_in[...].astype(F32))
    gains_in = jnp.where(row16 < 2, gains_in, 0.0).astype(BF)
    row_hot = lax.broadcasted_iota(jnp.int32, (16, 128), 0)
    gain_hot = jnp.where((lane_iota((16, 128)) == 64 + row_hot) & (row_hot < 2), 1.0, 0.0).astype(BF)
    last_q = jnp.concatenate([wq_all[:, 512:576], jnp.zeros((80, 64), F32)], axis=1)
    wa_in[1, :, 0:128] = (last_q + pad_rows(mm_tn(gains_in, gain_hot))).astype(BF)

    def kv_head(n, want_low):
        block = wkv_all[:, 128 * (n // 2) : 128 * (n // 2) + 128]
        return block if (n % 2 == 0) == want_low else pltpu.roll(block, 64, 1)

    for g in range(3):
        both = jnp.where(low80, kv_head(g, True), kv_head(3 + g, False))
        wa_in[1, :, 128 + 128 * g : 256 + 128 * g] = both.astype(BF)

    for half, ref in ((0, wg_in), (1, wu_in)):
        whole = pad_rows(ref[...]).astype(BF)
        for t in range(12):
            wb_in[half, up_tile(half, t)] = whole[:, 128 * t : 128 * t + 128]
    whole = pad_rows(wd_in[...]).astype(BF)
    for t in range(12):
        half, at = down_tile(t)
        wb_in[half, at] = whole[:, 128 * t : 128 * t + 128]
    whole = jnp.concatenate([pad_rows(wo_in[...]), jnp.zeros((80, 64), F32)], axis=1).astype(BF)
    for t in range(5):
        wb_in[t // 4, 18 + t % 4] = whole[:, 128 * t : 128 * t + 128]
    wb_in[0, 22:24] = jnp.zeros((2, 80, 128), BF)
    wb_in[1, 19:24] = jnp.zeros((5, 80, 128), BF)
    pl.semaphore_wait(barrier, 23)

    zz = 2 * zh + zl
    order = ("ayb", "yba", "yab")

    def pick(n, u, w):
        return u if n < 2 else u * (1 - k) + w * k

    def coord(n, axis):
        if axis == "y":
            return yy
        return pick(n, zz, xx) if axis == "a" else pick(n, xx, zz)

    def along(n, axis, step):
        if axis == "y":
            return f, ctx_at(zl, (yy + step) % 4, k)
        z = (zz + step) % 4
        by_x = (zh * 4 + (xx + step) % 4, c)
        by_z = ((z // 2) * 4 + xx, ctx_at(z % 2, yy, k))
        first, second = (by_z, by_x) if axis == "a" else (by_x, by_z)
        return pick(n, first[0], second[0]), pick(n, first[1], second[1])

    def region(n, done, axis=None, step=0):
        at = []
        for name in "aby":
            if name in done:
                at.append(slice(None))
            else:
                at.append((coord(n, name) + 4 - step) % 4 if name == axis else coord(n, name))
        return wb.at[(k, n, *at)]

    sem_x = take(16)
    for step in range(1, 16):
        send(xc.at[(c + step) % 16], xc_r.at[c], sem_x + step, f, (c + step) % 16)
    local = [
        pltpu.make_async_copy(xc.at[c], xc_r.at[c], ls.at[0]),
        pltpu.make_async_copy(wa_in.at[k], wa.at[k, f], ls.at[1]),
        *(
            pltpu.make_async_copy(
                wb_in.at[k, 8 * n + 2 * yy + zl], region(n, ()), ls.at[4 + n]
            )
            for n in range(3)
        ),
        pltpu.make_async_copy(cos_in.at[:, c], cos_s, ls.at[2]),
        pltpu.make_async_copy(sin_in.at[:, c], sin_s, ls.at[3]),
    ]
    for copy in local:
        copy.start()

    def gather_first(w_in, w, sem):
        send(w_in.at[k], w.at[k, f], sem, fz, c)
        for step in range(1, 4):
            send(w_in.at[k], w.at[k, f], sem + step, zh * 4 + (xx + step) % 4, c)

    def gather_second(w, sem):
        arrived(w.at[k, fz], sem)
        return [
            send(w.at[k, fz], w.at[k, fz], sem + 3 + step, zh * 4 + (xx + step) % 4, c)
            for step in range(1, 4)
        ]

    def gather_third(w, sem):
        for step in range(1, 4):
            from_x = (xx + 4 - step) % 4
            arrived(w.at[k, zh * 4 + from_x], sem + step)
            arrived(w.at[k, (1 - zh) * 4 + from_x], sem + 3 + step)
        return [send(w.at[k], w.at[k], sem + 7, f, other)]

    def gather_last(w, sem):
        arrived(w.at[1 - k], sem + 7)

    sem_b = take(30)

    def spread(turn):
        if turn > 0:
            spread_wait(turn - 1)
        out = []
        for n in range(3):
            axis, done = order[n][turn], order[n][:turn]
            for step in range(1, 4):
                if turn == 0:
                    src = wb_in.at[k, 8 * n + 2 * yy + zl]
                else:
                    src = region(n, done)
                copy = send(
                    src, region(n, done), sem_b + 9 * turn + 3 * n + step - 1, *along(n, axis, step)
                )
                if turn > 0:
                    out.append(copy)
        return out

    def spread_wait(turn, groups=(0, 1, 2)):
        for n in groups:
            axis, done = order[n][turn], order[n][:turn]
            for step in range(1, 4):
                arrived(region(n, done, axis, step), sem_b + 9 * turn + 3 * n + step - 1)

    sem_a = take(8)
    gather_first(wa_in, wa, sem_a)
    spread(0)

    def make_bias(slot, carry):
        e = ctx_at((slot // 2) % 2, slot // 4, slot % 2)
        j = lax.broadcasted_iota(jnp.int32, (128, 128), 0)
        i = lax.broadcasted_iota(jnp.int32, (128, 128), 1)
        ok = (j // 8 < i // 8) | ((j // 8 == i // 8) & (8 * e + j % 8 <= 8 * c + i % 8))
        bias[pl.ds(pl.multiple_of(slot * 128, 128), 128), :] = jnp.where(ok, 0.0, NEG)
        return carry

    lax.fori_loop(0, 16, make_bias, 0)
    gather_second(wa, sem_a)
    for copy in local:
        copy.wait()
    for step in range(1, 16):
        arrived(xc_r.at[(c + 16 - step) % 16], sem_x + step)

    x_raw = xc_r[:, 0:16, :].reshape(ROWS, DP)
    lane = lane_iota((ROWS, DP))
    tag = jnp.sum(jnp.where(lane == 72, x_raw.astype(F32), 0.0), axis=1, keepdims=True)
    place = lane_iota((ROWS, ROWS)).astype(F32)
    perm[...] = jnp.where(tag == place, 1.0, 0.0).astype(BF)
    perm_t = jnp.where(tag == place, 1.0, 0.0).T.astype(BF)
    x = mm(perm_t, x_raw)
    x = jnp.where(lane % 80 < 72, x, 0.0)
    xs[...] = x
    dy[...] = mm(perm_t, xc_r[:, 16:32, :].reshape(ROWS, DP)).astype(BF)

    from_wb = spread(1)
    gather_third(wa, sem_a)
    r1 = lax.rsqrt(jnp.sum(x * x, axis=-1, keepdims=True) * (1.0 / D) + 1e-5)
    gather_last(wa, sem_a)

    def gain_row(which):
        hot = jnp.where(lane_iota((16, 128)) == 64 + which, 1.0, 0.0).astype(BF)
        block = wa[1, :, :, 0:128].reshape(DP, 128)
        return mm_nt(hot, block)[0:1, :]

    gain1, gain2 = gain_row(0), gain_row(1)
    a1 = x * r1 * gain1
    a1b = a1.astype(BF)
    act1[...] = a1b
    act1t[...] = a1.T.astype(BF)

    cos = cos_s[...].reshape(ROWS, 128)
    sin = sin_s[...].reshape(ROWS, 128)
    low = lane_iota((ROWS, 128)) < 64
    cos_kv = jnp.where(low, cos, 1.0)
    sin_kv = jnp.where(low, sin, 0.0)

    mine = slot_at(zl, yy, k)
    kv_pre = mm(a1b, wa[1, :, :, 128:512].reshape(DP, 384))
    for g in range(3):
        u = kv_pre[:, 128 * g : 128 * g + 128]
        kv[mine, g] = (u * cos_kv + partner_lanes(u) * sin_kv).astype(BF)
    sem_k = take(16)

    near = slot_at(1 - zl, yy, k)

    def kv_along_y(slot, a):
        for off in STEPS[1:]:
            send(kv.at[slot], kv.at[slot], sem_k + a * 4 + off, f, ctx_at(zl, (yy + off) % 4, k))

    send(kv.at[mine], kv.at[mine], sem_k, f, other)
    send(kv.at[mine], kv.at[mine], sem_k + 4, f, ctx_at(1 - zl, yy, k))
    kv_along_y(mine, 0)

    def kv_direct(off):
        for a in (0, 1):
            if (a, off) != (0, 0):
                at = slot_at(zl if a == 0 else 1 - zl, (yy + 4 - off) % 4, k)
                arrived(kv.at[at], sem_k + a * 4 + off)
                send(kv.at[at], kv.at[at], sem_k + 8 + a * 4 + off, f, other)

    def kv_across(off):
        for a in (0, 1):
            at = slot_at(zl if a == 0 else 1 - zl, (yy + 4 - off) % 4, 1 - k)
            arrived(kv.at[at], sem_k if (a, off) == (0, 0) else sem_k + 8 + a * 4 + off)

    from_wb += spread(2)

    for t in range(5):
        w = wa[0, :, :, 128 * t : 128 * t + 128] if t < 4 else wa[1, :, :, 0:128]
        u = mm(a1b, w.reshape(DP, 128))
        u = (u * cos + partner_lanes(u) * sin).astype(BF).astype(F32) * 0.125
        for half in range(2):
            h = 2 * t + half
            if h < 9:
                g, r = h // 3, h % 3
                v = jnp.where(low, u if half == 0 else pltpu.roll(u, 64, 1), 0.0)
                vt = v.T
                for ih in range(2):
                    at = 384 * ih + 128 * r
                    qx[g, at : at + 128, :] = v[128 * ih : 128 * ih + 128].astype(BF)
                    qt[g, :, at : at + 128] = vt[:, 128 * ih : 128 * ih + 128].astype(BF)

    kv_direct(0)
    kv_along_y(near, 1)

    st_m[...] = jnp.full(st_m.shape, NEG, F32)
    st_l[...] = jnp.zeros(st_l.shape, F32)
    acc[...] = jnp.zeros(acc.shape, F32)

    def three(b):
        return jnp.concatenate([b, b, b], axis=1)

    def fold_forward(off):
        group = (yy + 4 - off) % 4

        def per_head(g, carry):
            b3 = three(bias[pl.ds(pl.multiple_of(group * 512, 512), 512), :])
            for key_half, lane_half in ((0, 0), (0, 1), (1, 1)):
                at = 384 * lane_half
                rows = kv[pl.ds(group * 4, 4), g, 128 * key_half : 128 * key_half + 128, :]
                rows = rows.reshape(512, 128)
                s = mm(rows, qt[g, :, at : at + 384])
                if key_half == lane_half:
                    s = s + b3
                old = st_m[g, :, at : at + 384]
                new = jnp.maximum(old, jnp.max(s, axis=0, keepdims=True))
                p = jnp.exp(s - new)
                scale = jnp.exp(old - new)
                st_m[g, :, at : at + 384] = new
                st_l[g, :, at : at + 384] = (
                    st_l[g, :, at : at + 384] * scale + jnp.sum(p, axis=0, keepdims=True)
                )
                acc[g, :, at : at + 384] = acc[g, :, at : at + 384] * scale + mm_tn(
                    rows, p.astype(BF)
                )
            return carry

        lax.fori_loop(0, 3, per_head, 0)

    kv_direct(STEPS[1])
    kv_across(0)
    fold_forward(0)
    kv_direct(STEPS[2])
    kv_across(STEPS[1])
    fold_forward(STEPS[1])
    kv_direct(STEPS[3])
    kv_across(STEPS[2])
    fold_forward(STEPS[2])
    kv_across(STEPS[3])
    for n in (1, 0, 2):
        spread_wait(2, (n,))
        from_wb.append(send(wb.at[k, n], wb.at[k, n], sem_b + 27 + n, f, other))
    fold_forward(STEPS[3])

    def head_rows(ref, g, r):
        return jnp.concatenate(
            [ref[g, :, 384 * ih + 128 * r : 384 * ih + 128 * r + 128].T for ih in range(2)], axis=0
        )

    for g in range(3):
        ot[g] = acc[g] / st_l[g]
        st_l[g] = st_m[g] + jnp.log(st_l[g])
    for t in range(5):
        a = pltpu.roll(head_rows(ot, 2 * t // 3, 2 * t % 3), 64, 1)
        b = head_rows(ot, (2 * t + 1) // 3, (2 * t + 1) % 3) if t < 4 else jnp.zeros((ROWS, 128), F32)
        attb[:, 128 * t : 128 * t + 128] = jnp.where(low, a, b).astype(BF)

    for n in range(3):
        arrived(wb.at[1 - k, n], sem_b + 27 + n)

    def fixed(half, n):
        return isinstance(half, int) and isinstance(n, int) and (half, n) == LAST

    def tile_at(half, n, y, z):
        if fixed(half, n):
            blocks = [wb[1, 2, :, 2 * q + z, y] for q in range(2)]
        else:
            blocks = [wb[half, n, 2 * q + z, :, y] for q in range(2)]
        return jnp.concatenate(blocks, axis=0).reshape(DP, 128)

    def put_tile(half, n, y, z, value):
        value = value.astype(BF).reshape(2, 4, 80, 128)
        for q in range(2):
            if fixed(half, n):
                wb[1, 2, :, 2 * q + z, y] = value[q]
            else:
                wb[half, n, 2 * q + z, :, y] = value[q]

    def pair(half, p):
        return jnp.concatenate([tile_at(half, p // 4, p % 4, z) for z in range(2)], axis=1)

    def put_pair(half, p, value):
        for z in range(2):
            put_tile(half, p // 4, p % 4, z, value[:, 128 * z : 128 * z + 128])

    def out_tile(t):
        return tile_at(0, 2, 1 + t // 2, t % 2) if t < 4 else tile_at(1, 2, 1, 0)

    out_w = jnp.concatenate([out_tile(t) for t in range(5)], axis=1)
    m0 = xs[...] + mm_nt(attb[...], out_w)
    r2 = lax.rsqrt(jnp.sum(m0 * m0, axis=-1, keepdims=True) * (1.0 / D) + 1e-5)
    mid[...] = m0
    a2 = m0 * r2 * gain2
    a2b = a2.astype(BF)
    a2t = a2.T.astype(BF)
    dyb = dy[...]
    dyt = dyb.astype(F32).T.astype(BF)

    for copy in from_wb:
        copy.wait_send()
    sends[:] = [copy for copy in sends if all(copy is not done for done in from_wb)]

    def ff(j, carry):
        total, dact = carry
        last = isinstance(j, int)
        at_g, at_u, at_d = ((0, 8), (1, 7), (1, 8)) if last else ((0, j), (1, j), (j // 3, 5 + j % 3))
        wg, wu, wd = pair(*at_g), pair(*at_u), pair(*at_d)
        gate, up = mm(a2b, wg), mm(a2b, wu)
        sig = jax.nn.sigmoid(gate)
        swish = gate * sig
        hid = (swish * up).astype(BF)
        total = total + mm_nt(hid, wd)
        dh = mm(dyb, wd)
        dg = (dh * up * sig * (1.0 + gate * (1.0 - sig))).astype(BF)
        du = (dh * swish).astype(BF)
        put_pair(*at_d, mm(dyt, hid))
        put_pair(*at_g, mm(a2t, dg))
        put_pair(*at_u, mm(a2t, du))
        dact = dact + mm_nt(dg, wg) + mm_nt(du, wu)
        return total, dact

    zero = jnp.zeros((ROWS, DP), F32)
    total, dact = ff(5, lax.fori_loop(0, 5, ff, (zero, zero)))

    sem_r = take(42)

    def add(ref, at, got_at):
        v = ref[at].astype(F32)
        for r in got_at:
            v = v + r.astype(F32)
        return v

    def red_core(n):
        send(wb.at[1 - k, n], gbc.at[n], sem_r + n, f, other)

    def red_one(n):
        arrived(gbc.at[n], sem_r + n)

        def body(i, carry):
            wb[k, n, i // 4, i % 4] = (
                wb[k, n, i // 4, i % 4].astype(F32) + gbc[n, i // 4, i % 4].astype(F32)
            ).astype(BF)
            return carry

        lax.fori_loop(0, 16, body, 0)
        axis = order[n][2]
        for step in range(1, 4):
            to = (coord(n, axis) + step) % 4
            src = wb.at[k, n, to] if axis == "a" else wb.at[k, n, :, to]
            send(src, q1.at[n, step - 1], sem_r + 3 + 3 * n + step - 1, *along(n, axis, step))

    def red_two(n):
        for step in range(3):
            arrived(q1.at[n, step], sem_r + 3 + 3 * n + step)
        axis, at = order[n][2], coord(n, order[n][2])

        def body(i, carry):
            v = (wb[k, n, at, i] if axis == "a" else wb[k, n, i, at]).astype(F32)
            for step in range(3):
                v = v + q1[n, step, i].astype(F32)
            t1[n, i] = v.astype(BF)
            return carry

        lax.fori_loop(0, 4, body, 0)
        axis = order[n][1]
        for step in range(1, 4):
            to = (coord(n, axis) + step) % 4
            src = t1.at[n, :, to] if axis == "y" else t1.at[n, to]
            send(src, q2.at[n, step - 1], sem_r + 12 + 3 * n + step - 1, *along(n, axis, step))

    def red_three(n):
        for step in range(3):
            arrived(q2.at[n, step], sem_r + 12 + 3 * n + step)
        axis, at = order[n][1], coord(n, order[n][1])
        own = (n, slice(None), at) if axis == "y" else (n, at)
        t2[n] = add(t1, own, [q2[n, i] for i in range(3)]).astype(BF)
        axis = order[n][0]
        for step in range(1, 4):
            to = (coord(n, axis) + step) % 4
            send(t2.at[n, to], q3.at[n, step - 1], sem_r + 21 + 3 * n + step - 1, *along(n, axis, step))

    def red_four():
        for n in range(3):
            for step in range(3):
                arrived(q3.at[n, step], sem_r + 21 + 3 * n + step)
            own = add(t2, (n, coord(n, order[n][0])), [q3[n, i] for i in range(3)])
            gbf[k, yy, zl, n] = own.astype(BF)
        piece = gbf.at[k, yy, zl]
        for a, off in CHIPS:
            to = ctx_at(zl if a == 0 else 1 - zl, (yy + off) % 4, k)
            send(piece, piece, sem_r + 30 + 4 * a + off, f, to)

    def red_five():
        for a, off in CHIPS:
            z = zl if a == 0 else 1 - zl
            arrived(gbf.at[k, (yy + 4 - off) % 4, z], sem_r + 30 + 4 * a + off)
        send(gbf.at[k], gbf.at[k], sem_r + 38, f, other)

    def red_six():
        arrived(gbf.at[1 - k], sem_r + 38)

    sem_g = take(24)

    def in_core():
        send(ga.at[1 - k], gac, sem_g, f, other)

    def in_one():
        arrived(gac, sem_g)
        ga[k] = (ga[k].astype(F32) + gac[...].astype(F32)).astype(BF)
        for step in range(1, 8):
            to = (f + step) % 8
            send(ga.at[k, to], gax.at[step - 1], sem_g + step, to, c)

    def in_two():
        for step in range(1, 8):
            arrived(gax.at[step - 1], sem_g + step)
        v = add(ga, (k, f), [gax[i] for i in range(7)])
        for t in range(4):
            gay_s[t] = v[:, 128 * t : 128 * t + 128].astype(BF)
        for a, off in CHIPS:
            y = (yy + off) % 4
            to = ctx_at(zl if a == 0 else 1 - zl, y, k)
            send(gay_s.at[y], gay.at[4 * a + off], sem_g + 8 + 4 * a + off, f, to)

    def in_three():
        for a, off in CHIPS:
            arrived(gay.at[4 * a + off], sem_g + 8 + 4 * a + off)
        gaf[k, yy] = add(gay_s, yy, [gay[4 * a + off] for a, off in CHIPS]).astype(BF)
        for step in range(1, 4):
            send(gaf.at[k, yy], gaf.at[k, yy], sem_g + 16 + step, *along(0, "y", step))

    def in_four():
        for step in range(1, 4):
            arrived(gaf.at[k, (yy + 4 - step) % 4], sem_g + 16 + step)
        send(gaf.at[k], gaf.at[k], sem_g + 20, f, other)

    def in_five():
        arrived(gaf.at[1 - k], sem_g + 20)

    red_core(0)
    red_core(1)

    def give_back(value, src, dst, sem):
        src[...] = mm(perm[...], value.astype(BF)).astype(BF).reshape(16, 16, DP)
        for step in range(1, 16):
            send(src.at[(c + step) % 16], dst.at[c], sem + step, f, (c + step) % 16)
        dst[c] = src[c]

    sem_o = take(16)
    sem_i = take(16)
    m0 = mid[...]
    give_back(m0 + total, bo_s, bo_r, sem_o)

    dyf = dyb.astype(F32)
    gain_grad2 = jnp.sum(dact * m0 * r2, axis=0, keepdims=True)
    wgt = dact * gain2
    inner = jnp.sum(wgt * m0, axis=-1, keepdims=True) * (1.0 / D)
    dm = dyf + r2 * wgt - m0 * (r2 * r2 * r2) * inner
    dmid[...] = dm
    dmb = dm.astype(BF)
    dmt = dm.T.astype(BF)

    for t in range(5):
        u = mm(dmb, out_tile(t)).astype(BF).astype(F32)
        for half in range(2):
            h = 2 * t + half
            if h < 9:
                g, r = h // 3, h % 3
                v = jnp.where(low, 0.0, u if half == 1 else pltpu.roll(u, 64, 1))
                vt = v.T
                for ih in range(2):
                    at = 384 * ih + 128 * r
                    dox[g, at : at + 128, :] = v[128 * ih : 128 * ih + 128].astype(BF)
                    dot_[g, :, at : at + 128] = vt[:, 128 * ih : 128 * ih + 128].astype(BF)
    grad_out = mm(dmt, attb[...]).astype(BF)
    for t in range(5):
        at = (0, 2, 1 + t // 2, t % 2) if t < 4 else (1, 2, 1, 0)
        put_tile(*at, grad_out[:, 128 * t : 128 * t + 128])
    red_core(2)

    for g in range(3):
        st_m[g] = jnp.sum(dot_[g].astype(F32) * ot[g], axis=0, keepdims=True)
    dqt[...] = jnp.zeros(dqt.shape, F32)

    def fold_backward(at_step, off):
        group = (yy + 4 - off) % 4

        def per_head(g, carry):
            b3 = three(bias[pl.ds(pl.multiple_of(group * 512, 512), 512), :])
            for key_half in range(2):
                rows = kv[pl.ds(group * 4, 4), g, 128 * key_half : 128 * key_half + 128, :]
                rows = rows.reshape(512, 128)
                grad = None
                for lane_half in range(key_half, 2):
                    at = 384 * lane_half
                    s = mm(rows, qt[g, :, at : at + 384])
                    if key_half == lane_half:
                        s = s + b3
                    p = jnp.exp(s - st_l[g, :, at : at + 384])
                    dp = mm(rows, dot_[g, :, at : at + 384])
                    ds = (p * (dp - st_m[g, :, at : at + 384])).astype(BF)
                    part = mm(ds, qx[g, at : at + 384, :]) + mm(
                        p.astype(BF), dox[g, at : at + 384, :]
                    )
                    grad = part if grad is None else grad + part
                    dqt[g, :, at : at + 384] += mm_tn(rows, ds)
                dkv_p[at_step, :, g, 128 * key_half : 128 * key_half + 128, :] = grad.astype(
                    BF
                ).reshape(4, 128, 128)
            return carry

        lax.fori_loop(0, 3, per_head, 0)

    sem_d1 = take(8)
    sem_d = take(4)

    def dkv_first(at_step):
        for z in range(2):
            send(
                dkv_p.at[at_step, 2 * z + 1 - k], d1_r.at[at_step, z], sem_d1 + 2 * at_step + z,
                f, other,
            )

    def dkv_second(at_step, off):
        for z in range(2):
            arrived(d1_r.at[at_step, z], sem_d1 + 2 * at_step + z)
        for z in range(2):
            d2_s[at_step, z] = (
                dkv_p[at_step, 2 * z + k].astype(F32) + d1_r[at_step, z].astype(F32)
            ).astype(BF)
        if off != 0:
            send(
                d2_s.at[at_step], d2_r.at[off - 1], sem_d + off,
                f, ctx_at(zl, (yy + 4 - off) % 4, k),
            )

    red_one(0)
    red_one(1)
    red_one(2)
    fold_backward(0, BACK[0])
    dkv_first(0)
    dkv_second(0, BACK[0])
    fold_backward(1, BACK[1])
    dkv_first(1)
    dkv_second(1, BACK[1])
    fold_backward(2, BACK[2])
    dkv_first(2)
    dkv_second(2, BACK[2])
    for n in range(3):
        red_two(n)
    fold_backward(3, BACK[3])
    dkv_first(3)
    for n in range(3):
        red_three(n)

    dq_tiles = []
    for t in range(5):
        a = head_rows(dqt, 2 * t // 3, 2 * t % 3)
        if t < 4:
            b = pltpu.roll(head_rows(dqt, (2 * t + 1) // 3, (2 * t + 1) % 3), 64, 1)
        else:
            b = jnp.zeros((ROWS, 128), F32)
        u = jnp.where(low, a, b) * 0.125
        dq_tiles.append((u * cos - partner_lanes(u) * sin).astype(BF))
    dq = jnp.concatenate(dq_tiles, axis=1)
    a1t = act1t[...]
    ga[0] = mm(a1t, dq[:, 0:512]).astype(BF).reshape(8, 80, 512)
    dact1 = mm_nt(dq[:, 0:512], wa[0].reshape(DP, 512)) + mm_nt(
        dq[:, 512:640], wa[1, :, :, 0:128].reshape(DP, 128)
    )
    dkv_second(3, BACK[3])
    for off in range(1, 4):
        arrived(d2_r.at[off - 1], sem_d + off)
    dz_s[...] = add(d2_s, (3, 1 - zl), [d2_r[i, 1 - zl] for i in range(3)]).astype(BF)
    send(dz_s, dz_r, sem_d, f, ctx_at(1 - zl, yy, k))
    red_four()
    dkv = add(d2_s, (3, zl), [d2_r[i, zl] for i in range(3)])
    arrived(dz_r, sem_d)
    dkv = dkv + dz_r[...].astype(F32)
    for g in range(3):
        u = dkv[g]
        u = (u * cos_kv - partner_lanes(u) * sin_kv).astype(BF)
        at = 128 + 128 * g
        ga[1, :, :, at : at + 128] = mm(a1t, u).astype(BF).reshape(8, 80, 128)
        dact1 = dact1 + mm_nt(u, wa[1, :, :, at : at + 128].reshape(DP, 128))

    x = xs[...]
    gain_grad1 = jnp.sum(dact1 * x * r1, axis=0, keepdims=True)
    gains = jnp.concatenate([gain_grad1, gain_grad2, jnp.zeros((6, DP), F32)], axis=0)
    hot = jnp.where(
        lane_iota((8, 128)) == 64 + lax.broadcasted_iota(jnp.int32, (8, 128), 0), 1.0, 0.0
    )
    hot = jnp.where(lax.broadcasted_iota(jnp.int32, (8, 128), 0) < 2, hot, 0.0)
    gain_cols = mm(gains.T.astype(BF), hot.astype(BF))
    ga[1, :, :, 0:128] = (mm(a1t, dq[:, 512:640]) + gain_cols).astype(BF).reshape(8, 80, 128)
    in_core()

    wgt = dact1 * gain1
    inner = jnp.sum(wgt * x, axis=-1, keepdims=True) * (1.0 / D)
    give_back(
        dmid[...] + r1 * wgt - x * (r1 * r1 * r1) * inner, ig_s, ig_r, sem_i
    )
    in_one()
    red_five()
    for step in range(1, 16):
        arrived(bo_r.at[(c + 16 - step) % 16], sem_o + step)
    bo_out[...] = bo_r[...]
    red_six()
    gb_out[...] = gbf[...]
    in_two()
    in_three()
    for step in range(1, 16):
        arrived(ig_r.at[(c + 16 - step) % 16], sem_i + step)
    ig_out[...] = ig_r[...]
    in_four()
    in_five()
    ga_out[...] = gaf[...]
    for copy in sends:
        copy.wait_send()


def tables():
    freq = np.power(np.float32(100000.0), -(np.arange(32, dtype=np.float32) * np.float32(2.0 / 64)))
    angle = np.arange(4096, dtype=np.float32)[:, None] * freq[None, :].astype(np.float32)
    cos, sin = np.cos(angle), np.sin(angle)
    cos = np.concatenate([cos, cos, cos, cos], axis=1)
    sin = np.concatenate([-sin, sin, -sin, sin], axis=1)
    shape = (32, 16, 8, 128)
    return cos.reshape(shape).astype(np.float32), sin.reshape(shape).astype(np.float32)


def placements():
    cols = np.zeros((D, DP), np.float32)
    at = np.arange(D)
    cols[at, at // 72 * 80 + at % 72] = 1.0
    rows = np.zeros((ROWS, ROWS), np.float32)
    at = np.arange(ROWS)
    rows[at, at // 8 % 2 * 128 + at // 16 * 8 + at % 8] = 1.0
    return jnp.asarray(cols, BF), jnp.asarray(rows, BF)


def finish(
    bo_h, ig_h, ga_h, gb_h, cols_h, rows_h,
    out, grad_in, n1, gq, gkv, go, n2, gg, gu, gd,
    bo, ig, ga, gb, cols, rows, sems,
):
    copies = [
        pltpu.make_async_copy(src, dst, sems.at[n])
        for n, (src, dst) in enumerate(
            ((gb_h, gb), (cols_h, cols), (rows_h, rows), (bo_h, bo), (ig_h, ig), (ga_h, ga))
        )
    ]
    for copy in copies:
        copy.start()
    for copy in copies:
        copy.wait()
    for src, dst in ((bo, out), (ig, grad_in)):
        narrow = mm_nt(cols[...], src[...].reshape(ROWS, DP)).astype(BF)
        dst[...] = mm(narrow, rows[...]).astype(dst.dtype)

    def part(ref, *at):
        return ref[at].astype(F32)

    for t in range(4):
        gq[:, 128 * t : 128 * t + 128] = part(ga, 0, t)[0:72]
    last = part(ga, 1, 0)
    gq[:, 512:576] = last[0:72, 0:64]
    row = lax.broadcasted_iota(jnp.int32, (16, 128), 0)
    hot = jnp.where((lane_iota((16, 128)) == 64 + row) & (row < 2), 1.0, 0.0).astype(BF)
    gains = mm_nt(hot, ga[1, 0])
    n1[...] = gains[0:1, 0:72]
    n2[...] = gains[1:2, 0:72]
    low = lane_iota((80, 128)) < 64
    tiles = [part(ga, 1, 1 + g) for g in range(3)]
    turn = [pltpu.roll(t, 64, 1) for t in tiles]
    heads = [
        jnp.where(low, tiles[0], turn[1]),
        jnp.where(low, tiles[2], tiles[0]),
        jnp.where(low, turn[1], tiles[2]),
    ]
    for g in range(3):
        gkv[:, 128 * g : 128 * g + 128] = heads[g][0:72]

    def tile(half, t):
        return part(gb, half, (t % 8) // 2, t % 2, t // 8)

    for half, ref in ((0, gg), (1, gu)):
        for t in range(12):
            ref[:, 128 * t : 128 * t + 128] = tile(half, up_tile(half, t))[0:72]
    for t in range(12):
        gd[:, 128 * t : 128 * t + 128] = tile(*down_tile(t))[0:72]
    for t in range(4):
        go[:, 128 * t : 128 * t + 128] = tile(0, 18 + t)[0:72]
    go[:, 512:576] = tile(1, 18)[0:72, 0:64]


def local(tokens, positions, gain1, wq, wkv, wo, gain2, wg, wu, wd, cotangent):
    cos, sin = tables()
    cols, rows = placements()

    def v(shape, dtype=BF):
        return pltpu.VMEM(shape, dtype)

    any_space = pl.BlockSpec(memory_space=pl.ANY)
    vmem = pl.BlockSpec(memory_space=pltpu.VMEM)
    scratch = [
        v((D, ROWS)), v((D, ROWS)), v((72, 576)), v((72, 384)), v((72, 576)), v((72, 1536)),
        v((72, 1536)), v((72, 1536)), v((D, DP)), v((ROWS, ROWS)),
        v((16, 32, DP)), v((2, 80, WA)), v((2, TB, 80, 128)),
        v((16, 32, DP)), v((2, 8, 80, WA)), v((2, 3, 4, 4, 4, 80, 128)),
        v((32, 8, 128), F32), v((32, 8, 128), F32),
        v((16, 3, 256, 128)), v((2048, 128), F32), v((ROWS, ROWS)),
        v((3, 128, 768)), v((3, 768, 128)), v((3, 128, 768)), v((3, 768, 128)),
        v((3, 1, 768), F32), v((3, 1, 768), F32), v((3, 128, 768), F32), v((3, 128, 768), F32),
        v((3, 128, 768), F32),
        v((ROWS, DP), F32), v((ROWS, DP)), v((ROWS, DP), F32), v((ROWS, DP)), v((DP, ROWS)),
        v((ROWS, DP)), v((ROWS, DP), F32),
        v((4, 4, 3, 256, 128)), v((4, 2, 3, 256, 128)), v((4, 2, 3, 256, 128)),
        v((3, 2, 3, 256, 128)), v((3, 256, 128)), v((3, 256, 128)),
        v((2, 8, 80, WA)), v((8, 80, WA)), v((7, 80, WA)),
        v((4, 80, 128)), v((8, 80, 128)), v((2, 4, 80, 128)),
        v((3, 4, 4, 4, 80, 128)), v((3, 3, 4, 4, 80, 128)), v((3, 4, 4, 80, 128)),
        v((3, 3, 4, 80, 128)), v((3, 4, 80, 128)),
        v((3, 3, 80, 128)), v((2, 4, 2, 3, 80, 128)),
        v((16, 16, DP)), v((16, 16, DP)), v((16, 16, DP)), v((16, 16, DP)),
        pltpu.SemaphoreType.DMA((184,)), pltpu.SemaphoreType.DMA((184,)),
        pltpu.SemaphoreType.DMA((17,)),
    ]
    bo, ig, ga, gb = pl.pallas_call(
        kernel,
        out_shape=(
            jax.ShapeDtypeStruct((16, 16, DP), BF),
            jax.ShapeDtypeStruct((16, 16, DP), BF),
            jax.ShapeDtypeStruct((2, 4, 80, 128), BF),
            jax.ShapeDtypeStruct((2, 4, 2, 3, 80, 128), BF),
        ),
        in_specs=[pl.BlockSpec(memory_space=pltpu.SMEM)] + [vmem] * 2 + [any_space] * 12,
        out_specs=(vmem,) * 4,
        scratch_shapes=scratch,
        compiler_params=pltpu.CompilerParams(
            collective_id=0, has_side_effects=True, vmem_limit_bytes=62 * 1024 * 1024
        ),
        name="layer",
    )(
        positions, gain1.reshape(1, 72), gain2.reshape(1, 72), tokens[0].T, cotangent[0].T,
        wq, wkv, wo.T, wg, wu, wd.T, cols, rows, jnp.asarray(cos), jnp.asarray(sin),
    )

    def f32(*shape):
        return jax.ShapeDtypeStruct(shape, F32)

    outs = pl.pallas_call(
        finish,
        out_shape=(
            jax.ShapeDtypeStruct((D, ROWS), BF), f32(D, ROWS), f32(1, 72), f32(72, 576),
            f32(72, 384), f32(72, 576), f32(1, 72), f32(72, 1536), f32(72, 1536), f32(72, 1536),
        ),
        in_specs=[any_space] * 6,
        out_specs=(vmem,) * 10,
        scratch_shapes=[
            v((16, 16, DP)), v((16, 16, DP)), v((2, 4, 80, 128)), v((2, 4, 2, 3, 80, 128)),
            v((D, DP)), v((ROWS, ROWS)), pltpu.SemaphoreType.DMA((6,)),
        ],
        compiler_params=pltpu.CompilerParams(vmem_limit_bytes=60 * 1024 * 1024),
        name="finish",
    )(bo, ig, ga, gb, cols, rows)
    out, grad_in, n1, gq, gkv, go, n2, gg, gu, gd = outs
    return out.T[None], grad_in.T[None], n1.reshape(72), gq, gkv, go.T, n2.reshape(72), gg, gu, gd.T


def solution(mesh):
    rows, model, last = P("fsdp", "ctx", None), P("fsdp", None), P(None, "fsdp")
    gain = P("fsdp")
    return jax.shard_map(
        local,
        mesh=mesh,
        in_specs=(rows, P("fsdp", "ctx"), gain, model, model, last, gain, model, model, last, rows),
        out_specs=(rows, rows, gain, model, model, last, gain, model, model, last),
        check_vma=False,
    )
```

```python
import numpy as np

import jax
import jax.numpy as jnp
from jax import lax
from jax.experimental import pallas as pl
from jax.experimental.pallas import tpu as pltpu
from jax.sharding import PartitionSpec as P

MESH = pl.DeviceIdType.MESH
BF = jnp.bfloat16
F32 = jnp.float32
D = 576
DP = 640
ROWS = 256
WA = 512
TB = 24
FC = 256
NEG = -1e30
STEPS = (0, 1, 3, 2)
BACK = (2, 1, 3, 0)
LAST = (1, 2)
CHIPS = ((0, 1), (0, 3), (1, 0), (1, 1), (1, 3), (0, 2), (1, 2))


def mm(a, b):
    return jnp.dot(a, b, preferred_element_type=F32)


def mm_nt(a, b):
    return lax.dot_general(a, b, (((1,), (1,)), ((), ())), preferred_element_type=F32)


def mm_tn(a, b):
    return lax.dot_general(a, b, (((0,), (0,)), ((), ())), preferred_element_type=F32)


def up_tile(half, t):
    return t if t < 10 else t + (6 if half == 0 else 4)


def down_tile(t):
    return t // 6, 10 + t % 6 if t < 10 else 6 + t


def lane_iota(shape):
    return lax.broadcasted_iota(jnp.int32, shape, len(shape) - 1)


def partner_lanes(u):
    lane = lane_iota(u.shape)
    return jnp.where(lane % 64 < 32, pltpu.roll(u, 96, 1), pltpu.roll(u, 32, 1))


def kernel(
    pos, g1_in, g2_in, tok_h, cot_h, wq_h, wkv_h, wo_h, wg_h, wu_h, wd_h, cols_h, rows_h, cos_in, sin_in,
    bo_out, ig_out, ga_out, gb_out,
    tok, cot, wq_in, wkv_in, wo_in, wg_in, wu_in, wd_in, spread_cols, spread_rows,
    xc, wa_in, wb_in, xc_r, wa, wb, cos_s, sin_s, kv, bias, perm,
    qt, qx, dot_, dox, st_m, st_l, acc, ot, dqt,
    xs, dy, mid, act1, act1t, attb, dmid,
    dkv_p, d1_r, d2_s, d2_r, dz_s, dz_r,
    ga, gac, gax, gay_s, gay, gaf,
    gbc, q1, t1, q2, t2, q3, gbf,
    bo_s, bo_r, ig_s, ig_r,
    ss, rs, ls,
):
    f = lax.axis_index("fsdp")
    c = lax.axis_index("ctx")
    zh, xx = f // 4, f % 4
    zl, yy, k = c // 8, (c // 2) % 4, c % 2
    fz = (1 - zh) * 4 + xx

    def ctx_at(z, y, core):
        return z * 8 + y * 2 + core

    def slot_at(z, y, core):
        return y * 4 + z * 2 + core

    other = ctx_at(zl, yy, 1 - k)
    sends = []
    used = [0]

    def take(n):
        used[0] += n
        return used[0] - n

    def remote(src, dst, sem, fs, cs):
        return pltpu.make_async_remote_copy(
            src_ref=src, dst_ref=dst, send_sem=ss.at[sem], recv_sem=rs.at[sem],
            device_id={"fsdp": fs, "ctx": cs}, device_id_type=MESH,
        )

    def send(src, dst, sem, fs, cs):
        copy = remote(src, dst, sem, fs, cs)
        copy.start()
        sends.append(copy)
        return copy

    def arrived(dst, sem):
        remote(dst, dst, sem, f, other).wait_recv()

    loads = [
        pltpu.make_async_copy(src, dst, ls.at[7 + n])
        for n, (src, dst) in enumerate(
            (
                (wq_h, wq_in), (wkv_h, wkv_in), (tok_h, tok), (cols_h, spread_cols),
                (rows_h, spread_rows), (cot_h, cot), (wg_h, wg_in), (wu_h, wu_in), (wd_h, wd_in),
                (wo_h, wo_in),
            )
        )
    ]
    for copy in loads:
        copy.start()

    barrier = pltpu.get_barrier_semaphore()
    for step in range(1, 16):
        pl.semaphore_signal(
            barrier, inc=1, device_id={"fsdp": f, "ctx": (c + step) % 16}, device_id_type=MESH
        )
    for step in range(1, 8):
        pl.semaphore_signal(
            barrier, inc=1, device_id={"fsdp": (f + step) % 8, "ctx": c}, device_id_type=MESH
        )
    pl.semaphore_signal(
        barrier, inc=1, device_id={"fsdp": fz, "ctx": ctx_at(1 - zl, yy, k)}, device_id_type=MESH
    )

    rows_of = lax.broadcasted_iota(jnp.int32, (ROWS, 1), 0)
    run = jnp.where((rows_of // 8) % 2 == 0, pos[0, 0], pos[0, 128]).astype(F32)
    tag = run * (1.0 / 16.0) + (rows_of % 8).astype(F32)

    def pack_rows(ref):
        return mm(spread_rows[...], mm_tn(ref[...], spread_cols[...]).astype(BF))

    for copy in loads:
        copy.wait()
    xc[:, 0:16, :] = (
        jnp.where(lane_iota((ROWS, DP)) == 72, tag, pack_rows(tok)).astype(BF).reshape(16, 16, DP)
    )
    xc[:, 16:32, :] = pack_rows(cot).astype(BF).reshape(16, 16, DP)

    def pad_rows(value):
        return jnp.concatenate([value.astype(F32), jnp.zeros((8, value.shape[1]), F32)], axis=0)

    wq_all = pad_rows(wq_in[...])
    wkv_all = pad_rows(wkv_in[...])
    low80 = lane_iota((80, 128)) < 64
    wa_in[0] = wq_all[:, 0:512].astype(BF)
    row16 = lax.broadcasted_iota(jnp.int32, (16, 72), 0)
    gains_in = jnp.where(row16 == 0, g1_in[...].astype(F32), g2_in[...].astype(F32))
    gains_in = jnp.where(row16 < 2, gains_in, 0.0).astype(BF)
    row_hot = lax.broadcasted_iota(jnp.int32, (16, 128), 0)
    gain_hot = jnp.where((lane_iota((16, 128)) == 64 + row_hot) & (row_hot < 2), 1.0, 0.0).astype(BF)
    last_q = jnp.concatenate([wq_all[:, 512:576], jnp.zeros((80, 64), F32)], axis=1)
    wa_in[1, :, 0:128] = (last_q + pad_rows(mm_tn(gains_in, gain_hot))).astype(BF)

    def kv_head(n, want_low):
        block = wkv_all[:, 128 * (n // 2) : 128 * (n // 2) + 128]
        return block if (n % 2 == 0) == want_low else pltpu.roll(block, 64, 1)

    for g in range(3):
        both = jnp.where(low80, kv_head(g, True), kv_head(3 + g, False))
        wa_in[1, :, 128 + 128 * g : 256 + 128 * g] = both.astype(BF)

    for half, ref in ((0, wg_in), (1, wu_in)):
        whole = pad_rows(ref[...]).astype(BF)
        for t in range(12):
            wb_in[half, up_tile(half, t)] = whole[:, 128 * t : 128 * t + 128]
    whole = pad_rows(wd_in[...]).astype(BF)
    for t in range(12):
        half, at = down_tile(t)
        wb_in[half, at] = whole[:, 128 * t : 128 * t + 128]
    whole = jnp.concatenate([pad_rows(wo_in[...]), jnp.zeros((80, 64), F32)], axis=1).astype(BF)
    for t in range(5):
        wb_in[t // 4, 18 + t % 4] = whole[:, 128 * t : 128 * t + 128]
    wb_in[0, 22:24] = jnp.zeros((2, 80, 128), BF)
    wb_in[1, 19:24] = jnp.zeros((5, 80, 128), BF)
    pl.semaphore_wait(barrier, 23)

    zz = 2 * zh + zl
    order = ("ayb", "yba", "yab")

    def pick(n, u, w):
        return u if n < 2 else u * (1 - k) + w * k

    def coord(n, axis):
        if axis == "y":
            return yy
        return pick(n, zz, xx) if axis == "a" else pick(n, xx, zz)

    def along(n, axis, step):
        if axis == "y":
            return f, ctx_at(zl, (yy + step) % 4, k)
        z = (zz + step) % 4
        by_x = (zh * 4 + (xx + step) % 4, c)
        by_z = ((z // 2) * 4 + xx, ctx_at(z % 2, yy, k))
        first, second = (by_z, by_x) if axis == "a" else (by_x, by_z)
        return pick(n, first[0], second[0]), pick(n, first[1], second[1])

    def region(n, done, axis=None, step=0):
        at = []
        for name in "aby":
            if name in done:
                at.append(slice(None))
            else:
                at.append((coord(n, name) + 4 - step) % 4 if name == axis else coord(n, name))
        return wb.at[(k, n, *at)]

    sem_x = take(16)
    for step in range(1, 16):
        to = (c + step) % 16
        send(xc.at[to, 0:16], xc_r.at[c, 0:16], sem_x + step, f, to)
    local = [
        pltpu.make_async_copy(xc.at[c], xc_r.at[c], ls.at[0]),
        pltpu.make_async_copy(wa_in.at[k], wa.at[k, f], ls.at[1]),
        *(
            pltpu.make_async_copy(
                wb_in.at[k, 8 * n + 2 * yy + zl], region(n, ()), ls.at[4 + n]
            )
            for n in range(3)
        ),
        pltpu.make_async_copy(cos_in.at[:, c], cos_s, ls.at[2]),
        pltpu.make_async_copy(sin_in.at[:, c], sin_s, ls.at[3]),
    ]
    for copy in local:
        copy.start()

    def gather_first(w_in, w, sem):
        send(w_in.at[k], w.at[k, f], sem, fz, c)
        for step in range(1, 4):
            send(w_in.at[k], w.at[k, f], sem + step, zh * 4 + (xx + step) % 4, c)

    def gather_second(w, sem):
        arrived(w.at[k, fz], sem)
        return [
            send(w.at[k, fz], w.at[k, fz], sem + 3 + step, zh * 4 + (xx + step) % 4, c)
            for step in range(1, 4)
        ]

    def gather_third(w, sem):
        for step in range(1, 4):
            from_x = (xx + 4 - step) % 4
            arrived(w.at[k, zh * 4 + from_x], sem + step)
            arrived(w.at[k, (1 - zh) * 4 + from_x], sem + 3 + step)
        return [send(w.at[k], w.at[k], sem + 7, f, other)]

    def gather_last(w, sem):
        arrived(w.at[1 - k], sem + 7)

    sem_b = take(30)

    def spread(turn):
        if turn > 0:
            spread_wait(turn - 1)
        out = []
        for n in range(3):
            axis, done = order[n][turn], order[n][:turn]
            for step in range(1, 4):
                if turn == 0:
                    src = wb_in.at[k, 8 * n + 2 * yy + zl]
                else:
                    src = region(n, done)
                copy = send(
                    src, region(n, done), sem_b + 9 * turn + 3 * n + step - 1, *along(n, axis, step)
                )
                if turn > 0:
                    out.append(copy)
        return out

    def spread_wait(turn, groups=(0, 1, 2)):
        for n in groups:
            axis, done = order[n][turn], order[n][:turn]
            for step in range(1, 4):
                arrived(region(n, done, axis, step), sem_b + 9 * turn + 3 * n + step - 1)

    sem_a = take(8)
    gather_first(wa_in, wa, sem_a)
    spread(0)
    sem_c = take(16)
    for step in range(1, 16):
        to = (c + step) % 16
        send(xc.at[to, 16:32], xc_r.at[c, 16:32], sem_c + step, f, to)

    def make_bias(slot, carry):
        e = ctx_at((slot // 2) % 2, slot // 4, slot % 2)
        j = lax.broadcasted_iota(jnp.int32, (128, 128), 0)
        i = lax.broadcasted_iota(jnp.int32, (128, 128), 1)
        ok = (j // 8 < i // 8) | ((j // 8 == i // 8) & (8 * e + j % 8 <= 8 * c + i % 8))
        bias[pl.ds(pl.multiple_of(slot * 128, 128), 128), :] = jnp.where(ok, 0.0, NEG)
        return carry

    lax.fori_loop(0, 16, make_bias, 0)
    gather_second(wa, sem_a)
    for copy in local:
        copy.wait()
    from_wb = spread(1)
    for step in range(1, 16):
        arrived(xc_r.at[(c + 16 - step) % 16, 0:16], sem_x + step)

    x_raw = xc_r[:, 0:16, :].reshape(ROWS, DP)
    lane = lane_iota((ROWS, DP))
    tag = jnp.sum(jnp.where(lane == 72, x_raw.astype(F32), 0.0), axis=1, keepdims=True)
    place = lane_iota((ROWS, ROWS)).astype(F32)
    perm[...] = jnp.where(tag == place, 1.0, 0.0).astype(BF)
    perm_t = jnp.where(tag == place, 1.0, 0.0).T.astype(BF)
    x = mm(perm_t, x_raw)
    x = jnp.where(lane % 80 < 72, x, 0.0)
    xs[...] = x

    gather_third(wa, sem_a)
    r1 = lax.rsqrt(jnp.sum(x * x, axis=-1, keepdims=True) * (1.0 / D) + 1e-5)
    gather_last(wa, sem_a)

    def gain_row(which):
        hot = jnp.where(lane_iota((16, 128)) == 64 + which, 1.0, 0.0).astype(BF)
        block = wa[1, :, :, 0:128].reshape(DP, 128)
        return mm_nt(hot, block)[0:1, :]

    gain1, gain2 = gain_row(0), gain_row(1)
    a1 = x * r1 * gain1
    a1b = a1.astype(BF)
    act1[...] = a1b
    act1t[...] = a1.T.astype(BF)

    cos = cos_s[...].reshape(ROWS, 128)
    sin = sin_s[...].reshape(ROWS, 128)
    low = lane_iota((ROWS, 128)) < 64
    cos_kv = jnp.where(low, cos, 1.0)
    sin_kv = jnp.where(low, sin, 0.0)

    mine = slot_at(zl, yy, k)
    kv_pre = mm(a1b, wa[1, :, :, 128:512].reshape(DP, 384))
    for g in range(3):
        u = kv_pre[:, 128 * g : 128 * g + 128]
        kv[mine, g] = (u * cos_kv + partner_lanes(u) * sin_kv).astype(BF)
    sem_k = take(16)

    near = slot_at(1 - zl, yy, k)

    def kv_along_y(slot, a):
        for off in (1, 3):
            send(kv.at[slot], kv.at[slot], sem_k + a * 4 + off, f, ctx_at(zl, (yy + off) % 4, k))

    send(kv.at[mine], kv.at[mine], sem_k, f, other)
    send(kv.at[mine], kv.at[mine], sem_k + 4, f, ctx_at(1 - zl, yy, k))
    kv_along_y(mine, 0)

    def kv_direct(off):
        for a in (0, 1):
            if (a, off) != (0, 0):
                at = slot_at(zl if a == 0 else 1 - zl, (yy + 4 - off) % 4, k)
                arrived(kv.at[at], sem_k + a * 4 + off)
                send(kv.at[at], kv.at[at], sem_k + 8 + a * 4 + off, f, other)
                if (a, off) in ((0, 1), (1, 3)):
                    to = ctx_at(zl, (yy + off) % 4, k)
                    send(kv.at[at], kv.at[at], sem_k + a * 4 + 2, f, to)

    def kv_across(off):
        for a in (0, 1):
            at = slot_at(zl if a == 0 else 1 - zl, (yy + 4 - off) % 4, 1 - k)
            arrived(kv.at[at], sem_k if (a, off) == (0, 0) else sem_k + 8 + a * 4 + off)

    from_wb += spread(2)

    for t in range(5):
        w = wa[0, :, :, 128 * t : 128 * t + 128] if t < 4 else wa[1, :, :, 0:128]
        u = mm(a1b, w.reshape(DP, 128))
        u = (u * cos + partner_lanes(u) * sin).astype(BF).astype(F32) * 0.125
        for half in range(2):
            h = 2 * t + half
            if h < 9:
                g, r = h // 3, h % 3
                v = jnp.where(low, u if half == 0 else pltpu.roll(u, 64, 1), 0.0)
                vt = v.T
                for ih in range(2):
                    at = 384 * ih + 128 * r
                    qx[g, at : at + 128, :] = v[128 * ih : 128 * ih + 128].astype(BF)
                    qt[g, :, at : at + 128] = vt[:, 128 * ih : 128 * ih + 128].astype(BF)

    kv_direct(0)
    kv_along_y(near, 1)

    for step in range(1, 16):
        arrived(xc_r.at[(c + 16 - step) % 16, 16:32], sem_c + step)
    dy[...] = mm_tn(perm[...], xc_r[:, 16:32, :].reshape(ROWS, DP)).astype(BF)

    st_m[...] = jnp.full(st_m.shape, NEG, F32)
    st_l[...] = jnp.zeros(st_l.shape, F32)
    acc[...] = jnp.zeros(acc.shape, F32)

    def three(b):
        return jnp.concatenate([b, b, b], axis=1)

    def fold_forward(off):
        group = (yy + 4 - off) % 4

        def per_head(g, carry):
            b3 = three(bias[pl.ds(pl.multiple_of(group * 512, 512), 512), :])
            for key_half, lane_half in ((0, 0), (0, 1), (1, 1)):
                at = 384 * lane_half
                rows = kv[pl.ds(group * 4, 4), g, 128 * key_half : 128 * key_half + 128, :]
                rows = rows.reshape(512, 128)
                s = mm(rows, qt[g, :, at : at + 384])
                if key_half == lane_half:
                    s = s + b3
                old = st_m[g, :, at : at + 384]
                new = jnp.maximum(old, jnp.max(s, axis=0, keepdims=True))
                p = jnp.exp(s - new)
                scale = jnp.exp(old - new)
                st_m[g, :, at : at + 384] = new
                st_l[g, :, at : at + 384] = (
                    st_l[g, :, at : at + 384] * scale + jnp.sum(p, axis=0, keepdims=True)
                )
                acc[g, :, at : at + 384] = acc[g, :, at : at + 384] * scale + mm_tn(
                    rows, p.astype(BF)
                )
            return carry

        lax.fori_loop(0, 3, per_head, 0)

    kv_direct(STEPS[1])
    kv_across(0)
    fold_forward(0)
    kv_direct(STEPS[2])
    kv_across(STEPS[1])
    fold_forward(STEPS[1])
    kv_direct(STEPS[3])
    kv_across(STEPS[2])
    fold_forward(STEPS[2])
    kv_across(STEPS[3])
    for n in (1, 0, 2):
        spread_wait(2, (n,))
        from_wb.append(send(wb.at[k, n], wb.at[k, n], sem_b + 27 + n, f, other))
    fold_forward(STEPS[3])

    def head_rows(ref, g, r):
        return jnp.concatenate(
            [ref[g, :, 384 * ih + 128 * r : 384 * ih + 128 * r + 128].T for ih in range(2)], axis=0
        )

    for g in range(3):
        ot[g] = acc[g] / st_l[g]
        st_l[g] = st_m[g] + jnp.log(st_l[g])
    for t in range(5):
        a = pltpu.roll(head_rows(ot, 2 * t // 3, 2 * t % 3), 64, 1)
        b = head_rows(ot, (2 * t + 1) // 3, (2 * t + 1) % 3) if t < 4 else jnp.zeros((ROWS, 128), F32)
        attb[:, 128 * t : 128 * t + 128] = jnp.where(low, a, b).astype(BF)

    for n in range(3):
        arrived(wb.at[1 - k, n], sem_b + 27 + n)

    def fixed(half, n):
        return isinstance(half, int) and isinstance(n, int) and (half, n) == LAST

    def tile_at(half, n, y, z):
        if fixed(half, n):
            blocks = [wb[1, 2, :, 2 * q + z, y] for q in range(2)]
        else:
            blocks = [wb[half, n, 2 * q + z, :, y] for q in range(2)]
        return jnp.concatenate(blocks, axis=0).reshape(DP, 128)

    def put_tile(half, n, y, z, value):
        value = value.astype(BF).reshape(2, 4, 80, 128)
        for q in range(2):
            if fixed(half, n):
                wb[1, 2, :, 2 * q + z, y] = value[q]
            else:
                wb[half, n, 2 * q + z, :, y] = value[q]

    def pair(half, p):
        return jnp.concatenate([tile_at(half, p // 4, p % 4, z) for z in range(2)], axis=1)

    def put_pair(half, p, value):
        for z in range(2):
            put_tile(half, p // 4, p % 4, z, value[:, 128 * z : 128 * z + 128])

    def out_tile(t):
        return tile_at(0, 2, 1 + t // 2, t % 2) if t < 4 else tile_at(1, 2, 1, 0)

    out_w = jnp.concatenate([out_tile(t) for t in range(5)], axis=1)
    m0 = xs[...] + mm_nt(attb[...], out_w)
    r2 = lax.rsqrt(jnp.sum(m0 * m0, axis=-1, keepdims=True) * (1.0 / D) + 1e-5)
    mid[...] = m0
    a2 = m0 * r2 * gain2
    a2b = a2.astype(BF)
    a2t = a2.T.astype(BF)
    dyb = dy[...]
    dyt = dyb.astype(F32).T.astype(BF)

    for copy in from_wb:
        copy.wait_send()
    sends[:] = [copy for copy in sends if all(copy is not done for done in from_wb)]

    def ff(j, carry):
        total, dact = carry
        last = isinstance(j, int)
        at_g, at_u, at_d = ((0, 8), (1, 7), (1, 8)) if last else ((0, j), (1, j), (j // 3, 5 + j % 3))
        wg, wu, wd = pair(*at_g), pair(*at_u), pair(*at_d)
        gate, up = mm(a2b, wg), mm(a2b, wu)
        sig = jax.nn.sigmoid(gate)
        swish = gate * sig
        hid = (swish * up).astype(BF)
        total = total + mm_nt(hid, wd)
        dh = mm(dyb, wd)
        dg = (dh * up * sig * (1.0 + gate * (1.0 - sig))).astype(BF)
        du = (dh * swish).astype(BF)
        put_pair(*at_d, mm(dyt, hid))
        put_pair(*at_g, mm(a2t, dg))
        put_pair(*at_u, mm(a2t, du))
        dact = dact + mm_nt(dg, wg) + mm_nt(du, wu)
        return total, dact

    zero = jnp.zeros((ROWS, DP), F32)
    total, dact = ff(5, lax.fori_loop(0, 5, ff, (zero, zero)))

    sem_r = take(42)

    def add(ref, at, got_at):
        v = ref[at].astype(F32)
        for r in got_at:
            v = v + r.astype(F32)
        return v

    def red_core(n):
        send(wb.at[1 - k, n], gbc.at[n], sem_r + n, f, other)

    def red_one(n):
        arrived(gbc.at[n], sem_r + n)

        def body(i, carry):
            wb[k, n, i // 4, i % 4] = (
                wb[k, n, i // 4, i % 4].astype(F32) + gbc[n, i // 4, i % 4].astype(F32)
            ).astype(BF)
            return carry

        lax.fori_loop(0, 16, body, 0)
        axis = order[n][2]
        for step in range(1, 4):
            to = (coord(n, axis) + step) % 4
            src = wb.at[k, n, to] if axis == "a" else wb.at[k, n, :, to]
            send(src, q1.at[n, step - 1], sem_r + 3 + 3 * n + step - 1, *along(n, axis, step))

    def red_two(n):
        for step in range(3):
            arrived(q1.at[n, step], sem_r + 3 + 3 * n + step)
        axis, at = order[n][2], coord(n, order[n][2])

        def body(i, carry):
            v = (wb[k, n, at, i] if axis == "a" else wb[k, n, i, at]).astype(F32)
            for step in range(3):
                v = v + q1[n, step, i].astype(F32)
            t1[n, i] = v.astype(BF)
            return carry

        lax.fori_loop(0, 4, body, 0)
        axis = order[n][1]
        for step in range(1, 4):
            to = (coord(n, axis) + step) % 4
            src = t1.at[n, :, to] if axis == "y" else t1.at[n, to]
            send(src, q2.at[n, step - 1], sem_r + 12 + 3 * n + step - 1, *along(n, axis, step))

    def red_three(n):
        for step in range(3):
            arrived(q2.at[n, step], sem_r + 12 + 3 * n + step)
        axis, at = order[n][1], coord(n, order[n][1])
        own = (n, slice(None), at) if axis == "y" else (n, at)
        t2[n] = add(t1, own, [q2[n, i] for i in range(3)]).astype(BF)
        axis = order[n][0]
        for step in range(1, 4):
            to = (coord(n, axis) + step) % 4
            send(t2.at[n, to], q3.at[n, step - 1], sem_r + 21 + 3 * n + step - 1, *along(n, axis, step))

    def red_four():
        for n in range(3):
            for step in range(3):
                arrived(q3.at[n, step], sem_r + 21 + 3 * n + step)
            own = add(t2, (n, coord(n, order[n][0])), [q3[n, i] for i in range(3)])
            gbf[k, yy, zl, n] = own.astype(BF)
        piece = gbf.at[k, yy, zl]
        for a, off in CHIPS:
            to = ctx_at(zl if a == 0 else 1 - zl, (yy + off) % 4, k)
            send(piece, piece, sem_r + 30 + 4 * a + off, f, to)

    def red_five():
        for a, off in CHIPS:
            z = zl if a == 0 else 1 - zl
            arrived(gbf.at[k, (yy + 4 - off) % 4, z], sem_r + 30 + 4 * a + off)
        send(gbf.at[k], gbf.at[k], sem_r + 38, f, other)

    def red_six():
        arrived(gbf.at[1 - k], sem_r + 38)

    sem_g = take(36)

    def in_core(p):
        send(ga.at[p, 1 - k], gac.at[p], sem_g + 18 * p, f, other)

    def in_one(p):
        arrived(gac.at[p], sem_g + 18 * p)
        ga[p, k] = (ga[p, k].astype(F32) + gac[p].astype(F32)).astype(BF)
        for step in range(1, 8):
            to = (f + step) % 8
            send(ga.at[p, k, to], gax.at[p, step - 1], sem_g + 18 * p + step, to, c)

    def in_two(p):
        for step in range(1, 8):
            arrived(gax.at[p, step - 1], sem_g + 18 * p + step)
        gay_s[p] = add(ga, (p, k, f), [gax[p, i] for i in range(7)]).astype(BF)
        for a, off in CHIPS:
            to = ctx_at(zl if a == 0 else 1 - zl, (yy + off) % 4, k)
            send(gay_s.at[p], gay.at[p, 4 * a + off], sem_g + 18 * p + 8 + 4 * a + off, f, to)

    def in_three(p):
        for a, off in CHIPS:
            arrived(gay.at[p, 4 * a + off], sem_g + 18 * p + 8 + 4 * a + off)
        gaf[p, k] = add(gay_s, p, [gay[p, 4 * a + off] for a, off in CHIPS]).astype(BF)
        send(gaf.at[p, k], gaf.at[p, k], sem_g + 18 * p + 16, f, other)

    def in_four(p):
        arrived(gaf.at[p, 1 - k], sem_g + 18 * p + 16)

    red_core(0)
    red_core(1)

    def give_back(value, src, dst, sem):
        src[...] = mm(perm[...], value.astype(BF)).astype(BF).reshape(16, 16, DP)
        for step in range(1, 16):
            send(src.at[(c + step) % 16], dst.at[c], sem + step, f, (c + step) % 16)
        dst[c] = src[c]

    sem_o = take(16)
    sem_i = take(16)
    m0 = mid[...]
    give_back(m0 + total, bo_s, bo_r, sem_o)

    dyf = dyb.astype(F32)
    gain_grad2 = jnp.sum(dact * m0 * r2, axis=0, keepdims=True)
    wgt = dact * gain2
    inner = jnp.sum(wgt * m0, axis=-1, keepdims=True) * (1.0 / D)
    dm = dyf + r2 * wgt - m0 * (r2 * r2 * r2) * inner
    dmid[...] = dm
    dmb = dm.astype(BF)
    dmt = dm.T.astype(BF)

    for t in range(5):
        u = mm(dmb, out_tile(t)).astype(BF).astype(F32)
        for half in range(2):
            h = 2 * t + half
            if h < 9:
                g, r = h // 3, h % 3
                v = jnp.where(low, 0.0, u if half == 1 else pltpu.roll(u, 64, 1))
                vt = v.T
                for ih in range(2):
                    at = 384 * ih + 128 * r
                    dox[g, at : at + 128, :] = v[128 * ih : 128 * ih + 128].astype(BF)
                    dot_[g, :, at : at + 128] = vt[:, 128 * ih : 128 * ih + 128].astype(BF)
    grad_out = mm(dmt, attb[...]).astype(BF)
    for t in range(5):
        at = (0, 2, 1 + t // 2, t % 2) if t < 4 else (1, 2, 1, 0)
        put_tile(*at, grad_out[:, 128 * t : 128 * t + 128])
    red_core(2)

    for g in range(3):
        st_m[g] = jnp.sum(dot_[g].astype(F32) * ot[g], axis=0, keepdims=True)
    dqt[...] = jnp.zeros(dqt.shape, F32)

    def fold_backward(at_step, off):
        group = (yy + 4 - off) % 4

        def per_head(g, carry):
            b3 = three(bias[pl.ds(pl.multiple_of(group * 512, 512), 512), :])
            for key_half in range(2):
                rows = kv[pl.ds(group * 4, 4), g, 128 * key_half : 128 * key_half + 128, :]
                rows = rows.reshape(512, 128)
                grad = None
                for lane_half in range(key_half, 2):
                    at = 384 * lane_half
                    s = mm(rows, qt[g, :, at : at + 384])
                    if key_half == lane_half:
                        s = s + b3
                    p = jnp.exp(s - st_l[g, :, at : at + 384])
                    dp = mm(rows, dot_[g, :, at : at + 384])
                    ds = (p * (dp - st_m[g, :, at : at + 384])).astype(BF)
                    part = mm(ds, qx[g, at : at + 384, :]) + mm(
                        p.astype(BF), dox[g, at : at + 384, :]
                    )
                    grad = part if grad is None else grad + part
                    dqt[g, :, at : at + 384] += mm_tn(rows, ds)
                dkv_p[at_step, :, g, 128 * key_half : 128 * key_half + 128, :] = grad.astype(
                    BF
                ).reshape(4, 128, 128)
            return carry

        lax.fori_loop(0, 3, per_head, 0)

    sem_d1 = take(8)
    sem_d = take(4)

    def dkv_first(at_step):
        for z in range(2):
            send(
                dkv_p.at[at_step, 2 * z + 1 - k], d1_r.at[at_step, z], sem_d1 + 2 * at_step + z,
                f, other,
            )

    def dkv_second(at_step, off):
        for z in range(2):
            arrived(d1_r.at[at_step, z], sem_d1 + 2 * at_step + z)
        for z in range(2):
            d2_s[at_step, z] = (
                dkv_p[at_step, 2 * z + k].astype(F32) + d1_r[at_step, z].astype(F32)
            ).astype(BF)
        if off != 0:
            send(
                d2_s.at[at_step], d2_r.at[off - 1], sem_d + off,
                f, ctx_at(zl, (yy + 4 - off) % 4, k),
            )

    red_one(0)
    red_one(1)
    red_one(2)
    fold_backward(0, BACK[0])
    dkv_first(0)
    dkv_second(0, BACK[0])
    fold_backward(1, BACK[1])
    dkv_first(1)
    dkv_second(1, BACK[1])
    fold_backward(2, BACK[2])
    dkv_first(2)
    dkv_second(2, BACK[2])
    fold_backward(3, BACK[3])
    dkv_first(3)
    for n in (1, 0, 2):
        red_two(n)
    dkv_second(3, BACK[3])
    for off in range(1, 4):
        arrived(d2_r.at[off - 1], sem_d + off)
    dz_s[...] = add(d2_s, (3, 1 - zl), [d2_r[i, 1 - zl] for i in range(3)]).astype(BF)
    send(dz_s, dz_r, sem_d, f, ctx_at(1 - zl, yy, k))

    dq_tiles = []
    for t in range(5):
        a = head_rows(dqt, 2 * t // 3, 2 * t % 3)
        if t < 4:
            b = pltpu.roll(head_rows(dqt, (2 * t + 1) // 3, (2 * t + 1) % 3), 64, 1)
        else:
            b = jnp.zeros((ROWS, 128), F32)
        u = jnp.where(low, a, b) * 0.125
        dq_tiles.append((u * cos - partner_lanes(u) * sin).astype(BF))
    dq = jnp.concatenate(dq_tiles, axis=1)
    a1t = act1t[...]
    grad_q = mm(a1t, dq)
    for half in range(2):
        ga[0, half] = grad_q[:, 256 * half : 256 * half + 256].astype(BF).reshape(8, 80, 256)
    in_core(0)
    dact1 = mm_nt(dq[:, 0:512], wa[0].reshape(DP, 512)) + mm_nt(
        dq[:, 512:640], wa[1, :, :, 0:128].reshape(DP, 128)
    )
    in_one(0)
    for n in (1, 0, 2):
        red_three(n)
    dkv = add(d2_s, (3, zl), [d2_r[i, zl] for i in range(3)])
    arrived(dz_r, sem_d)
    dkv = dkv + dz_r[...].astype(F32)
    for g in range(3):
        u = dkv[g]
        u = (u * cos_kv - partner_lanes(u) * sin_kv).astype(BF)
        at = 128 + 128 * g
        part = mm(a1t, u).astype(BF).reshape(8, 80, 128)
        lanes = slice(128, 256) if g != 1 else slice(0, 128)
        ga[1, 0 if g == 0 else 1, :, :, lanes] = part
        dact1 = dact1 + mm_nt(u, wa[1, :, :, at : at + 128].reshape(DP, 128))

    x = xs[...]
    gain_grad1 = jnp.sum(dact1 * x * r1, axis=0, keepdims=True)
    gains = jnp.concatenate([gain_grad1, gain_grad2, jnp.zeros((6, DP), F32)], axis=0)
    hot = jnp.where(
        lane_iota((8, 128)) == 64 + lax.broadcasted_iota(jnp.int32, (8, 128), 0), 1.0, 0.0
    )
    hot = jnp.where(lax.broadcasted_iota(jnp.int32, (8, 128), 0) < 2, hot, 0.0)
    gain_cols = mm(gains.T.astype(BF), hot.astype(BF))
    ga[1, 0, :, :, 0:128] = (grad_q[:, 512:640] + gain_cols).astype(BF).reshape(8, 80, 128)
    in_core(1)
    red_four()

    wgt = dact1 * gain1
    inner = jnp.sum(wgt * x, axis=-1, keepdims=True) * (1.0 / D)
    give_back(
        dmid[...] + r1 * wgt - x * (r1 * r1 * r1) * inner, ig_s, ig_r, sem_i
    )
    in_one(1)
    in_two(0)
    in_two(1)
    red_five()
    in_three(0)
    for step in range(1, 16):
        arrived(bo_r.at[(c + 16 - step) % 16], sem_o + step)
    bo_out[...] = bo_r[...]
    in_three(1)
    for step in range(1, 16):
        arrived(ig_r.at[(c + 16 - step) % 16], sem_i + step)
    ig_out[...] = ig_r[...]
    red_six()
    gb_out[...] = gbf[...]
    in_four(0)
    in_four(1)
    ga_out[...] = gaf[...]
    for copy in sends:
        copy.wait_send()


def tables():
    freq = np.power(np.float32(100000.0), -(np.arange(32, dtype=np.float32) * np.float32(2.0 / 64)))
    angle = np.arange(4096, dtype=np.float32)[:, None] * freq[None, :].astype(np.float32)
    cos, sin = np.cos(angle), np.sin(angle)
    cos = np.concatenate([cos, cos, cos, cos], axis=1)
    sin = np.concatenate([-sin, sin, -sin, sin], axis=1)
    shape = (32, 16, 8, 128)
    return cos.reshape(shape).astype(np.float32), sin.reshape(shape).astype(np.float32)


def placements():
    cols = np.zeros((D, DP), np.float32)
    at = np.arange(D)
    cols[at, at // 72 * 80 + at % 72] = 1.0
    rows = np.zeros((ROWS, ROWS), np.float32)
    at = np.arange(ROWS)
    rows[at, at // 8 % 2 * 128 + at // 16 * 8 + at % 8] = 1.0
    return jnp.asarray(cols, BF), jnp.asarray(rows, BF)


def finish(
    bo_h, ig_h, ga_h, gb_h, cols_h, rows_h,
    out, grad_in, n1, gq, gkv, go, n2, gg, gu, gd,
    bo, ig, ga, gb, cols, rows, sems,
):
    copies = [
        pltpu.make_async_copy(src, dst, sems.at[n])
        for n, (src, dst) in enumerate(
            ((gb_h, gb), (cols_h, cols), (rows_h, rows), (bo_h, bo), (ig_h, ig), (ga_h, ga))
        )
    ]
    for copy in copies:
        copy.start()
    for copy in copies:
        copy.wait()
    for src, dst in ((bo, out), (ig, grad_in)):
        narrow = mm_nt(cols[...], src[...].reshape(ROWS, DP)).astype(BF)
        dst[...] = mm(narrow, rows[...]).astype(dst.dtype)

    def part(ref, *at):
        return ref[at].astype(F32)

    for t in range(4):
        gq[:, 128 * t : 128 * t + 128] = part(ga, 0, t // 2)[0:72, 128 * (t % 2) : 128 * (t % 2) + 128]
    last = part(ga, 1, 0)[:, 0:128]
    gq[:, 512:576] = last[0:72, 0:64]
    row = lax.broadcasted_iota(jnp.int32, (16, 128), 0)
    hot = jnp.where((lane_iota((16, 128)) == 64 + row) & (row < 2), 1.0, 0.0).astype(BF)
    gains = mm_nt(hot, last.astype(BF))
    n1[...] = gains[0:1, 0:72]
    n2[...] = gains[1:2, 0:72]
    low = lane_iota((80, 128)) < 64
    tiles = [part(ga, 1, 0)[:, 128:256], part(ga, 1, 1)[:, 0:128], part(ga, 1, 1)[:, 128:256]]
    turn = [pltpu.roll(t, 64, 1) for t in tiles]
    heads = [
        jnp.where(low, tiles[0], turn[1]),
        jnp.where(low, tiles[2], tiles[0]),
        jnp.where(low, turn[1], tiles[2]),
    ]
    for g in range(3):
        gkv[:, 128 * g : 128 * g + 128] = heads[g][0:72]

    def tile(half, t):
        return part(gb, half, (t % 8) // 2, t % 2, t // 8)

    for half, ref in ((0, gg), (1, gu)):
        for t in range(12):
            ref[:, 128 * t : 128 * t + 128] = tile(half, up_tile(half, t))[0:72]
    for t in range(12):
        gd[:, 128 * t : 128 * t + 128] = tile(*down_tile(t))[0:72]
    for t in range(4):
        go[:, 128 * t : 128 * t + 128] = tile(0, 18 + t)[0:72]
    go[:, 512:576] = tile(1, 18)[0:72, 0:64]


def local(tokens, positions, gain1, wq, wkv, wo, gain2, wg, wu, wd, cotangent):
    cos, sin = tables()
    cols, rows = placements()

    def v(shape, dtype=BF):
        return pltpu.VMEM(shape, dtype)

    any_space = pl.BlockSpec(memory_space=pl.ANY)
    vmem = pl.BlockSpec(memory_space=pltpu.VMEM)
    scratch = [
        v((D, ROWS)), v((D, ROWS)), v((72, 576)), v((72, 384)), v((72, 576)), v((72, 1536)),
        v((72, 1536)), v((72, 1536)), v((D, DP)), v((ROWS, ROWS)),
        v((16, 32, DP)), v((2, 80, WA)), v((2, TB, 80, 128)),
        v((16, 32, DP)), v((2, 8, 80, WA)), v((2, 3, 4, 4, 4, 80, 128)),
        v((32, 8, 128), F32), v((32, 8, 128), F32),
        v((16, 3, 256, 128)), v((2048, 128), F32), v((ROWS, ROWS)),
        v((3, 128, 768)), v((3, 768, 128)), v((3, 128, 768)), v((3, 768, 128)),
        v((3, 1, 768), F32), v((3, 1, 768), F32), v((3, 128, 768), F32), v((3, 128, 768), F32),
        v((3, 128, 768), F32),
        v((ROWS, DP), F32), v((ROWS, DP)), v((ROWS, DP), F32), v((ROWS, DP)), v((DP, ROWS)),
        v((ROWS, DP)), v((ROWS, DP), F32),
        v((4, 4, 3, 256, 128)), v((4, 2, 3, 256, 128)), v((4, 2, 3, 256, 128)),
        v((3, 2, 3, 256, 128)), v((3, 256, 128)), v((3, 256, 128)),
        v((2, 2, 8, 80, 256)), v((2, 8, 80, 256)), v((2, 7, 80, 256)),
        v((2, 80, 256)), v((2, 8, 80, 256)), v((2, 2, 80, 256)),
        v((3, 4, 4, 4, 80, 128)), v((3, 3, 4, 4, 80, 128)), v((3, 4, 4, 80, 128)),
        v((3, 3, 4, 80, 128)), v((3, 4, 80, 128)),
        v((3, 3, 80, 128)), v((2, 4, 2, 3, 80, 128)),
        v((16, 16, DP)), v((16, 16, DP)), v((16, 16, DP)), v((16, 16, DP)),
        pltpu.SemaphoreType.DMA((216,)), pltpu.SemaphoreType.DMA((216,)),
        pltpu.SemaphoreType.DMA((17,)),
    ]
    bo, ig, ga, gb = pl.pallas_call(
        kernel,
        out_shape=(
            jax.ShapeDtypeStruct((16, 16, DP), BF),
            jax.ShapeDtypeStruct((16, 16, DP), BF),
            jax.ShapeDtypeStruct((2, 2, 80, 256), BF),
            jax.ShapeDtypeStruct((2, 4, 2, 3, 80, 128), BF),
        ),
        in_specs=[pl.BlockSpec(memory_space=pltpu.SMEM)] + [vmem] * 2 + [any_space] * 12,
        out_specs=(vmem,) * 4,
        scratch_shapes=scratch,
        compiler_params=pltpu.CompilerParams(
            collective_id=0, has_side_effects=True, vmem_limit_bytes=62 * 1024 * 1024
        ),
        name="layer",
    )(
        positions, gain1.reshape(1, 72), gain2.reshape(1, 72), tokens[0].T, cotangent[0].T,
        wq, wkv, wo.T, wg, wu, wd.T, cols, rows, jnp.asarray(cos), jnp.asarray(sin),
    )

    def f32(*shape):
        return jax.ShapeDtypeStruct(shape, F32)

    outs = pl.pallas_call(
        finish,
        out_shape=(
            jax.ShapeDtypeStruct((D, ROWS), BF), f32(D, ROWS), f32(1, 72), f32(72, 576),
            f32(72, 384), f32(72, 576), f32(1, 72), f32(72, 1536), f32(72, 1536), f32(72, 1536),
        ),
        in_specs=[any_space] * 6,
        out_specs=(vmem,) * 10,
        scratch_shapes=[
            v((16, 16, DP)), v((16, 16, DP)), v((2, 2, 80, 256)), v((2, 4, 2, 3, 80, 128)),
            v((D, DP)), v((ROWS, ROWS)), pltpu.SemaphoreType.DMA((6,)),
        ],
        compiler_params=pltpu.CompilerParams(vmem_limit_bytes=60 * 1024 * 1024),
        name="finish",
    )(bo, ig, ga, gb, cols, rows)
    out, grad_in, n1, gq, gkv, go, n2, gg, gu, gd = outs
    return out.T[None], grad_in.T[None], n1.reshape(72), gq, gkv, go.T, n2.reshape(72), gg, gu, gd.T


def solution(mesh):
    rows, model, last = P("fsdp", "ctx", None), P("fsdp", None), P(None, "fsdp")
    gain = P("fsdp")
    return jax.shard_map(
        local,
        mesh=mesh,
        in_specs=(rows, P("fsdp", "ctx"), gain, model, model, last, gain, model, model, last, rows),
        out_specs=(rows, rows, gain, model, model, last, gain, model, model, last),
        check_vma=False,
    )
```

```python
import numpy as np

import jax
import jax.numpy as jnp
from jax import lax
from jax.experimental import pallas as pl
from jax.experimental.pallas import tpu as pltpu
from jax.sharding import PartitionSpec as P

MESH = pl.DeviceIdType.MESH
BF = jnp.bfloat16
F32 = jnp.float32
D = 576
DP = 640
ROWS = 256
WA = 512
TB = 24
FC = 256
NEG = -1e30
STEPS = (0, 1, 3, 2)
BACK = (2, 1, 3, 0)
LAST = (1, 2)
CHIPS = ((0, 1), (0, 3), (1, 0), (1, 1), (1, 3), (0, 2), (1, 2))


def mm(a, b):
    return jnp.dot(a, b, preferred_element_type=F32)


def mm_nt(a, b):
    return lax.dot_general(a, b, (((1,), (1,)), ((), ())), preferred_element_type=F32)


def mm_tn(a, b):
    return lax.dot_general(a, b, (((0,), (0,)), ((), ())), preferred_element_type=F32)


def up_tile(half, t):
    return t if t < 10 else t + (6 if half == 0 else 4)


def down_tile(t):
    return t // 6, 10 + t % 6 if t < 10 else 6 + t


def lane_iota(shape):
    return lax.broadcasted_iota(jnp.int32, shape, len(shape) - 1)


def partner_lanes(u):
    lane = lane_iota(u.shape)
    return jnp.where(lane % 64 < 32, pltpu.roll(u, 96, 1), pltpu.roll(u, 32, 1))


def kernel(
    pos, g1_in, g2_in, tok_h, cot_h, wq_h, wkv_h, wo_h, wg_h, wu_h, wd_h, cols_h, rows_h, cos_in, sin_in,
    bo_out, ig_out, ga_out, gb_out,
    tok, cot, wq_in, wkv_in, wo_in, wg_in, wu_in, wd_in, spread_cols, spread_rows,
    xc, wa_in, wb_in, xc_r, wa, wb, cos_s, sin_s, kv, bias, perm,
    qt, qx, dot_, dox, st_m, st_l, acc, ot, dqt,
    xs, dy, mid, act1, act1t, attb, dmid,
    dkv_p, d1_r, d2_s, d2_r, dz_s, dz_r,
    ga, gac, gax, gay_s, gay, gaf,
    gbc, q1, t1, q2, t2, q3, gbf,
    bo_s, bo_r, ig_s, ig_r,
    ss, rs, ls,
):
    f = lax.axis_index("fsdp")
    c = lax.axis_index("ctx")
    zh, xx = f // 4, f % 4
    zl, yy, k = c // 8, (c // 2) % 4, c % 2
    fz = (1 - zh) * 4 + xx

    def ctx_at(z, y, core):
        return z * 8 + y * 2 + core

    def slot_at(z, y, core):
        return y * 4 + z * 2 + core

    other = ctx_at(zl, yy, 1 - k)
    sends = []
    used = [0]

    def take(n):
        used[0] += n
        return used[0] - n

    def remote(src, dst, sem, fs, cs):
        return pltpu.make_async_remote_copy(
            src_ref=src, dst_ref=dst, send_sem=ss.at[sem], recv_sem=rs.at[sem],
            device_id={"fsdp": fs, "ctx": cs}, device_id_type=MESH,
        )

    def send(src, dst, sem, fs, cs):
        copy = remote(src, dst, sem, fs, cs)
        copy.start()
        sends.append(copy)
        return copy

    def arrived(dst, sem):
        remote(dst, dst, sem, f, other).wait_recv()

    loads = [
        pltpu.make_async_copy(src, dst, ls.at[7 + n])
        for n, (src, dst) in enumerate(
            (
                (wq_h, wq_in), (wkv_h, wkv_in), (tok_h, tok), (cols_h, spread_cols),
                (rows_h, spread_rows), (cot_h, cot), (wg_h, wg_in), (wu_h, wu_in), (wd_h, wd_in),
                (wo_h, wo_in),
            )
        )
    ]
    for copy in loads:
        copy.start()

    barrier = pltpu.get_barrier_semaphore()
    for step in range(1, 16):
        pl.semaphore_signal(
            barrier, inc=1, device_id={"fsdp": f, "ctx": (c + step) % 16}, device_id_type=MESH
        )
    for step in range(1, 8):
        pl.semaphore_signal(
            barrier, inc=1, device_id={"fsdp": (f + step) % 8, "ctx": c}, device_id_type=MESH
        )
    pl.semaphore_signal(
        barrier, inc=1, device_id={"fsdp": fz, "ctx": ctx_at(1 - zl, yy, k)}, device_id_type=MESH
    )

    rows_of = lax.broadcasted_iota(jnp.int32, (ROWS, 1), 0)
    run = jnp.where((rows_of // 8) % 2 == 0, pos[0, 0], pos[0, 128]).astype(F32)
    tag = run * (1.0 / 16.0) + (rows_of % 8).astype(F32)

    def pack_rows(ref):
        return mm(spread_rows[...], mm_tn(ref[...], spread_cols[...]).astype(BF))

    for copy in loads:
        copy.wait()
    xc[:, 0:16, :] = (
        jnp.where(lane_iota((ROWS, DP)) == 72, tag, pack_rows(tok)).astype(BF).reshape(16, 16, DP)
    )
    xc[:, 16:32, :] = pack_rows(cot).astype(BF).reshape(16, 16, DP)

    def pad_rows(value):
        return jnp.concatenate([value.astype(F32), jnp.zeros((8, value.shape[1]), F32)], axis=0)

    wq_all = pad_rows(wq_in[...])
    wkv_all = pad_rows(wkv_in[...])
    low80 = lane_iota((80, 128)) < 64
    wa_in[0] = wq_all[:, 0:512].astype(BF)
    row16 = lax.broadcasted_iota(jnp.int32, (16, 72), 0)
    gains_in = jnp.where(row16 == 0, g1_in[...].astype(F32), g2_in[...].astype(F32))
    gains_in = jnp.where(row16 < 2, gains_in, 0.0).astype(BF)
    row_hot = lax.broadcasted_iota(jnp.int32, (16, 128), 0)
    gain_hot = jnp.where((lane_iota((16, 128)) == 64 + row_hot) & (row_hot < 2), 1.0, 0.0).astype(BF)
    last_q = jnp.concatenate([wq_all[:, 512:576], jnp.zeros((80, 64), F32)], axis=1)
    wa_in[1, :, 0:128] = (last_q + pad_rows(mm_tn(gains_in, gain_hot))).astype(BF)

    def kv_head(n, want_low):
        block = wkv_all[:, 128 * (n // 2) : 128 * (n // 2) + 128]
        return block if (n % 2 == 0) == want_low else pltpu.roll(block, 64, 1)

    for g in range(3):
        both = jnp.where(low80, kv_head(g, True), kv_head(3 + g, False))
        wa_in[1, :, 128 + 128 * g : 256 + 128 * g] = both.astype(BF)

    for half, ref in ((0, wg_in), (1, wu_in)):
        whole = pad_rows(ref[...]).astype(BF)
        for t in range(12):
            wb_in[half, up_tile(half, t)] = whole[:, 128 * t : 128 * t + 128]
    whole = pad_rows(wd_in[...]).astype(BF)
    for t in range(12):
        half, at = down_tile(t)
        wb_in[half, at] = whole[:, 128 * t : 128 * t + 128]
    whole = jnp.concatenate([pad_rows(wo_in[...]), jnp.zeros((80, 64), F32)], axis=1).astype(BF)
    for t in range(5):
        wb_in[t // 4, 18 + t % 4] = whole[:, 128 * t : 128 * t + 128]
    wb_in[0, 22:24] = jnp.zeros((2, 80, 128), BF)
    wb_in[1, 19:24] = jnp.zeros((5, 80, 128), BF)
    pl.semaphore_wait(barrier, 23)

    zz = 2 * zh + zl
    order = ("ayb", "yba", "yab")

    def pick(n, u, w):
        return u if n < 2 else u * (1 - k) + w * k

    def coord(n, axis):
        if axis == "y":
            return yy
        return pick(n, zz, xx) if axis == "a" else pick(n, xx, zz)

    def along(n, axis, step):
        if axis == "y":
            return f, ctx_at(zl, (yy + step) % 4, k)
        z = (zz + step) % 4
        by_x = (zh * 4 + (xx + step) % 4, c)
        by_z = ((z // 2) * 4 + xx, ctx_at(z % 2, yy, k))
        first, second = (by_z, by_x) if axis == "a" else (by_x, by_z)
        return pick(n, first[0], second[0]), pick(n, first[1], second[1])

    def region(n, done, axis=None, step=0):
        at = []
        for name in "aby":
            if name in done:
                at.append(slice(None))
            else:
                at.append((coord(n, name) + 4 - step) % 4 if name == axis else coord(n, name))
        return wb.at[(k, n, *at)]

    local = [
        pltpu.make_async_copy(xc.at[c], xc_r.at[c], ls.at[0]),
        pltpu.make_async_copy(wa_in.at[k], wa.at[k, f], ls.at[1]),
        *(
            pltpu.make_async_copy(
                wb_in.at[k, 8 * n + 2 * yy + zl], region(n, ()), ls.at[4 + n]
            )
            for n in range(3)
        ),
        pltpu.make_async_copy(cos_in.at[:, c], cos_s, ls.at[2]),
        pltpu.make_async_copy(sin_in.at[:, c], sin_s, ls.at[3]),
    ]
    for copy in local:
        copy.start()

    def gather_first(w_in, w, sem):
        send(w_in.at[k], w.at[k, f], sem, fz, c)
        for step in range(1, 4):
            send(w_in.at[k], w.at[k, f], sem + step, zh * 4 + (xx + step) % 4, c)

    def gather_second(w, sem):
        arrived(w.at[k, fz], sem)
        return [
            send(w.at[k, fz], w.at[k, fz], sem + 3 + step, zh * 4 + (xx + step) % 4, c)
            for step in range(1, 4)
        ]

    def gather_third(w, sem):
        for step in range(1, 4):
            from_x = (xx + 4 - step) % 4
            arrived(w.at[k, zh * 4 + from_x], sem + step)
            arrived(w.at[k, (1 - zh) * 4 + from_x], sem + 3 + step)
        return [send(w.at[k], w.at[k], sem + 7, f, other)]

    def gather_last(w, sem):
        arrived(w.at[1 - k], sem + 7)

    sem_b = take(30)

    def spread(turn):
        if turn > 0:
            spread_wait(turn - 1)
        out = []
        for n in range(3):
            axis, done = order[n][turn], order[n][:turn]
            for step in range(1, 4):
                if turn == 0:
                    src = wb_in.at[k, 8 * n + 2 * yy + zl]
                else:
                    src = region(n, done)
                copy = send(
                    src, region(n, done), sem_b + 9 * turn + 3 * n + step - 1, *along(n, axis, step)
                )
                if turn > 0:
                    out.append(copy)
        return out

    def spread_wait(turn, groups=(0, 1, 2)):
        for n in groups:
            axis, done = order[n][turn], order[n][:turn]
            for step in range(1, 4):
                arrived(region(n, done, axis, step), sem_b + 9 * turn + 3 * n + step - 1)

    sem_a = take(8)
    gather_first(wa_in, wa, sem_a)
    sem_x = take(16)
    for step in range(1, 16):
        to = (c + step) % 16
        send(xc.at[to, 0:16], xc_r.at[c, 0:16], sem_x + step, f, to)
    gather_second(wa, sem_a)
    spread(0)
    sem_c = take(16)
    for step in range(1, 16):
        to = (c + step) % 16
        send(xc.at[to, 16:32], xc_r.at[c, 16:32], sem_c + step, f, to)

    def make_bias(slot, carry):
        e = ctx_at((slot // 2) % 2, slot // 4, slot % 2)
        j = lax.broadcasted_iota(jnp.int32, (128, 128), 0)
        i = lax.broadcasted_iota(jnp.int32, (128, 128), 1)
        ok = (j // 8 < i // 8) | ((j // 8 == i // 8) & (8 * e + j % 8 <= 8 * c + i % 8))
        bias[pl.ds(pl.multiple_of(slot * 128, 128), 128), :] = jnp.where(ok, 0.0, NEG)
        return carry

    lax.fori_loop(0, 16, make_bias, 0)
    for copy in local:
        copy.wait()
    from_wb = spread(1)
    for step in range(1, 16):
        arrived(xc_r.at[(c + 16 - step) % 16, 0:16], sem_x + step)

    x_raw = xc_r[:, 0:16, :].reshape(ROWS, DP)
    lane = lane_iota((ROWS, DP))
    tag = jnp.sum(jnp.where(lane == 72, x_raw.astype(F32), 0.0), axis=1, keepdims=True)
    place = lane_iota((ROWS, ROWS)).astype(F32)
    perm[...] = jnp.where(tag == place, 1.0, 0.0).astype(BF)
    perm_t = jnp.where(tag == place, 1.0, 0.0).T.astype(BF)
    x = mm(perm_t, x_raw)
    x = jnp.where(lane % 80 < 72, x, 0.0)
    xs[...] = x

    gather_third(wa, sem_a)
    r1 = lax.rsqrt(jnp.sum(x * x, axis=-1, keepdims=True) * (1.0 / D) + 1e-5)
    gather_last(wa, sem_a)

    def gain_row(which):
        hot = jnp.where(lane_iota((16, 128)) == 64 + which, 1.0, 0.0).astype(BF)
        block = wa[1, :, :, 0:128].reshape(DP, 128)
        return mm_nt(hot, block)[0:1, :]

    gain1, gain2 = gain_row(0), gain_row(1)
    a1 = x * r1 * gain1
    a1b = a1.astype(BF)
    act1[...] = a1b
    act1t[...] = a1.T.astype(BF)

    cos = cos_s[...].reshape(ROWS, 128)
    sin = sin_s[...].reshape(ROWS, 128)
    low = lane_iota((ROWS, 128)) < 64
    cos_kv = jnp.where(low, cos, 1.0)
    sin_kv = jnp.where(low, sin, 0.0)

    mine = slot_at(zl, yy, k)
    kv_pre = mm(a1b, wa[1, :, :, 128:512].reshape(DP, 384))
    for g in range(3):
        u = kv_pre[:, 128 * g : 128 * g + 128]
        kv[mine, g] = (u * cos_kv + partner_lanes(u) * sin_kv).astype(BF)
    sem_k = take(16)

    near = slot_at(1 - zl, yy, k)

    def kv_along_y(slot, a):
        for off in (1, 3):
            send(kv.at[slot], kv.at[slot], sem_k + a * 4 + off, f, ctx_at(zl, (yy + off) % 4, k))

    send(kv.at[mine], kv.at[mine], sem_k, f, other)
    send(kv.at[mine], kv.at[mine], sem_k + 4, f, ctx_at(1 - zl, yy, k))
    kv_along_y(mine, 0)

    def kv_direct(off):
        for a in (0, 1):
            if (a, off) != (0, 0):
                at = slot_at(zl if a == 0 else 1 - zl, (yy + 4 - off) % 4, k)
                arrived(kv.at[at], sem_k + a * 4 + off)
                send(kv.at[at], kv.at[at], sem_k + 8 + a * 4 + off, f, other)
                if (a, off) in ((0, 1), (1, 3)):
                    to = ctx_at(zl, (yy + off) % 4, k)
                    send(kv.at[at], kv.at[at], sem_k + a * 4 + 2, f, to)

    def kv_across(off):
        for a in (0, 1):
            at = slot_at(zl if a == 0 else 1 - zl, (yy + 4 - off) % 4, 1 - k)
            arrived(kv.at[at], sem_k if (a, off) == (0, 0) else sem_k + 8 + a * 4 + off)

    from_wb += spread(2)
    for t in range(5):
        w = wa[0, :, :, 128 * t : 128 * t + 128] if t < 4 else wa[1, :, :, 0:128]
        u = mm(a1b, w.reshape(DP, 128))
        u = (u * cos + partner_lanes(u) * sin).astype(BF).astype(F32) * 0.125
        for half in range(2):
            h = 2 * t + half
            if h < 9:
                g, r = h // 3, h % 3
                v = jnp.where(low, u if half == 0 else pltpu.roll(u, 64, 1), 0.0)
                vt = v.T
                for ih in range(2):
                    at = 384 * ih + 128 * r
                    qx[g, at : at + 128, :] = v[128 * ih : 128 * ih + 128].astype(BF)
                    qt[g, :, at : at + 128] = vt[:, 128 * ih : 128 * ih + 128].astype(BF)

    kv_direct(0)
    kv_along_y(near, 1)

    for step in range(1, 16):
        arrived(xc_r.at[(c + 16 - step) % 16, 16:32], sem_c + step)
    dy[...] = mm_tn(perm[...], xc_r[:, 16:32, :].reshape(ROWS, DP)).astype(BF)

    st_m[...] = jnp.full(st_m.shape, NEG, F32)
    st_l[...] = jnp.zeros(st_l.shape, F32)
    acc[...] = jnp.zeros(acc.shape, F32)

    def three(b):
        return jnp.concatenate([b, b, b], axis=1)

    def fold_forward(off):
        group = (yy + 4 - off) % 4

        def per_head(g, carry):
            b3 = three(bias[pl.ds(pl.multiple_of(group * 512, 512), 512), :])
            for key_half, lane_half in ((0, 0), (0, 1), (1, 1)):
                at = 384 * lane_half
                rows = kv[pl.ds(group * 4, 4), g, 128 * key_half : 128 * key_half + 128, :]
                rows = rows.reshape(512, 128)
                s = mm(rows, qt[g, :, at : at + 384])
                if key_half == lane_half:
                    s = s + b3
                old = st_m[g, :, at : at + 384]
                new = jnp.maximum(old, jnp.max(s, axis=0, keepdims=True))
                p = jnp.exp(s - new)
                scale = jnp.exp(old - new)
                st_m[g, :, at : at + 384] = new
                st_l[g, :, at : at + 384] = (
                    st_l[g, :, at : at + 384] * scale + jnp.sum(p, axis=0, keepdims=True)
                )
                acc[g, :, at : at + 384] = acc[g, :, at : at + 384] * scale + mm_tn(
                    rows, p.astype(BF)
                )
            return carry

        lax.fori_loop(0, 3, per_head, 0)

    kv_direct(STEPS[1])
    kv_across(0)
    fold_forward(0)
    kv_direct(STEPS[2])
    kv_across(STEPS[1])
    fold_forward(STEPS[1])
    kv_direct(STEPS[3])
    kv_across(STEPS[2])
    fold_forward(STEPS[2])
    kv_across(STEPS[3])
    for n in (1, 0, 2):
        spread_wait(2, (n,))
        from_wb.append(send(wb.at[k, n], wb.at[k, n], sem_b + 27 + n, f, other))
    fold_forward(STEPS[3])

    def head_rows(ref, g, r):
        return jnp.concatenate(
            [ref[g, :, 384 * ih + 128 * r : 384 * ih + 128 * r + 128].T for ih in range(2)], axis=0
        )

    for g in range(3):
        ot[g] = acc[g] / st_l[g]
        st_l[g] = st_m[g] + jnp.log(st_l[g])
    for t in range(5):
        a = pltpu.roll(head_rows(ot, 2 * t // 3, 2 * t % 3), 64, 1)
        b = head_rows(ot, (2 * t + 1) // 3, (2 * t + 1) % 3) if t < 4 else jnp.zeros((ROWS, 128), F32)
        attb[:, 128 * t : 128 * t + 128] = jnp.where(low, a, b).astype(BF)

    for n in range(3):
        arrived(wb.at[1 - k, n], sem_b + 27 + n)

    def fixed(half, n):
        return isinstance(half, int) and isinstance(n, int) and (half, n) == LAST

    def tile_at(half, n, y, z):
        if fixed(half, n):
            blocks = [wb[1, 2, :, 2 * q + z, y] for q in range(2)]
        else:
            blocks = [wb[half, n, 2 * q + z, :, y] for q in range(2)]
        return jnp.concatenate(blocks, axis=0).reshape(DP, 128)

    def put_tile(half, n, y, z, value):
        value = value.astype(BF).reshape(2, 4, 80, 128)
        for q in range(2):
            if fixed(half, n):
                wb[1, 2, :, 2 * q + z, y] = value[q]
            else:
                wb[half, n, 2 * q + z, :, y] = value[q]

    def pair(half, p):
        return jnp.concatenate([tile_at(half, p // 4, p % 4, z) for z in range(2)], axis=1)

    def put_pair(half, p, value):
        for z in range(2):
            put_tile(half, p // 4, p % 4, z, value[:, 128 * z : 128 * z + 128])

    def out_tile(t):
        return tile_at(0, 2, 1 + t // 2, t % 2) if t < 4 else tile_at(1, 2, 1, 0)

    out_w = jnp.concatenate([out_tile(t) for t in range(5)], axis=1)
    m0 = xs[...] + mm_nt(attb[...], out_w)
    r2 = lax.rsqrt(jnp.sum(m0 * m0, axis=-1, keepdims=True) * (1.0 / D) + 1e-5)
    mid[...] = m0
    a2 = m0 * r2 * gain2
    a2b = a2.astype(BF)
    a2t = a2.T.astype(BF)
    dyb = dy[...]
    dyt = dyb.astype(F32).T.astype(BF)

    for copy in from_wb:
        copy.wait_send()
    sends[:] = [copy for copy in sends if all(copy is not done for done in from_wb)]

    def ff(j, carry):
        total, dact = carry
        last = isinstance(j, int)
        at_g, at_u, at_d = ((0, 8), (1, 7), (1, 8)) if last else ((0, j), (1, j), (j // 3, 5 + j % 3))
        wg, wu, wd = pair(*at_g), pair(*at_u), pair(*at_d)
        gate, up = mm(a2b, wg), mm(a2b, wu)
        sig = jax.nn.sigmoid(gate)
        swish = gate * sig
        hid = (swish * up).astype(BF)
        total = total + mm_nt(hid, wd)
        dh = mm(dyb, wd)
        dg = (dh * up * sig * (1.0 + gate * (1.0 - sig))).astype(BF)
        du = (dh * swish).astype(BF)
        put_pair(*at_d, mm(dyt, hid))
        put_pair(*at_g, mm(a2t, dg))
        put_pair(*at_u, mm(a2t, du))
        dact = dact + mm_nt(dg, wg) + mm_nt(du, wu)
        return total, dact

    zero = jnp.zeros((ROWS, DP), F32)
    total, dact = ff(5, lax.fori_loop(0, 5, ff, (zero, zero)))

    sem_r = take(42)

    def add(ref, at, got_at):
        v = ref[at].astype(F32)
        for r in got_at:
            v = v + r.astype(F32)
        return v

    def red_core(n):
        send(wb.at[1 - k, n], gbc.at[n], sem_r + n, f, other)

    def red_one(n):
        arrived(gbc.at[n], sem_r + n)

        def body(i, carry):
            wb[k, n, i // 4, i % 4] = (
                wb[k, n, i // 4, i % 4].astype(F32) + gbc[n, i // 4, i % 4].astype(F32)
            ).astype(BF)
            return carry

        lax.fori_loop(0, 16, body, 0)
        axis = order[n][2]
        for step in range(1, 4):
            to = (coord(n, axis) + step) % 4
            src = wb.at[k, n, to] if axis == "a" else wb.at[k, n, :, to]
            send(src, q1.at[n, step - 1], sem_r + 3 + 3 * n + step - 1, *along(n, axis, step))

    def red_two(n):
        for step in range(3):
            arrived(q1.at[n, step], sem_r + 3 + 3 * n + step)
        axis, at = order[n][2], coord(n, order[n][2])

        def body(i, carry):
            v = (wb[k, n, at, i] if axis == "a" else wb[k, n, i, at]).astype(F32)
            for step in range(3):
                v = v + q1[n, step, i].astype(F32)
            t1[n, i] = v.astype(BF)
            return carry

        lax.fori_loop(0, 4, body, 0)
        axis = order[n][1]
        for step in range(1, 4):
            to = (coord(n, axis) + step) % 4
            src = t1.at[n, :, to] if axis == "y" else t1.at[n, to]
            send(src, q2.at[n, step - 1], sem_r + 12 + 3 * n + step - 1, *along(n, axis, step))

    def red_three(n):
        for step in range(3):
            arrived(q2.at[n, step], sem_r + 12 + 3 * n + step)
        axis, at = order[n][1], coord(n, order[n][1])
        own = (n, slice(None), at) if axis == "y" else (n, at)
        t2[n] = add(t1, own, [q2[n, i] for i in range(3)]).astype(BF)
        axis = order[n][0]
        for step in range(1, 4):
            to = (coord(n, axis) + step) % 4
            send(t2.at[n, to], q3.at[n, step - 1], sem_r + 21 + 3 * n + step - 1, *along(n, axis, step))

    def red_four():
        for n in range(3):
            for step in range(3):
                arrived(q3.at[n, step], sem_r + 21 + 3 * n + step)
            own = add(t2, (n, coord(n, order[n][0])), [q3[n, i] for i in range(3)])
            gbf[k, yy, zl, n] = own.astype(BF)
        piece = gbf.at[k, yy, zl]
        for a, off in CHIPS:
            to = ctx_at(zl if a == 0 else 1 - zl, (yy + off) % 4, k)
            send(piece, piece, sem_r + 30 + 4 * a + off, f, to)

    def red_five():
        for a, off in CHIPS:
            z = zl if a == 0 else 1 - zl
            arrived(gbf.at[k, (yy + 4 - off) % 4, z], sem_r + 30 + 4 * a + off)
        send(gbf.at[k], gbf.at[k], sem_r + 38, f, other)

    def red_six():
        arrived(gbf.at[1 - k], sem_r + 38)

    sem_g = take(36)

    def in_core(p):
        send(ga.at[p, 1 - k], gac.at[p], sem_g + 18 * p, f, other)

    def in_one(p):
        arrived(gac.at[p], sem_g + 18 * p)
        ga[p, k] = (ga[p, k].astype(F32) + gac[p].astype(F32)).astype(BF)
        for step in range(1, 8):
            to = (f + step) % 8
            send(ga.at[p, k, to], gax.at[p, step - 1], sem_g + 18 * p + step, to, c)

    def in_two(p):
        for step in range(1, 8):
            arrived(gax.at[p, step - 1], sem_g + 18 * p + step)
        gay_s[p] = add(ga, (p, k, f), [gax[p, i] for i in range(7)]).astype(BF)
        for a, off in CHIPS:
            to = ctx_at(zl if a == 0 else 1 - zl, (yy + off) % 4, k)
            send(gay_s.at[p], gay.at[p, 4 * a + off], sem_g + 18 * p + 8 + 4 * a + off, f, to)

    def in_three(p):
        for a, off in CHIPS:
            arrived(gay.at[p, 4 * a + off], sem_g + 18 * p + 8 + 4 * a + off)
        gaf[p, k] = add(gay_s, p, [gay[p, 4 * a + off] for a, off in CHIPS]).astype(BF)
        send(gaf.at[p, k], gaf.at[p, k], sem_g + 18 * p + 16, f, other)

    def in_four(p):
        arrived(gaf.at[p, 1 - k], sem_g + 18 * p + 16)

    red_core(0)
    red_core(1)

    def give_back(value, src, dst, sem):
        src[...] = mm(perm[...], value.astype(BF)).astype(BF).reshape(16, 16, DP)
        for step in range(1, 16):
            send(src.at[(c + step) % 16], dst.at[c], sem + step, f, (c + step) % 16)
        dst[c] = src[c]

    sem_o = take(16)
    sem_i = take(16)
    m0 = mid[...]
    give_back(m0 + total, bo_s, bo_r, sem_o)

    dyf = dyb.astype(F32)
    gain_grad2 = jnp.sum(dact * m0 * r2, axis=0, keepdims=True)
    wgt = dact * gain2
    inner = jnp.sum(wgt * m0, axis=-1, keepdims=True) * (1.0 / D)
    dm = dyf + r2 * wgt - m0 * (r2 * r2 * r2) * inner
    dmid[...] = dm
    dmb = dm.astype(BF)
    dmt = dm.T.astype(BF)

    for t in range(5):
        u = mm(dmb, out_tile(t)).astype(BF).astype(F32)
        for half in range(2):
            h = 2 * t + half
            if h < 9:
                g, r = h // 3, h % 3
                v = jnp.where(low, 0.0, u if half == 1 else pltpu.roll(u, 64, 1))
                vt = v.T
                for ih in range(2):
                    at = 384 * ih + 128 * r
                    dox[g, at : at + 128, :] = v[128 * ih : 128 * ih + 128].astype(BF)
                    dot_[g, :, at : at + 128] = vt[:, 128 * ih : 128 * ih + 128].astype(BF)
    grad_out = mm(dmt, attb[...]).astype(BF)
    for t in range(5):
        at = (0, 2, 1 + t // 2, t % 2) if t < 4 else (1, 2, 1, 0)
        put_tile(*at, grad_out[:, 128 * t : 128 * t + 128])
    red_core(2)

    for g in range(3):
        st_m[g] = jnp.sum(dot_[g].astype(F32) * ot[g], axis=0, keepdims=True)
    dqt[...] = jnp.zeros(dqt.shape, F32)

    def fold_backward(at_step, off):
        group = (yy + 4 - off) % 4

        def per_head(g, carry):
            b3 = three(bias[pl.ds(pl.multiple_of(group * 512, 512), 512), :])
            for key_half in range(2):
                rows = kv[pl.ds(group * 4, 4), g, 128 * key_half : 128 * key_half + 128, :]
                rows = rows.reshape(512, 128)
                grad = None
                for lane_half in range(key_half, 2):
                    at = 384 * lane_half
                    s = mm(rows, qt[g, :, at : at + 384])
                    if key_half == lane_half:
                        s = s + b3
                    p = jnp.exp(s - st_l[g, :, at : at + 384])
                    dp = mm(rows, dot_[g, :, at : at + 384])
                    ds = (p * (dp - st_m[g, :, at : at + 384])).astype(BF)
                    part = mm(ds, qx[g, at : at + 384, :]) + mm(
                        p.astype(BF), dox[g, at : at + 384, :]
                    )
                    grad = part if grad is None else grad + part
                    dqt[g, :, at : at + 384] += mm_tn(rows, ds)
                dkv_p[at_step, :, g, 128 * key_half : 128 * key_half + 128, :] = grad.astype(
                    BF
                ).reshape(4, 128, 128)
            return carry

        lax.fori_loop(0, 3, per_head, 0)

    sem_d1 = take(8)
    sem_d = take(4)

    def dkv_first(at_step):
        for z in range(2):
            send(
                dkv_p.at[at_step, 2 * z + 1 - k], d1_r.at[at_step, z], sem_d1 + 2 * at_step + z,
                f, other,
            )

    def dkv_second(at_step, off):
        for z in range(2):
            arrived(d1_r.at[at_step, z], sem_d1 + 2 * at_step + z)
        for z in range(2):
            d2_s[at_step, z] = (
                dkv_p[at_step, 2 * z + k].astype(F32) + d1_r[at_step, z].astype(F32)
            ).astype(BF)
        if off != 0:
            send(
                d2_s.at[at_step], d2_r.at[off - 1], sem_d + off,
                f, ctx_at(zl, (yy + 4 - off) % 4, k),
            )

    red_one(0)
    red_one(1)
    red_one(2)
    fold_backward(0, BACK[0])
    dkv_first(0)
    dkv_second(0, BACK[0])
    fold_backward(1, BACK[1])
    dkv_first(1)
    dkv_second(1, BACK[1])
    fold_backward(2, BACK[2])
    dkv_first(2)
    dkv_second(2, BACK[2])
    fold_backward(3, BACK[3])
    dkv_first(3)
    for n in (1, 0, 2):
        red_two(n)
    dkv_second(3, BACK[3])
    for off in range(1, 4):
        arrived(d2_r.at[off - 1], sem_d + off)
    dz_s[...] = add(d2_s, (3, 1 - zl), [d2_r[i, 1 - zl] for i in range(3)]).astype(BF)
    send(dz_s, dz_r, sem_d, f, ctx_at(1 - zl, yy, k))

    dq_tiles = []
    for t in range(5):
        a = head_rows(dqt, 2 * t // 3, 2 * t % 3)
        if t < 4:
            b = pltpu.roll(head_rows(dqt, (2 * t + 1) // 3, (2 * t + 1) % 3), 64, 1)
        else:
            b = jnp.zeros((ROWS, 128), F32)
        u = jnp.where(low, a, b) * 0.125
        dq_tiles.append((u * cos - partner_lanes(u) * sin).astype(BF))
    dq = jnp.concatenate(dq_tiles, axis=1)
    a1t = act1t[...]
    grad_q = mm(a1t, dq)
    for half in range(2):
        ga[0, half] = grad_q[:, 256 * half : 256 * half + 256].astype(BF).reshape(8, 80, 256)
    in_core(0)
    dact1 = mm_nt(dq[:, 0:512], wa[0].reshape(DP, 512)) + mm_nt(
        dq[:, 512:640], wa[1, :, :, 0:128].reshape(DP, 128)
    )
    in_one(0)
    dkv = add(d2_s, (3, zl), [d2_r[i, zl] for i in range(3)])
    arrived(dz_r, sem_d)
    dkv = dkv + dz_r[...].astype(F32)
    for g in range(3):
        u = dkv[g]
        u = (u * cos_kv - partner_lanes(u) * sin_kv).astype(BF)
        at = 128 + 128 * g
        part = mm(a1t, u).astype(BF).reshape(8, 80, 128)
        lanes = slice(128, 256) if g != 1 else slice(0, 128)
        ga[1, 0 if g == 0 else 1, :, :, lanes] = part
        dact1 = dact1 + mm_nt(u, wa[1, :, :, at : at + 128].reshape(DP, 128))

    x = xs[...]
    gain_grad1 = jnp.sum(dact1 * x * r1, axis=0, keepdims=True)
    gains = jnp.concatenate([gain_grad1, gain_grad2, jnp.zeros((6, DP), F32)], axis=0)
    hot = jnp.where(
        lane_iota((8, 128)) == 64 + lax.broadcasted_iota(jnp.int32, (8, 128), 0), 1.0, 0.0
    )
    hot = jnp.where(lax.broadcasted_iota(jnp.int32, (8, 128), 0) < 2, hot, 0.0)
    gain_cols = mm(gains.T.astype(BF), hot.astype(BF))
    ga[1, 0, :, :, 0:128] = (grad_q[:, 512:640] + gain_cols).astype(BF).reshape(8, 80, 128)
    in_core(1)
    in_one(1)
    for n in (1, 0, 2):
        red_three(n)

    wgt = dact1 * gain1
    inner = jnp.sum(wgt * x, axis=-1, keepdims=True) * (1.0 / D)
    give_back(
        dmid[...] + r1 * wgt - x * (r1 * r1 * r1) * inner, ig_s, ig_r, sem_i
    )
    red_four()
    in_two(0)
    in_two(1)
    red_five()
    in_three(0)
    for step in range(1, 16):
        arrived(bo_r.at[(c + 16 - step) % 16], sem_o + step)
    bo_out[...] = bo_r[...]
    in_three(1)
    for step in range(1, 16):
        arrived(ig_r.at[(c + 16 - step) % 16], sem_i + step)
    ig_out[...] = ig_r[...]
    red_six()
    gb_out[...] = gbf[...]
    in_four(0)
    in_four(1)
    ga_out[...] = gaf[...]
    for copy in sends:
        copy.wait_send()


def tables():
    freq = np.power(np.float32(100000.0), -(np.arange(32, dtype=np.float32) * np.float32(2.0 / 64)))
    angle = np.arange(4096, dtype=np.float32)[:, None] * freq[None, :].astype(np.float32)
    cos, sin = np.cos(angle), np.sin(angle)
    cos = np.concatenate([cos, cos, cos, cos], axis=1)
    sin = np.concatenate([-sin, sin, -sin, sin], axis=1)
    shape = (32, 16, 8, 128)
    return cos.reshape(shape).astype(np.float32), sin.reshape(shape).astype(np.float32)


def placements():
    cols = np.zeros((D, DP), np.float32)
    at = np.arange(D)
    cols[at, at // 72 * 80 + at % 72] = 1.0
    rows = np.zeros((ROWS, ROWS), np.float32)
    at = np.arange(ROWS)
    rows[at, at // 8 % 2 * 128 + at // 16 * 8 + at % 8] = 1.0
    return jnp.asarray(cols, BF), jnp.asarray(rows, BF)


def finish(
    bo_h, ig_h, ga_h, gb_h, cols_h, rows_h,
    out, grad_in, n1, gq, gkv, go, n2, gg, gu, gd,
    bo, ig, ga, gb, cols, rows, sems,
):
    copies = [
        pltpu.make_async_copy(src, dst, sems.at[n])
        for n, (src, dst) in enumerate(
            ((gb_h, gb), (cols_h, cols), (rows_h, rows), (bo_h, bo), (ig_h, ig), (ga_h, ga))
        )
    ]
    for copy in copies:
        copy.start()
    for copy in copies:
        copy.wait()
    for src, dst in ((bo, out), (ig, grad_in)):
        narrow = mm_nt(cols[...], src[...].reshape(ROWS, DP)).astype(BF)
        dst[...] = mm(narrow, rows[...]).astype(dst.dtype)

    def part(ref, *at):
        return ref[at].astype(F32)

    for t in range(4):
        gq[:, 128 * t : 128 * t + 128] = part(ga, 0, t // 2)[0:72, 128 * (t % 2) : 128 * (t % 2) + 128]
    last = part(ga, 1, 0)[:, 0:128]
    gq[:, 512:576] = last[0:72, 0:64]
    row = lax.broadcasted_iota(jnp.int32, (16, 128), 0)
    hot = jnp.where((lane_iota((16, 128)) == 64 + row) & (row < 2), 1.0, 0.0).astype(BF)
    gains = mm_nt(hot, last.astype(BF))
    n1[...] = gains[0:1, 0:72]
    n2[...] = gains[1:2, 0:72]
    low = lane_iota((80, 128)) < 64
    tiles = [part(ga, 1, 0)[:, 128:256], part(ga, 1, 1)[:, 0:128], part(ga, 1, 1)[:, 128:256]]
    turn = [pltpu.roll(t, 64, 1) for t in tiles]
    heads = [
        jnp.where(low, tiles[0], turn[1]),
        jnp.where(low, tiles[2], tiles[0]),
        jnp.where(low, turn[1], tiles[2]),
    ]
    for g in range(3):
        gkv[:, 128 * g : 128 * g + 128] = heads[g][0:72]

    def tile(half, t):
        return part(gb, half, (t % 8) // 2, t % 2, t // 8)

    for half, ref in ((0, gg), (1, gu)):
        for t in range(12):
            ref[:, 128 * t : 128 * t + 128] = tile(half, up_tile(half, t))[0:72]
    for t in range(12):
        gd[:, 128 * t : 128 * t + 128] = tile(*down_tile(t))[0:72]
    for t in range(4):
        go[:, 128 * t : 128 * t + 128] = tile(0, 18 + t)[0:72]
    go[:, 512:576] = tile(1, 18)[0:72, 0:64]


def local(tokens, positions, gain1, wq, wkv, wo, gain2, wg, wu, wd, cotangent):
    cos, sin = tables()
    cols, rows = placements()

    def v(shape, dtype=BF):
        return pltpu.VMEM(shape, dtype)

    any_space = pl.BlockSpec(memory_space=pl.ANY)
    vmem = pl.BlockSpec(memory_space=pltpu.VMEM)
    scratch = [
        v((D, ROWS)), v((D, ROWS)), v((72, 576)), v((72, 384)), v((72, 576)), v((72, 1536)),
        v((72, 1536)), v((72, 1536)), v((D, DP)), v((ROWS, ROWS)),
        v((16, 32, DP)), v((2, 80, WA)), v((2, TB, 80, 128)),
        v((16, 32, DP)), v((2, 8, 80, WA)), v((2, 3, 4, 4, 4, 80, 128)),
        v((32, 8, 128), F32), v((32, 8, 128), F32),
        v((16, 3, 256, 128)), v((2048, 128), F32), v((ROWS, ROWS)),
        v((3, 128, 768)), v((3, 768, 128)), v((3, 128, 768)), v((3, 768, 128)),
        v((3, 1, 768), F32), v((3, 1, 768), F32), v((3, 128, 768), F32), v((3, 128, 768), F32),
        v((3, 128, 768), F32),
        v((ROWS, DP), F32), v((ROWS, DP)), v((ROWS, DP), F32), v((ROWS, DP)), v((DP, ROWS)),
        v((ROWS, DP)), v((ROWS, DP), F32),
        v((4, 4, 3, 256, 128)), v((4, 2, 3, 256, 128)), v((4, 2, 3, 256, 128)),
        v((3, 2, 3, 256, 128)), v((3, 256, 128)), v((3, 256, 128)),
        v((2, 2, 8, 80, 256)), v((2, 8, 80, 256)), v((2, 7, 80, 256)),
        v((2, 80, 256)), v((2, 8, 80, 256)), v((2, 2, 80, 256)),
        v((3, 4, 4, 4, 80, 128)), v((3, 3, 4, 4, 80, 128)), v((3, 4, 4, 80, 128)),
        v((3, 3, 4, 80, 128)), v((3, 4, 80, 128)),
        v((3, 3, 80, 128)), v((2, 4, 2, 3, 80, 128)),
        v((16, 16, DP)), v((16, 16, DP)), v((16, 16, DP)), v((16, 16, DP)),
        pltpu.SemaphoreType.DMA((216,)), pltpu.SemaphoreType.DMA((216,)),
        pltpu.SemaphoreType.DMA((17,)),
    ]
    bo, ig, ga, gb = pl.pallas_call(
        kernel,
        out_shape=(
            jax.ShapeDtypeStruct((16, 16, DP), BF),
            jax.ShapeDtypeStruct((16, 16, DP), BF),
            jax.ShapeDtypeStruct((2, 2, 80, 256), BF),
            jax.ShapeDtypeStruct((2, 4, 2, 3, 80, 128), BF),
        ),
        in_specs=[pl.BlockSpec(memory_space=pltpu.SMEM)] + [vmem] * 2 + [any_space] * 12,
        out_specs=(vmem,) * 4,
        scratch_shapes=scratch,
        compiler_params=pltpu.CompilerParams(
            collective_id=0, has_side_effects=True, vmem_limit_bytes=62 * 1024 * 1024
        ),
        name="layer",
    )(
        positions, gain1.reshape(1, 72), gain2.reshape(1, 72), tokens[0].T, cotangent[0].T,
        wq, wkv, wo.T, wg, wu, wd.T, cols, rows, jnp.asarray(cos), jnp.asarray(sin),
    )

    def f32(*shape):
        return jax.ShapeDtypeStruct(shape, F32)

    outs = pl.pallas_call(
        finish,
        out_shape=(
            jax.ShapeDtypeStruct((D, ROWS), BF), f32(D, ROWS), f32(1, 72), f32(72, 576),
            f32(72, 384), f32(72, 576), f32(1, 72), f32(72, 1536), f32(72, 1536), f32(72, 1536),
        ),
        in_specs=[any_space] * 6,
        out_specs=(vmem,) * 10,
        scratch_shapes=[
            v((16, 16, DP)), v((16, 16, DP)), v((2, 2, 80, 256)), v((2, 4, 2, 3, 80, 128)),
            v((D, DP)), v((ROWS, ROWS)), pltpu.SemaphoreType.DMA((6,)),
        ],
        compiler_params=pltpu.CompilerParams(vmem_limit_bytes=60 * 1024 * 1024),
        name="finish",
    )(bo, ig, ga, gb, cols, rows)
    out, grad_in, n1, gq, gkv, go, n2, gg, gu, gd = outs
    return out.T[None], grad_in.T[None], n1.reshape(72), gq, gkv, go.T, n2.reshape(72), gg, gu, gd.T


def solution(mesh):
    rows, model, last = P("fsdp", "ctx", None), P("fsdp", None), P(None, "fsdp")
    gain = P("fsdp")
    return jax.shard_map(
        local,
        mesh=mesh,
        in_specs=(rows, P("fsdp", "ctx"), gain, model, model, last, gain, model, model, last, rows),
        out_specs=(rows, rows, gain, model, model, last, gain, model, model, last),
        check_vma=False,
    )
```

```python
import numpy as np

import jax
import jax.numpy as jnp
from jax import lax
from jax.experimental import pallas as pl
from jax.experimental.pallas import tpu as pltpu
from jax.sharding import PartitionSpec as P

MESH = pl.DeviceIdType.MESH
BF = jnp.bfloat16
F32 = jnp.float32
D = 576
DP = 640
ROWS = 256
WA = 512
TB = 24
FC = 256
NEG = -1e30
STEPS = (0, 1, 3, 2)
BACK = (2, 1, 3, 0)
LAST = (1, 2)
CHIPS = ((0, 1), (0, 3), (1, 0), (1, 1), (1, 3), (0, 2), (1, 2))


def mm(a, b):
    return jnp.dot(a, b, preferred_element_type=F32)


def mm_nt(a, b):
    return lax.dot_general(a, b, (((1,), (1,)), ((), ())), preferred_element_type=F32)


def mm_tn(a, b):
    return lax.dot_general(a, b, (((0,), (0,)), ((), ())), preferred_element_type=F32)


def up_tile(half, t):
    return t if t < 10 else t + (6 if half == 0 else 4)


def down_tile(t):
    return t // 6, 10 + t % 6 if t < 10 else 6 + t


def lane_iota(shape):
    return lax.broadcasted_iota(jnp.int32, shape, len(shape) - 1)


def partner_lanes(u):
    lane = lane_iota(u.shape)
    return jnp.where(lane % 64 < 32, pltpu.roll(u, 96, 1), pltpu.roll(u, 32, 1))


def kernel(
    pos, g1_in, g2_in, tok_h, cot_h, wq_h, wkv_h, wo_h, wg_h, wu_h, wd_h, cols_h, rows_h, cos_in, sin_in,
    bo_out, ig_out, ga_out, gb_out,
    tok, cot, wq_in, wkv_in, wo_in, wg_in, wu_in, wd_in, spread_cols, spread_rows,
    xc, wa_in, wb_in, xc_r, wa, wb, cos_s, sin_s, kv, bias, perm,
    qt, qx, dot_, dox, st_m, st_l, acc, ot, dqt,
    xs, dy, mid, act1, act1t, attb, dmid,
    dkv_p, d1_r, d2_s, d2_r, dz_s, dz_r,
    ga, gac, gax, gay_s, gay, gaf,
    gbc, q1, t1, q2, t2, q3, gbf,
    bo_s, bo_r, ig_s, ig_r,
    ss, rs, ls,
):
    f = lax.axis_index("fsdp")
    c = lax.axis_index("ctx")
    zh, xx = f // 4, f % 4
    zl, yy, k = c // 8, (c // 2) % 4, c % 2
    fz = (1 - zh) * 4 + xx

    def ctx_at(z, y, core):
        return z * 8 + y * 2 + core

    def slot_at(z, y, core):
        return y * 4 + z * 2 + core

    other = ctx_at(zl, yy, 1 - k)
    sends = []
    used = [0]

    def take(n):
        used[0] += n
        return used[0] - n

    def remote(src, dst, sem, fs, cs):
        return pltpu.make_async_remote_copy(
            src_ref=src, dst_ref=dst, send_sem=ss.at[sem], recv_sem=rs.at[sem],
            device_id={"fsdp": fs, "ctx": cs}, device_id_type=MESH,
        )

    def send(src, dst, sem, fs, cs):
        copy = remote(src, dst, sem, fs, cs)
        copy.start()
        sends.append(copy)
        return copy

    def drain(count):
        for copy in sends[:count]:
            copy.wait_send()
        del sends[:count]

    def arrived(dst, sem):
        remote(dst, dst, sem, f, other).wait_recv()

    loads = [
        pltpu.make_async_copy(src, dst, ls.at[7 + n])
        for n, (src, dst) in enumerate(
            (
                (wq_h, wq_in), (wkv_h, wkv_in), (tok_h, tok), (cols_h, spread_cols),
                (rows_h, spread_rows), (cot_h, cot), (wg_h, wg_in), (wu_h, wu_in), (wd_h, wd_in),
                (wo_h, wo_in),
            )
        )
    ]
    for copy in loads:
        copy.start()

    barrier = pltpu.get_barrier_semaphore()
    for step in range(1, 16):
        pl.semaphore_signal(
            barrier, inc=1, device_id={"fsdp": f, "ctx": (c + step) % 16}, device_id_type=MESH
        )
    for step in range(1, 8):
        pl.semaphore_signal(
            barrier, inc=1, device_id={"fsdp": (f + step) % 8, "ctx": c}, device_id_type=MESH
        )
    pl.semaphore_signal(
        barrier, inc=1, device_id={"fsdp": fz, "ctx": ctx_at(1 - zl, yy, k)}, device_id_type=MESH
    )

    rows_of = lax.broadcasted_iota(jnp.int32, (ROWS, 1), 0)
    run = jnp.where((rows_of // 8) % 2 == 0, pos[0, 0], pos[0, 128]).astype(F32)
    tag = run * (1.0 / 16.0) + (rows_of % 8).astype(F32)

    def pack_rows(ref):
        return mm(spread_rows[...], mm_tn(ref[...], spread_cols[...]).astype(BF))

    for copy in loads:
        copy.wait()
    xc[:, 0:16, :] = (
        jnp.where(lane_iota((ROWS, DP)) == 72, tag, pack_rows(tok)).astype(BF).reshape(16, 16, DP)
    )
    xc[:, 16:32, :] = pack_rows(cot).astype(BF).reshape(16, 16, DP)

    def pad_rows(value):
        return jnp.concatenate([value.astype(F32), jnp.zeros((8, value.shape[1]), F32)], axis=0)

    wq_all = pad_rows(wq_in[...])
    wkv_all = pad_rows(wkv_in[...])
    low80 = lane_iota((80, 128)) < 64
    wa_in[0] = wq_all[:, 0:512].astype(BF)
    row16 = lax.broadcasted_iota(jnp.int32, (16, 72), 0)
    gains_in = jnp.where(row16 == 0, g1_in[...].astype(F32), g2_in[...].astype(F32))
    gains_in = jnp.where(row16 < 2, gains_in, 0.0).astype(BF)
    row_hot = lax.broadcasted_iota(jnp.int32, (16, 128), 0)
    gain_hot = jnp.where((lane_iota((16, 128)) == 64 + row_hot) & (row_hot < 2), 1.0, 0.0).astype(BF)
    last_q = jnp.concatenate([wq_all[:, 512:576], jnp.zeros((80, 64), F32)], axis=1)
    wa_in[1, :, 0:128] = (last_q + pad_rows(mm_tn(gains_in, gain_hot))).astype(BF)

    def kv_head(n, want_low):
        block = wkv_all[:, 128 * (n // 2) : 128 * (n // 2) + 128]
        return block if (n % 2 == 0) == want_low else pltpu.roll(block, 64, 1)

    for g in range(3):
        both = jnp.where(low80, kv_head(g, True), kv_head(3 + g, False))
        wa_in[1, :, 128 + 128 * g : 256 + 128 * g] = both.astype(BF)

    for half, ref in ((0, wg_in), (1, wu_in)):
        whole = pad_rows(ref[...]).astype(BF)
        for t in range(12):
            wb_in[half, up_tile(half, t)] = whole[:, 128 * t : 128 * t + 128]
    whole = pad_rows(wd_in[...]).astype(BF)
    for t in range(12):
        half, at = down_tile(t)
        wb_in[half, at] = whole[:, 128 * t : 128 * t + 128]
    whole = jnp.concatenate([pad_rows(wo_in[...]), jnp.zeros((80, 64), F32)], axis=1).astype(BF)
    for t in range(5):
        wb_in[t // 4, 18 + t % 4] = whole[:, 128 * t : 128 * t + 128]
    wb_in[0, 22:24] = jnp.zeros((2, 80, 128), BF)
    wb_in[1, 19:24] = jnp.zeros((5, 80, 128), BF)
    pl.semaphore_wait(barrier, 23)

    zz = 2 * zh + zl
    order = ("ayb", "yba", "yab")

    def pick(n, u, w):
        return u if n < 2 else u * (1 - k) + w * k

    def coord(n, axis):
        if axis == "y":
            return yy
        return pick(n, zz, xx) if axis == "a" else pick(n, xx, zz)

    def along(n, axis, step):
        if axis == "y":
            return f, ctx_at(zl, (yy + step) % 4, k)
        z = (zz + step) % 4
        by_x = (zh * 4 + (xx + step) % 4, c)
        by_z = ((z // 2) * 4 + xx, ctx_at(z % 2, yy, k))
        first, second = (by_z, by_x) if axis == "a" else (by_x, by_z)
        return pick(n, first[0], second[0]), pick(n, first[1], second[1])

    def region(n, done, axis=None, step=0):
        at = []
        for name in "aby":
            if name in done:
                at.append(slice(None))
            else:
                at.append((coord(n, name) + 4 - step) % 4 if name == axis else coord(n, name))
        return wb.at[(k, n, *at)]

    local = [
        pltpu.make_async_copy(xc.at[c], xc_r.at[c], ls.at[0]),
        pltpu.make_async_copy(wa_in.at[k], wa.at[k, f], ls.at[1]),
        *(
            pltpu.make_async_copy(
                wb_in.at[k, 8 * n + 2 * yy + zl], region(n, ()), ls.at[4 + n]
            )
            for n in range(3)
        ),
        pltpu.make_async_copy(cos_in.at[:, c], cos_s, ls.at[2]),
        pltpu.make_async_copy(sin_in.at[:, c], sin_s, ls.at[3]),
    ]
    for copy in local:
        copy.start()

    def gather_first(w_in, w, sem):
        send(w_in.at[k], w.at[k, f], sem, fz, c)
        for step in range(1, 4):
            send(w_in.at[k], w.at[k, f], sem + step, zh * 4 + (xx + step) % 4, c)

    def gather_second(w, sem):
        arrived(w.at[k, fz], sem)
        return [
            send(w.at[k, fz], w.at[k, fz], sem + 3 + step, zh * 4 + (xx + step) % 4, c)
            for step in range(1, 4)
        ]

    def gather_third(w, sem):
        for step in range(1, 4):
            from_x = (xx + 4 - step) % 4
            arrived(w.at[k, zh * 4 + from_x], sem + step)
            arrived(w.at[k, (1 - zh) * 4 + from_x], sem + 3 + step)
        return [send(w.at[k], w.at[k], sem + 7, f, other)]

    def gather_last(w, sem):
        arrived(w.at[1 - k], sem + 7)

    sem_b = take(30)

    def spread(turn):
        if turn > 0:
            spread_wait(turn - 1)
        out = []
        for n in range(3):
            axis, done = order[n][turn], order[n][:turn]
            for step in range(1, 4):
                if turn == 0:
                    src = wb_in.at[k, 8 * n + 2 * yy + zl]
                else:
                    src = region(n, done)
                copy = send(
                    src, region(n, done), sem_b + 9 * turn + 3 * n + step - 1, *along(n, axis, step)
                )
                if turn > 0:
                    out.append(copy)
        return out

    def spread_wait(turn, groups=(0, 1, 2)):
        for n in groups:
            axis, done = order[n][turn], order[n][:turn]
            for step in range(1, 4):
                arrived(region(n, done, axis, step), sem_b + 9 * turn + 3 * n + step - 1)

    sem_a = take(8)
    gather_first(wa_in, wa, sem_a)
    sem_x = take(16)
    for step in range(1, 16):
        to = (c + step) % 16
        send(xc.at[to, 0:16], xc_r.at[c, 0:16], sem_x + step, f, to)
    gather_second(wa, sem_a)
    spread(0)
    sem_c = take(16)
    for step in range(1, 16):
        to = (c + step) % 16
        send(xc.at[to, 16:32], xc_r.at[c, 16:32], sem_c + step, f, to)

    def make_bias(slot, carry):
        e = ctx_at((slot // 2) % 2, slot // 4, slot % 2)
        j = lax.broadcasted_iota(jnp.int32, (128, 128), 0)
        i = lax.broadcasted_iota(jnp.int32, (128, 128), 1)
        ok = (j // 8 < i // 8) | ((j // 8 == i // 8) & (8 * e + j % 8 <= 8 * c + i % 8))
        bias[pl.ds(pl.multiple_of(slot * 128, 128), 128), :] = jnp.where(ok, 0.0, NEG)
        return carry

    lax.fori_loop(0, 16, make_bias, 0)
    for copy in local:
        copy.wait()
    from_wb = spread(1)
    for step in range(1, 16):
        arrived(xc_r.at[(c + 16 - step) % 16, 0:16], sem_x + step)

    x_raw = xc_r[:, 0:16, :].reshape(ROWS, DP)
    lane = lane_iota((ROWS, DP))
    tag = jnp.sum(jnp.where(lane == 72, x_raw.astype(F32), 0.0), axis=1, keepdims=True)
    place = lane_iota((ROWS, ROWS)).astype(F32)
    perm[...] = jnp.where(tag == place, 1.0, 0.0).astype(BF)
    perm_t = jnp.where(tag == place, 1.0, 0.0).T.astype(BF)
    x = mm(perm_t, x_raw)
    x = jnp.where(lane % 80 < 72, x, 0.0)
    xs[...] = x

    gather_third(wa, sem_a)
    r1 = lax.rsqrt(jnp.sum(x * x, axis=-1, keepdims=True) * (1.0 / D) + 1e-5)
    gather_last(wa, sem_a)

    def gain_row(which):
        hot = jnp.where(lane_iota((16, 128)) == 64 + which, 1.0, 0.0).astype(BF)
        block = wa[1, :, :, 0:128].reshape(DP, 128)
        return mm_nt(hot, block)[0:1, :]

    gain1, gain2 = gain_row(0), gain_row(1)
    a1 = x * r1 * gain1
    a1b = a1.astype(BF)
    act1[...] = a1b
    act1t[...] = a1.T.astype(BF)

    cos = cos_s[...].reshape(ROWS, 128)
    sin = sin_s[...].reshape(ROWS, 128)
    low = lane_iota((ROWS, 128)) < 64
    cos_kv = jnp.where(low, cos, 1.0)
    sin_kv = jnp.where(low, sin, 0.0)

    mine = slot_at(zl, yy, k)
    kv_pre = mm(a1b, wa[1, :, :, 128:512].reshape(DP, 384))
    for g in range(3):
        u = kv_pre[:, 128 * g : 128 * g + 128]
        kv[mine, g] = (u * cos_kv + partner_lanes(u) * sin_kv).astype(BF)
    sem_k = take(16)

    near = slot_at(1 - zl, yy, k)

    def kv_along_y(slot, a):
        for off in (1, 3):
            send(kv.at[slot], kv.at[slot], sem_k + a * 4 + off, f, ctx_at(zl, (yy + off) % 4, k))

    send(kv.at[mine], kv.at[mine], sem_k, f, other)
    send(kv.at[mine], kv.at[mine], sem_k + 4, f, ctx_at(1 - zl, yy, k))
    kv_along_y(mine, 0)

    def kv_direct(off):
        for a in (0, 1):
            if (a, off) != (0, 0):
                at = slot_at(zl if a == 0 else 1 - zl, (yy + 4 - off) % 4, k)
                arrived(kv.at[at], sem_k + a * 4 + off)
                send(kv.at[at], kv.at[at], sem_k + 8 + a * 4 + off, f, other)
                if (a, off) in ((0, 1), (1, 3)):
                    to = ctx_at(zl, (yy + off) % 4, k)
                    send(kv.at[at], kv.at[at], sem_k + a * 4 + 2, f, to)

    def kv_across(off):
        for a in (0, 1):
            at = slot_at(zl if a == 0 else 1 - zl, (yy + 4 - off) % 4, 1 - k)
            arrived(kv.at[at], sem_k if (a, off) == (0, 0) else sem_k + 8 + a * 4 + off)

    from_wb += spread(2)
    for t in range(5):
        w = wa[0, :, :, 128 * t : 128 * t + 128] if t < 4 else wa[1, :, :, 0:128]
        u = mm(a1b, w.reshape(DP, 128))
        u = (u * cos + partner_lanes(u) * sin).astype(BF).astype(F32) * 0.125
        for half in range(2):
            h = 2 * t + half
            if h < 9:
                g, r = h // 3, h % 3
                v = jnp.where(low, u if half == 0 else pltpu.roll(u, 64, 1), 0.0)
                vt = v.T
                for ih in range(2):
                    at = 384 * ih + 128 * r
                    qx[g, at : at + 128, :] = v[128 * ih : 128 * ih + 128].astype(BF)
                    qt[g, :, at : at + 128] = vt[:, 128 * ih : 128 * ih + 128].astype(BF)

    kv_direct(0)
    kv_along_y(near, 1)

    for step in range(1, 16):
        arrived(xc_r.at[(c + 16 - step) % 16, 16:32], sem_c + step)
    dy[...] = mm_tn(perm[...], xc_r[:, 16:32, :].reshape(ROWS, DP)).astype(BF)

    st_m[...] = jnp.full(st_m.shape, NEG, F32)
    st_l[...] = jnp.zeros(st_l.shape, F32)
    acc[...] = jnp.zeros(acc.shape, F32)

    def three(b):
        return jnp.concatenate([b, b, b], axis=1)

    def fold_forward(off):
        group = (yy + 4 - off) % 4

        def per_head(g, carry):
            b3 = three(bias[pl.ds(pl.multiple_of(group * 512, 512), 512), :])
            for key_half, lane_half in ((0, 0), (0, 1), (1, 1)):
                at = 384 * lane_half
                rows = kv[pl.ds(group * 4, 4), g, 128 * key_half : 128 * key_half + 128, :]
                rows = rows.reshape(512, 128)
                s = mm(rows, qt[g, :, at : at + 384])
                if key_half == lane_half:
                    s = s + b3
                old = st_m[g, :, at : at + 384]
                new = jnp.maximum(old, jnp.max(s, axis=0, keepdims=True))
                p = jnp.exp(s - new)
                scale = jnp.exp(old - new)
                st_m[g, :, at : at + 384] = new
                st_l[g, :, at : at + 384] = (
                    st_l[g, :, at : at + 384] * scale + jnp.sum(p, axis=0, keepdims=True)
                )
                acc[g, :, at : at + 384] = acc[g, :, at : at + 384] * scale + mm_tn(
                    rows, p.astype(BF)
                )
            return carry

        lax.fori_loop(0, 3, per_head, 0)

    kv_direct(STEPS[1])
    kv_across(0)
    fold_forward(0)
    kv_direct(STEPS[2])
    kv_across(STEPS[1])
    fold_forward(STEPS[1])
    kv_direct(STEPS[3])
    kv_across(STEPS[2])
    fold_forward(STEPS[2])
    kv_across(STEPS[3])
    for n in (1, 0, 2):
        spread_wait(2, (n,))
        from_wb.append(send(wb.at[k, n], wb.at[k, n], sem_b + 27 + n, f, other))
    fold_forward(STEPS[3])

    def head_rows(ref, g, r):
        return jnp.concatenate(
            [ref[g, :, 384 * ih + 128 * r : 384 * ih + 128 * r + 128].T for ih in range(2)], axis=0
        )

    for g in range(3):
        ot[g] = acc[g] / st_l[g]
        st_l[g] = st_m[g] + jnp.log(st_l[g])
    for t in range(5):
        a = pltpu.roll(head_rows(ot, 2 * t // 3, 2 * t % 3), 64, 1)
        b = head_rows(ot, (2 * t + 1) // 3, (2 * t + 1) % 3) if t < 4 else jnp.zeros((ROWS, 128), F32)
        attb[:, 128 * t : 128 * t + 128] = jnp.where(low, a, b).astype(BF)

    for n in range(3):
        arrived(wb.at[1 - k, n], sem_b + 27 + n)

    def fixed(half, n):
        return isinstance(half, int) and isinstance(n, int) and (half, n) == LAST

    def tile_at(half, n, y, z):
        if fixed(half, n):
            blocks = [wb[1, 2, :, 2 * q + z, y] for q in range(2)]
        else:
            blocks = [wb[half, n, 2 * q + z, :, y] for q in range(2)]
        return jnp.concatenate(blocks, axis=0).reshape(DP, 128)

    def put_tile(half, n, y, z, value):
        value = value.astype(BF).reshape(2, 4, 80, 128)
        for q in range(2):
            if fixed(half, n):
                wb[1, 2, :, 2 * q + z, y] = value[q]
            else:
                wb[half, n, 2 * q + z, :, y] = value[q]

    def pair(half, p):
        return jnp.concatenate([tile_at(half, p // 4, p % 4, z) for z in range(2)], axis=1)

    def put_pair(half, p, value):
        for z in range(2):
            put_tile(half, p // 4, p % 4, z, value[:, 128 * z : 128 * z + 128])

    def out_tile(t):
        return tile_at(0, 2, 1 + t // 2, t % 2) if t < 4 else tile_at(1, 2, 1, 0)

    out_w = jnp.concatenate([out_tile(t) for t in range(5)], axis=1)
    m0 = xs[...] + mm_nt(attb[...], out_w)
    r2 = lax.rsqrt(jnp.sum(m0 * m0, axis=-1, keepdims=True) * (1.0 / D) + 1e-5)
    mid[...] = m0
    a2 = m0 * r2 * gain2
    a2b = a2.astype(BF)
    a2t = a2.T.astype(BF)
    dyb = dy[...]
    dyt = dyb.astype(F32).T.astype(BF)

    for copy in from_wb:
        copy.wait_send()
    sends[:] = [copy for copy in sends if all(copy is not done for done in from_wb)]

    def ff(j, carry):
        total, dact = carry
        last = isinstance(j, int)
        at_g, at_u, at_d = ((0, 8), (1, 7), (1, 8)) if last else ((0, j), (1, j), (j // 3, 5 + j % 3))
        wg, wu, wd = pair(*at_g), pair(*at_u), pair(*at_d)
        gate, up = mm(a2b, wg), mm(a2b, wu)
        sig = jax.nn.sigmoid(gate)
        swish = gate * sig
        hid = (swish * up).astype(BF)
        total = total + mm_nt(hid, wd)
        dh = mm(dyb, wd)
        dg = (dh * up * sig * (1.0 + gate * (1.0 - sig))).astype(BF)
        du = (dh * swish).astype(BF)
        put_pair(*at_d, mm(dyt, hid))
        put_pair(*at_g, mm(a2t, dg))
        put_pair(*at_u, mm(a2t, du))
        dact = dact + mm_nt(dg, wg) + mm_nt(du, wu)
        return total, dact

    zero = jnp.zeros((ROWS, DP), F32)
    total, dact = ff(5, lax.fori_loop(0, 5, ff, (zero, zero)))

    sem_r = take(42)

    def add(ref, at, got_at):
        v = ref[at].astype(F32)
        for r in got_at:
            v = v + r.astype(F32)
        return v

    def red_core(n):
        send(wb.at[1 - k, n], gbc.at[n], sem_r + n, f, other)

    def red_one(n):
        arrived(gbc.at[n], sem_r + n)

        def body(i, carry):
            wb[k, n, i // 4, i % 4] = (
                wb[k, n, i // 4, i % 4].astype(F32) + gbc[n, i // 4, i % 4].astype(F32)
            ).astype(BF)
            return carry

        lax.fori_loop(0, 16, body, 0)
        axis = order[n][2]
        for step in range(1, 4):
            to = (coord(n, axis) + step) % 4
            src = wb.at[k, n, to] if axis == "a" else wb.at[k, n, :, to]
            send(src, q1.at[n, step - 1], sem_r + 3 + 3 * n + step - 1, *along(n, axis, step))

    def red_two(n):
        for step in range(3):
            arrived(q1.at[n, step], sem_r + 3 + 3 * n + step)
        axis, at = order[n][2], coord(n, order[n][2])

        def body(i, carry):
            v = (wb[k, n, at, i] if axis == "a" else wb[k, n, i, at]).astype(F32)
            for step in range(3):
                v = v + q1[n, step, i].astype(F32)
            t1[n, i] = v.astype(BF)
            return carry

        lax.fori_loop(0, 4, body, 0)
        axis = order[n][1]
        for step in range(1, 4):
            to = (coord(n, axis) + step) % 4
            src = t1.at[n, :, to] if axis == "y" else t1.at[n, to]
            send(src, q2.at[n, step - 1], sem_r + 12 + 3 * n + step - 1, *along(n, axis, step))

    def red_three(n):
        for step in range(3):
            arrived(q2.at[n, step], sem_r + 12 + 3 * n + step)
        axis, at = order[n][1], coord(n, order[n][1])
        own = (n, slice(None), at) if axis == "y" else (n, at)
        t2[n] = add(t1, own, [q2[n, i] for i in range(3)]).astype(BF)
        axis = order[n][0]
        for step in range(1, 4):
            to = (coord(n, axis) + step) % 4
            send(t2.at[n, to], q3.at[n, step - 1], sem_r + 21 + 3 * n + step - 1, *along(n, axis, step))

    def red_four():
        for n in range(3):
            for step in range(3):
                arrived(q3.at[n, step], sem_r + 21 + 3 * n + step)
            own = add(t2, (n, coord(n, order[n][0])), [q3[n, i] for i in range(3)])
            gbf[k, yy, zl, n] = own.astype(BF)
        piece = gbf.at[k, yy, zl]
        for a, off in CHIPS:
            to = ctx_at(zl if a == 0 else 1 - zl, (yy + off) % 4, k)
            send(piece, piece, sem_r + 30 + 4 * a + off, f, to)

    def red_five():
        for a, off in CHIPS:
            z = zl if a == 0 else 1 - zl
            arrived(gbf.at[k, (yy + 4 - off) % 4, z], sem_r + 30 + 4 * a + off)
        send(gbf.at[k], gbf.at[k], sem_r + 38, f, other)

    def red_six():
        arrived(gbf.at[1 - k], sem_r + 38)

    sem_g = take(36)

    def in_core(p):
        send(ga.at[p, 1 - k], gac.at[p], sem_g + 18 * p, f, other)

    def in_one(p):
        arrived(gac.at[p], sem_g + 18 * p)
        ga[p, k] = (ga[p, k].astype(F32) + gac[p].astype(F32)).astype(BF)
        for step in range(1, 8):
            to = (f + step) % 8
            send(ga.at[p, k, to], gax.at[p, step - 1], sem_g + 18 * p + step, to, c)

    def in_two(p):
        for step in range(1, 8):
            arrived(gax.at[p, step - 1], sem_g + 18 * p + step)
        gay_s[p] = add(ga, (p, k, f), [gax[p, i] for i in range(7)]).astype(BF)
        for a, off in CHIPS:
            to = ctx_at(zl if a == 0 else 1 - zl, (yy + off) % 4, k)
            send(gay_s.at[p], gay.at[p, 4 * a + off], sem_g + 18 * p + 8 + 4 * a + off, f, to)

    def in_three(p):
        for a, off in CHIPS:
            arrived(gay.at[p, 4 * a + off], sem_g + 18 * p + 8 + 4 * a + off)
        gaf[p, k] = add(gay_s, p, [gay[p, 4 * a + off] for a, off in CHIPS]).astype(BF)
        send(gaf.at[p, k], gaf.at[p, k], sem_g + 18 * p + 16, f, other)

    def in_four(p):
        arrived(gaf.at[p, 1 - k], sem_g + 18 * p + 16)

    red_core(0)
    red_core(1)

    def give_back(value, src, dst, sem):
        src[...] = mm(perm[...], value.astype(BF)).astype(BF).reshape(16, 16, DP)
        for step in range(1, 16):
            send(src.at[(c + step) % 16], dst.at[c], sem + step, f, (c + step) % 16)
        dst[c] = src[c]

    sem_o = take(16)
    sem_i = take(16)
    m0 = mid[...]
    give_back(m0 + total, bo_s, bo_r, sem_o)

    dyf = dyb.astype(F32)
    gain_grad2 = jnp.sum(dact * m0 * r2, axis=0, keepdims=True)
    wgt = dact * gain2
    inner = jnp.sum(wgt * m0, axis=-1, keepdims=True) * (1.0 / D)
    dm = dyf + r2 * wgt - m0 * (r2 * r2 * r2) * inner
    dmid[...] = dm
    dmb = dm.astype(BF)
    dmt = dm.T.astype(BF)

    for t in range(5):
        u = mm(dmb, out_tile(t)).astype(BF).astype(F32)
        for half in range(2):
            h = 2 * t + half
            if h < 9:
                g, r = h // 3, h % 3
                v = jnp.where(low, 0.0, u if half == 1 else pltpu.roll(u, 64, 1))
                vt = v.T
                for ih in range(2):
                    at = 384 * ih + 128 * r
                    dox[g, at : at + 128, :] = v[128 * ih : 128 * ih + 128].astype(BF)
                    dot_[g, :, at : at + 128] = vt[:, 128 * ih : 128 * ih + 128].astype(BF)
    grad_out = mm(dmt, attb[...]).astype(BF)
    for t in range(5):
        at = (0, 2, 1 + t // 2, t % 2) if t < 4 else (1, 2, 1, 0)
        put_tile(*at, grad_out[:, 128 * t : 128 * t + 128])
    red_core(2)

    for g in range(3):
        st_m[g] = jnp.sum(dot_[g].astype(F32) * ot[g], axis=0, keepdims=True)
    dqt[...] = jnp.zeros(dqt.shape, F32)

    def fold_backward(at_step, off):
        group = (yy + 4 - off) % 4

        def per_head(g, carry):
            b3 = three(bias[pl.ds(pl.multiple_of(group * 512, 512), 512), :])
            for key_half in range(2):
                rows = kv[pl.ds(group * 4, 4), g, 128 * key_half : 128 * key_half + 128, :]
                rows = rows.reshape(512, 128)
                grad = None
                for lane_half in range(key_half, 2):
                    at = 384 * lane_half
                    s = mm(rows, qt[g, :, at : at + 384])
                    if key_half == lane_half:
                        s = s + b3
                    p = jnp.exp(s - st_l[g, :, at : at + 384])
                    dp = mm(rows, dot_[g, :, at : at + 384])
                    ds = (p * (dp - st_m[g, :, at : at + 384])).astype(BF)
                    part = mm(ds, qx[g, at : at + 384, :]) + mm(
                        p.astype(BF), dox[g, at : at + 384, :]
                    )
                    grad = part if grad is None else grad + part
                    dqt[g, :, at : at + 384] += mm_tn(rows, ds)
                dkv_p[at_step, :, g, 128 * key_half : 128 * key_half + 128, :] = grad.astype(
                    BF
                ).reshape(4, 128, 128)
            return carry

        lax.fori_loop(0, 3, per_head, 0)

    sem_d1 = take(8)
    sem_d = take(4)

    def dkv_first(at_step):
        for z in range(2):
            send(
                dkv_p.at[at_step, 2 * z + 1 - k], d1_r.at[at_step, z], sem_d1 + 2 * at_step + z,
                f, other,
            )

    def dkv_second(at_step, off):
        for z in range(2):
            arrived(d1_r.at[at_step, z], sem_d1 + 2 * at_step + z)
        for z in range(2):
            d2_s[at_step, z] = (
                dkv_p[at_step, 2 * z + k].astype(F32) + d1_r[at_step, z].astype(F32)
            ).astype(BF)
        if off != 0:
            send(
                d2_s.at[at_step], d2_r.at[off - 1], sem_d + off,
                f, ctx_at(zl, (yy + 4 - off) % 4, k),
            )

    red_one(0)
    red_one(1)
    red_one(2)
    fold_backward(0, BACK[0])
    dkv_first(0)
    dkv_second(0, BACK[0])
    fold_backward(1, BACK[1])
    dkv_first(1)
    dkv_second(1, BACK[1])
    fold_backward(2, BACK[2])
    dkv_first(2)
    dkv_second(2, BACK[2])
    fold_backward(3, BACK[3])
    dkv_first(3)
    for n in (1, 0, 2):
        red_two(n)
    dkv_second(3, BACK[3])
    for off in range(1, 4):
        arrived(d2_r.at[off - 1], sem_d + off)
    dz_s[...] = add(d2_s, (3, 1 - zl), [d2_r[i, 1 - zl] for i in range(3)]).astype(BF)
    old = len(sends)
    send(dz_s, dz_r, sem_d, f, ctx_at(1 - zl, yy, k))

    dq_tiles = []
    for t in range(5):
        a = head_rows(dqt, 2 * t // 3, 2 * t % 3)
        if t < 4:
            b = pltpu.roll(head_rows(dqt, (2 * t + 1) // 3, (2 * t + 1) % 3), 64, 1)
        else:
            b = jnp.zeros((ROWS, 128), F32)
        u = jnp.where(low, a, b) * 0.125
        dq_tiles.append((u * cos - partner_lanes(u) * sin).astype(BF))
    dq = jnp.concatenate(dq_tiles, axis=1)
    a1t = act1t[...]
    grad_q = mm(a1t, dq)
    for half in range(2):
        ga[0, half] = grad_q[:, 256 * half : 256 * half + 256].astype(BF).reshape(8, 80, 256)
    in_core(0)
    dact1 = mm_nt(dq[:, 0:512], wa[0].reshape(DP, 512)) + mm_nt(
        dq[:, 512:640], wa[1, :, :, 0:128].reshape(DP, 128)
    )
    in_one(0)
    drain(old)
    dkv = add(d2_s, (3, zl), [d2_r[i, zl] for i in range(3)])
    arrived(dz_r, sem_d)
    dkv = dkv + dz_r[...].astype(F32)
    for g in range(3):
        u = dkv[g]
        u = (u * cos_kv - partner_lanes(u) * sin_kv).astype(BF)
        at = 128 + 128 * g
        part = mm(a1t, u).astype(BF).reshape(8, 80, 128)
        lanes = slice(128, 256) if g != 1 else slice(0, 128)
        ga[1, 0 if g == 0 else 1, :, :, lanes] = part
        dact1 = dact1 + mm_nt(u, wa[1, :, :, at : at + 128].reshape(DP, 128))

    x = xs[...]
    gain_grad1 = jnp.sum(dact1 * x * r1, axis=0, keepdims=True)
    gains = jnp.concatenate([gain_grad1, gain_grad2, jnp.zeros((6, DP), F32)], axis=0)
    hot = jnp.where(
        lane_iota((8, 128)) == 64 + lax.broadcasted_iota(jnp.int32, (8, 128), 0), 1.0, 0.0
    )
    hot = jnp.where(lax.broadcasted_iota(jnp.int32, (8, 128), 0) < 2, hot, 0.0)
    gain_cols = mm(gains.T.astype(BF), hot.astype(BF))
    ga[1, 0, :, :, 0:128] = (grad_q[:, 512:640] + gain_cols).astype(BF).reshape(8, 80, 128)
    old = len(sends)
    in_core(1)
    in_one(1)
    for n in (1, 0, 2):
        red_three(n)

    wgt = dact1 * gain1
    inner = jnp.sum(wgt * x, axis=-1, keepdims=True) * (1.0 / D)
    give_back(
        dmid[...] + r1 * wgt - x * (r1 * r1 * r1) * inner, ig_s, ig_r, sem_i
    )
    red_four()
    in_two(0)
    drain(old)
    old = len(sends)
    in_two(1)
    red_five()
    in_three(0)
    drain(old)
    for step in range(1, 16):
        arrived(bo_r.at[(c + 16 - step) % 16], sem_o + step)
    bo_out[...] = bo_r[...]
    in_three(1)
    for step in range(1, 16):
        arrived(ig_r.at[(c + 16 - step) % 16], sem_i + step)
    ig_out[...] = ig_r[...]
    red_six()
    gb_out[...] = gbf[...]
    in_four(0)
    in_four(1)
    ga_out[...] = gaf[...]
    for copy in sends:
        copy.wait_send()


def tables():
    freq = np.power(np.float32(100000.0), -(np.arange(32, dtype=np.float32) * np.float32(2.0 / 64)))
    angle = np.arange(4096, dtype=np.float32)[:, None] * freq[None, :].astype(np.float32)
    cos, sin = np.cos(angle), np.sin(angle)
    cos = np.concatenate([cos, cos, cos, cos], axis=1)
    sin = np.concatenate([-sin, sin, -sin, sin], axis=1)
    shape = (32, 16, 8, 128)
    return cos.reshape(shape).astype(np.float32), sin.reshape(shape).astype(np.float32)


def placements():
    cols = np.zeros((D, DP), np.float32)
    at = np.arange(D)
    cols[at, at // 72 * 80 + at % 72] = 1.0
    rows = np.zeros((ROWS, ROWS), np.float32)
    at = np.arange(ROWS)
    rows[at, at // 8 % 2 * 128 + at // 16 * 8 + at % 8] = 1.0
    return jnp.asarray(cols, BF), jnp.asarray(rows, BF)


def finish(
    bo_h, ig_h, ga_h, gb_h, cols_h, rows_h,
    out, grad_in, n1, gq, gkv, go, n2, gg, gu, gd,
    bo, ig, ga, gb, cols, rows, sems,
):
    copies = [
        pltpu.make_async_copy(src, dst, sems.at[n])
        for n, (src, dst) in enumerate(
            ((gb_h, gb), (cols_h, cols), (rows_h, rows), (bo_h, bo), (ig_h, ig), (ga_h, ga))
        )
    ]
    for copy in copies:
        copy.start()
    for copy in copies:
        copy.wait()
    for src, dst in ((bo, out), (ig, grad_in)):
        narrow = mm_nt(cols[...], src[...].reshape(ROWS, DP)).astype(BF)
        dst[...] = mm(narrow, rows[...]).astype(dst.dtype)

    def part(ref, *at):
        return ref[at].astype(F32)

    for t in range(4):
        gq[:, 128 * t : 128 * t + 128] = part(ga, 0, t // 2)[0:72, 128 * (t % 2) : 128 * (t % 2) + 128]
    last = part(ga, 1, 0)[:, 0:128]
    gq[:, 512:576] = last[0:72, 0:64]
    row = lax.broadcasted_iota(jnp.int32, (16, 128), 0)
    hot = jnp.where((lane_iota((16, 128)) == 64 + row) & (row < 2), 1.0, 0.0).astype(BF)
    gains = mm_nt(hot, last.astype(BF))
    n1[...] = gains[0:1, 0:72]
    n2[...] = gains[1:2, 0:72]
    low = lane_iota((80, 128)) < 64
    tiles = [part(ga, 1, 0)[:, 128:256], part(ga, 1, 1)[:, 0:128], part(ga, 1, 1)[:, 128:256]]
    turn = [pltpu.roll(t, 64, 1) for t in tiles]
    heads = [
        jnp.where(low, tiles[0], turn[1]),
        jnp.where(low, tiles[2], tiles[0]),
        jnp.where(low, turn[1], tiles[2]),
    ]
    for g in range(3):
        gkv[:, 128 * g : 128 * g + 128] = heads[g][0:72]

    def tile(half, t):
        return part(gb, half, (t % 8) // 2, t % 2, t // 8)

    for half, ref in ((0, gg), (1, gu)):
        for t in range(12):
            ref[:, 128 * t : 128 * t + 128] = tile(half, up_tile(half, t))[0:72]
    for t in range(12):
        gd[:, 128 * t : 128 * t + 128] = tile(*down_tile(t))[0:72]
    for t in range(4):
        go[:, 128 * t : 128 * t + 128] = tile(0, 18 + t)[0:72]
    go[:, 512:576] = tile(1, 18)[0:72, 0:64]


def local(tokens, positions, gain1, wq, wkv, wo, gain2, wg, wu, wd, cotangent):
    cos, sin = tables()
    cols, rows = placements()

    def v(shape, dtype=BF):
        return pltpu.VMEM(shape, dtype)

    any_space = pl.BlockSpec(memory_space=pl.ANY)
    vmem = pl.BlockSpec(memory_space=pltpu.VMEM)
    scratch = [
        v((D, ROWS)), v((D, ROWS)), v((72, 576)), v((72, 384)), v((72, 576)), v((72, 1536)),
        v((72, 1536)), v((72, 1536)), v((D, DP)), v((ROWS, ROWS)),
        v((16, 32, DP)), v((2, 80, WA)), v((2, TB, 80, 128)),
        v((16, 32, DP)), v((2, 8, 80, WA)), v((2, 3, 4, 4, 4, 80, 128)),
        v((32, 8, 128), F32), v((32, 8, 128), F32),
        v((16, 3, 256, 128)), v((2048, 128), F32), v((ROWS, ROWS)),
        v((3, 128, 768)), v((3, 768, 128)), v((3, 128, 768)), v((3, 768, 128)),
        v((3, 1, 768), F32), v((3, 1, 768), F32), v((3, 128, 768), F32), v((3, 128, 768), F32),
        v((3, 128, 768), F32),
        v((ROWS, DP), F32), v((ROWS, DP)), v((ROWS, DP), F32), v((ROWS, DP)), v((DP, ROWS)),
        v((ROWS, DP)), v((ROWS, DP), F32),
        v((4, 4, 3, 256, 128)), v((4, 2, 3, 256, 128)), v((4, 2, 3, 256, 128)),
        v((3, 2, 3, 256, 128)), v((3, 256, 128)), v((3, 256, 128)),
        v((2, 2, 8, 80, 256)), v((2, 8, 80, 256)), v((2, 7, 80, 256)),
        v((2, 80, 256)), v((2, 8, 80, 256)), v((2, 2, 80, 256)),
        v((3, 4, 4, 4, 80, 128)), v((3, 3, 4, 4, 80, 128)), v((3, 4, 4, 80, 128)),
        v((3, 3, 4, 80, 128)), v((3, 4, 80, 128)),
        v((3, 3, 80, 128)), v((2, 4, 2, 3, 80, 128)),
        v((16, 16, DP)), v((16, 16, DP)), v((16, 16, DP)), v((16, 16, DP)),
        pltpu.SemaphoreType.DMA((216,)), pltpu.SemaphoreType.DMA((216,)),
        pltpu.SemaphoreType.DMA((17,)),
    ]
    bo, ig, ga, gb = pl.pallas_call(
        kernel,
        out_shape=(
            jax.ShapeDtypeStruct((16, 16, DP), BF),
            jax.ShapeDtypeStruct((16, 16, DP), BF),
            jax.ShapeDtypeStruct((2, 2, 80, 256), BF),
            jax.ShapeDtypeStruct((2, 4, 2, 3, 80, 128), BF),
        ),
        in_specs=[pl.BlockSpec(memory_space=pltpu.SMEM)] + [vmem] * 2 + [any_space] * 12,
        out_specs=(vmem,) * 4,
        scratch_shapes=scratch,
        compiler_params=pltpu.CompilerParams(
            collective_id=0, has_side_effects=True, vmem_limit_bytes=62 * 1024 * 1024
        ),
        name="layer",
    )(
        positions, gain1.reshape(1, 72), gain2.reshape(1, 72), tokens[0].T, cotangent[0].T,
        wq, wkv, wo.T, wg, wu, wd.T, cols, rows, jnp.asarray(cos), jnp.asarray(sin),
    )

    def f32(*shape):
        return jax.ShapeDtypeStruct(shape, F32)

    outs = pl.pallas_call(
        finish,
        out_shape=(
            jax.ShapeDtypeStruct((D, ROWS), BF), f32(D, ROWS), f32(1, 72), f32(72, 576),
            f32(72, 384), f32(72, 576), f32(1, 72), f32(72, 1536), f32(72, 1536), f32(72, 1536),
        ),
        in_specs=[any_space] * 6,
        out_specs=(vmem,) * 10,
        scratch_shapes=[
            v((16, 16, DP)), v((16, 16, DP)), v((2, 2, 80, 256)), v((2, 4, 2, 3, 80, 128)),
            v((D, DP)), v((ROWS, ROWS)), pltpu.SemaphoreType.DMA((6,)),
        ],
        compiler_params=pltpu.CompilerParams(vmem_limit_bytes=60 * 1024 * 1024),
        name="finish",
    )(bo, ig, ga, gb, cols, rows)
    out, grad_in, n1, gq, gkv, go, n2, gg, gu, gd = outs
    return out.T[None], grad_in.T[None], n1.reshape(72), gq, gkv, go.T, n2.reshape(72), gg, gu, gd.T


def solution(mesh):
    rows, model, last = P("fsdp", "ctx", None), P("fsdp", None), P(None, "fsdp")
    gain = P("fsdp")
    return jax.shard_map(
        local,
        mesh=mesh,
        in_specs=(rows, P("fsdp", "ctx"), gain, model, model, last, gain, model, model, last, rows),
        out_specs=(rows, rows, gain, model, model, last, gain, model, model, last),
        check_vma=False,
    )
```
